32 devices in a mesh: rows: 8 (over z, x), tp: 4 (over y, core).
Axes of the slice: x: 2, y: 2, z: 4, core: 2. Of those that a mesh axis runs over, the one named last changes fastest.
Arguments:
- patches: bfloat16 [8, 768, 768], P('rows'), may hold values from -6 to 6
- segment_ids: int32 [8, 768], P('rows'), may hold values from 0 to 3, never falling along the last dimension, each value on 1 to 384 neighbouring positions
- mask_flags: int32 [8, 768], P('rows'), may hold values 0 or 1
- upstream: bfloat16 [8, 768, 768], P('rows'), may hold values from -6 to 6
- mask_embed: float32 [768], replicated, may hold values from -6 to 6
- norm_gain: float32 [2, 2, 768], replicated, may hold values from 0.5 to 1.5
- norm_shift: float32 [2, 2, 768], replicated, may hold values from -2 to 2
- in_weight: bfloat16 [2, 768, 3, 768], P(None, None, None, 'tp'), may hold values from -0.21875 to 0.21875
- in_bias: float32 [2, 2, 768], P(None, None, 'tp'), may hold values from -2 to 2
- out_weight: bfloat16 [2, 768, 768], P(None, 'tp'), may hold values from -0.875 to 0.875
- out_bias: float32 [2, 2, 768], replicated, may hold values from -2 to 2
- up_weight: bfloat16 [2, 768, 3072], P(None, None, 'tp'), may hold values from -0.21875 to 0.21875
- up_bias: float32 [2, 3072], P(None, 'tp'), may hold values from -2 to 2
- down_weight: bfloat16 [2, 3072, 768], P(None, 'tp'), may hold values from -0.109375 to 0.109375
- slow_mask_embed: float32 [768], replicated, may hold values from -6 to 6
- slow_norm_gain: float32 [2, 2, 768], replicated, may hold values from -3 to 3
- slow_norm_shift: float32 [2, 2, 768], replicated, may hold values from -2 to 2
- slow_in_weight: float32 [2, 768, 3, 768], P(None, 'rows', None, 'tp'), may hold values from -0.21875 to 0.21875
- slow_in_bias: float32 [2, 2, 768], P(None, None, 'tp'), may hold values from -2 to 2
- slow_out_weight: float32 [2, 768, 768], P(None, 'tp', 'rows'), may hold values from -0.875 to 0.875
- slow_out_bias: float32 [2, 2, 768], replicated, may hold values from -2 to 2
- slow_up_weight: float32 [2, 768, 3072], P(None, 'rows', 'tp'), may hold values from -0.21875 to 0.21875
- slow_up_bias: float32 [2, 3072], P(None, 'tp'), may hold values from -2 to 2
- slow_down_weight: float32 [2, 3072, 768], P(None, 'tp', 'rows'), may hold values from -0.109375 to 0.109375
Outputs:
- layer_out: bfloat16 [8, 768, 768], P('rows')
- grad_patches: bfloat16 [8, 768, 768], P('rows')
- grad_mask_embed: float32 [768], replicated
- grad_norm_gain: float32 [2, 2, 768], replicated
- grad_norm_shift: float32 [2, 2, 768], replicated
- grad_in_weight: float32 [2, 768, 3, 768], P(None, 'rows', None, 'tp')
- grad_in_bias: float32 [2, 2, 768], P(None, None, 'tp')
- grad_out_weight: float32 [2, 768, 768], P(None, 'tp', 'rows')
- grad_out_bias: float32 [2, 2, 768], replicated
- grad_up_weight: float32 [2, 768, 3072], P(None, 'rows', 'tp')
- grad_up_bias: float32 [2, 3072], P(None, 'tp')
- grad_down_weight: float32 [2, 3072, 768], P(None, 'tp', 'rows')
- fresh_mask_embed: float32 [768], replicated
- fresh_norm_gain: float32 [2, 2, 768], replicated
- fresh_norm_shift: float32 [2, 2, 768], replicated
- fresh_in_weight: float32 [2, 768, 3, 768], P(None, 'rows', None, 'tp')
- fresh_in_bias: float32 [2, 2, 768], P(None, None, 'tp')
- fresh_out_weight: float32 [2, 768, 768], P(None, 'tp', 'rows')
- fresh_out_bias: float32 [2, 2, 768], replicated
- fresh_up_weight: float32 [2, 768, 3072], P(None, 'rows', 'tp')
- fresh_up_bias: float32 [2, 3072], P(None, 'tp')
- fresh_down_weight: float32 [2, 3072, 768], P(None, 'tp', 'rows')
The draws below stay inside these ranges and needn't reach their ends.
Inputs may be any that keep to these rules, and one draw needn't show every extreme that they name: `segment_ids`: within each packed row the clip numbers never fall; each clip holds at most 384 patches.
All inputs are finite; a program needn't handle non-finite values. No bound on the sum of `mask_flags` on one device may be relied on, other than what follows from the above.
Results may differ from the reference program's by a relative error of at most 0.025.
Values may be sent and summed in bfloat16 or wider, within the bound.
No kernel may reach another device: no remote copies, remote signals or barrier semaphores. Data moves between devices by JAX's collectives and lax.ppermute only.
A program may use at most 192 MiB of HBM per device.

```python
import math
import jax
import jax.numpy as jnp
import numpy as np
from jax import lax

D = 768
HEADS = 12
HD = 64
FF = 3072
LAYERS = 2
LEN = 768
CLIPS = 4
HH = 768
ROWS = 8
N_TP = 4


def touch_ends(values, own_key, least, high):
    longest = values.shape.index(max(values.shape))
    spots = []
    for shift in (0, 1):
        where = [jax.random.randint(jax.random.fold_in(own_key, axis), (), 0, length) for axis, length in enumerate(values.shape)]
        where[longest] = (where[longest] + shift) % values.shape[longest]
        spots.append(tuple(where))
    return values.at[spots[0]].set(least).at[spots[1]].set(high)


def block_levels(rng, dims, shards, smallest, top_value):
    level = 1.0
    for position, shards_of in shards:
        draws = jax.random.uniform(jax.random.fold_in(jax.random.fold_in(rng, 6), position), (shards_of,), jnp.float32, smallest / len(shards), top_value / len(shards))
        level = level * jnp.repeat(jnp.exp(draws), dims[position] // shards_of).reshape((-1,) + (1,) * (len(dims) - 1 - position))
    return level


def length_profile(count, total, bound, lean):
    loads = [(1 << 20) // math.isqrt(rank ** lean) + 1 for rank in range(2, count + 1)]
    spare, holding = total - bound - (count - 1), [1] * (count - 1)
    while spare > 0:
        movable = [i for i in range(count - 1) if holding[i] < bound]
        pool, left = sum([loads[i] for i in movable]), spare
        for i in movable:
            extra = min(bound - holding[i], max(1, left * loads[i] // pool), spare)
            holding[i] = holding[i] + extra
            spare = spare - extra
    return np.array([bound] + holding)


def ragged(stream_key, amount, total, most, slope):
    if amount == 2:
        one = jax.random.randint(stream_key, (), max(1, total - most), min(most, total - 1) + 1)
        return jnp.stack([one, total - one])
    lengths = jnp.asarray(length_profile(amount, total, most, slope), jnp.int32)
    pairs = (amount - 1) // 2
    donor, receiver = lengths[1:1 + 2 * pairs:2], lengths[2:2 + 2 * pairs:2]
    slack = jnp.minimum(donor - 1, most - receiver)
    shifted = jax.random.randint(jax.random.fold_in(stream_key, 1), (pairs,), 0, 1 << 20) % (slack + 1)
    lengths = lengths.at[1:1 + 2 * pairs:2].set(donor - shifted).at[2:2 + 2 * pairs:2].set(receiver + shifted)
    return lengths[jax.random.permutation(jax.random.fold_in(stream_key, 2), amount)]


def gaussian(stream_key, shape, scale, bound, shards=(), kind=jnp.bfloat16):
    values = jax.random.normal(stream_key, shape, jnp.float32) * scale
    if len(shards) > 0:
        values = block_levels(stream_key, shape, shards, -0.22, 0.18) * values
    return jnp.clip(values, min=-bound, max=bound).astype(kind)


def setup_inputs(seed: int = 0) -> dict:
    streams_of = jax.random.split(jax.random.key(seed), 25)
    return {
        "patches": gaussian(streams_of[0], (ROWS, LEN, D), 1.0, 6.0, ((0, 8),)),
        "segment_ids": jax.vmap(lambda own: jnp.searchsorted(jnp.cumsum(ragged(own, CLIPS, LEN, LEN // 2, 0)), jnp.arange(LEN), side="right"))(jax.random.split(streams_of[1], ROWS)).reshape((ROWS, LEN)).astype(jnp.int32),
        "mask_flags": touch_ends((jax.random.randint(streams_of[2], (ROWS, LEN), 0, 5) < 2).astype(jnp.int32), jax.random.fold_in(streams_of[2], 1), 0, 1),
        "upstream": gaussian(streams_of[3], (ROWS, LEN, D), 1.0, 6.0, ((0, 8),)),
        "mask_embed": gaussian(streams_of[4], (D,), 1.0, 6.0, (), jnp.float32),
        "norm_gain": jnp.clip(1.0 + 0.1 * jax.random.normal(streams_of[5], (LAYERS, 2, D), jnp.float32), 0.5, 1.5),
        "norm_shift": gaussian(streams_of[6], (LAYERS, 2, D), 0.3, 2.0, (), jnp.float32),
        "in_weight": gaussian(streams_of[7], (LAYERS, D, 3, HH), D ** -0.5, 0.21875, ((3, 4),)),
        "in_bias": gaussian(streams_of[8], (LAYERS, 2, HH), 0.3, 2.0, ((2, 4),), jnp.float32),
        "out_weight": gaussian(streams_of[9], (LAYERS, HH, D), (HH // 16) ** -0.5, 0.875, ((1, 4),)),
        "out_bias": gaussian(streams_of[10], (LAYERS, 2, D), 0.3, 2.0, (), jnp.float32),
        "up_weight": gaussian(streams_of[11], (LAYERS, D, FF), D ** -0.5, 0.21875, ((2, 4),)),
        "up_bias": gaussian(streams_of[12], (LAYERS, FF), 0.3, 2.0, ((1, 4),), jnp.float32),
        "down_weight": gaussian(streams_of[13], (LAYERS, FF, D), FF ** -0.5, 0.109375, ((1, 4),)),
        "slow_mask_embed": gaussian(streams_of[14], (D,), 1.0, 6.0, (), jnp.float32),
        "slow_norm_gain": gaussian(streams_of[15], (LAYERS, 2, D), 0.5, 3.0, (), jnp.float32),
        "slow_norm_shift": gaussian(streams_of[16], (LAYERS, 2, D), 0.3, 2.0, (), jnp.float32),
        "slow_in_weight": gaussian(streams_of[17], (LAYERS, D, 3, HH), D ** -0.5, 0.21875, ((1, 8), (3, 4)), jnp.float32),
        "slow_in_bias": gaussian(streams_of[18], (LAYERS, 2, HH), 0.3, 2.0, ((2, 4),), jnp.float32),
        "slow_out_weight": gaussian(streams_of[19], (LAYERS, HH, D), (HH // 16) ** -0.5, 0.875, ((1, 4), (2, 8)), jnp.float32),
        "slow_out_bias": gaussian(streams_of[20], (LAYERS, 2, D), 0.3, 2.0, (), jnp.float32),
        "slow_up_weight": gaussian(streams_of[21], (LAYERS, D, FF), D ** -0.5, 0.21875, ((1, 8), (2, 4)), jnp.float32),
        "slow_up_bias": gaussian(streams_of[22], (LAYERS, FF), 0.3, 2.0, ((1, 4),), jnp.float32),
        "slow_down_weight": gaussian(streams_of[23], (LAYERS, FF, D), FF ** -0.5, 0.109375, ((1, 4), (2, 8)), jnp.float32),
    }


@jax.custom_vjp
def low(v):
    return lax.optimization_barrier(v.astype(jnp.bfloat16)).astype(jnp.float32)

@jax.custom_vjp
def low_back(v):
    return v

def low_keep(v):
    return (low(v), None)

def low_pass(kept, grad):
    return (grad,)

def back_keep(v):
    return (v, None)

def back_low(kept, grad):
    return (low(grad),)
low.defvjp(low_keep, low_pass)
low_back.defvjp(back_keep, back_low)
HIGHEST = lax.Precision.HIGHEST
EPSILON = 1e-06
DECAY = 0.8
NEGATIVE = -1e+30

def rounded_both(values):
    return low(low_back(values))

def layer_norm(values, gain, shift):
    center = values - lax.optimization_barrier(jnp.mean(values, axis=-1, keepdims=True))
    spread = lax.optimization_barrier(jnp.mean(center * center, axis=-1, keepdims=True))
    return center * lax.rsqrt(spread + EPSILON) * gain + shift

def grouped_sum(left, right):
    width = left.shape[1] // N_TP
    total = jnp.zeros((left.shape[0], right.shape[1]), left.dtype)
    for group_id in range(N_TP):
        first = group_id * width
        term = jnp.dot(left[:, first:first + width], right[first:first + width], precision=HIGHEST)
        total = total + low(term)
    return total

def grouped_project(normed, weight, bias):
    width = weight.shape[2] // N_TP
    pieces = []
    for group_id in range(N_TP):
        first = group_id * width
        piece = jnp.einsum('nd,dcw->ncw', low_back(normed), weight[:, :, first:first + width], precision=HIGHEST)
        pieces.append(piece + bias[:, first:first + width])
    return jnp.concatenate(pieces, axis=2)

def attention(queries, keys, values, segments):
    scores = jnp.einsum('bqhd,bkhd->bhqk', queries, keys, precision=HIGHEST) * HD ** (-0.5)
    scores = low_back(scores)
    same = segments[:, None, :, None] == segments[:, None, None, :]
    scores = jnp.where(same, scores, NEGATIVE)
    top = lax.optimization_barrier(jnp.max(scores, axis=-1, keepdims=True))
    expo = jnp.exp(scores - top)
    probs = expo / lax.optimization_barrier(jnp.sum(expo, axis=-1, keepdims=True))
    return jnp.einsum('bhqk,bkhd->bqhd', low(probs), values, precision=HIGHEST)

def block_forward(hidden, params, segments):
    gain, shift, in_w, in_b, out_w, out_b, up_w, up_b, down_w = params
    batch = hidden.shape[0]
    tokens = hidden.reshape(-1, D)
    normed = low(layer_norm(tokens, gain[0], shift[0]))
    bias_in = jnp.stack([in_b[0], jnp.zeros_like(in_b[0]), in_b[1]])
    projected = rounded_both(grouped_project(normed, in_w, bias_in))
    shaped = projected.reshape(batch, LEN, 3, HEADS, HD)
    mixed = attention(shaped[:, :, 0], shaped[:, :, 1], shaped[:, :, 2], segments)
    mixed = rounded_both(mixed.reshape(-1, HH))
    after = tokens + low_back(grouped_sum(mixed, out_w)) + out_b[0]
    normed_two = low(layer_norm(after, gain[1], shift[1]))
    upward = low_back(grouped_project(normed_two, up_w[:, None, :], up_b[None, :])[:, 0])
    active = low(jax.nn.gelu(upward, approximate=False))
    result = after + low_back(grouped_sum(active, down_w)) + out_b[1]
    return result.reshape(batch, LEN, D)

def forward(weights, patches, flags, segments):
    embed, gains, shifts, in_w, in_b, out_w, out_b, up_w, up_b, down_w = weights
    hidden = jnp.where(flags[..., None] > 0, embed, patches)
    for layer_id in range(LAYERS):
        params = (gains[layer_id], shifts[layer_id], in_w[layer_id], in_b[layer_id], out_w[layer_id], out_b[layer_id], up_w[layer_id], up_b[layer_id], down_w[layer_id])
        hidden = block_forward(hidden, params, segments)
    return hidden

def reference(patches, segment_ids, mask_flags, upstream, mask_embed, norm_gain, norm_shift, in_weight, in_bias, out_weight, out_bias, up_weight, up_bias, down_weight, slow_mask_embed, slow_norm_gain, slow_norm_shift, slow_in_weight, slow_in_bias, slow_out_weight, slow_out_bias, slow_up_weight, slow_up_bias, slow_down_weight):
    weights = tuple((item.astype(jnp.float32) for item in (mask_embed, norm_gain, norm_shift, in_weight, in_bias, out_weight, out_bias, up_weight, up_bias, down_weight)))
    group = math.gcd(ROWS, max(1, 2048 // LEN))
    steps_count = ROWS // group

    def regroup(array):
        return array.reshape((steps_count, group) + array.shape[1:])

    def one_group(totals, inputs):
        rows_in, segments, flags, cotangent = inputs

        def local_forward(params, values):
            return forward(params, values, flags, segments)
        result, pullback = jax.vjp(local_forward, weights, rows_in.astype(jnp.float32))
        grad_weights, grad_values = pullback(cotangent.astype(jnp.float32))
        totals = jax.tree.map(jnp.add, totals, grad_weights)
        return (totals, (result.astype(jnp.bfloat16), grad_values.astype(jnp.bfloat16)))
    zeros = jax.tree.map(jnp.zeros_like, weights)
    totals, (results, grad_values) = lax.scan(one_group, zeros, (regroup(patches), regroup(segment_ids), regroup(mask_flags), regroup(upstream)))
    layer_out = results.reshape(ROWS, LEN, D)
    grad_patches = grad_values.reshape(ROWS, LEN, D)
    slows = (slow_mask_embed, slow_norm_gain, slow_norm_shift, slow_in_weight, slow_in_bias, slow_out_weight, slow_out_bias, slow_up_weight, slow_up_bias, slow_down_weight)
    fresh = tuple((DECAY * slow + (1.0 - DECAY) * weight for slow, weight in zip(slows, weights)))
    return (layer_out, grad_patches, totals[0], totals[1], totals[2], totals[3], totals[4], totals[5], totals[6], totals[7], totals[8], totals[9], fresh[0], fresh[1], fresh[2], fresh[3], fresh[4], fresh[5], fresh[6], fresh[7], fresh[8], fresh[9])
```

```python
import jax
import jax.numpy as jnp
from jax import lax
from jax.sharding import PartitionSpec as P

HD = 64
LAYERS = 2
EPSILON = 1e-06
DECAY = 0.8
NEGATIVE = -1e30
F32 = jnp.float32
BF16 = jnp.bfloat16


def swap(x, axis, bit):
    n = lax.axis_size(axis)
    return lax.ppermute(x, axis, [(i, i ^ bit) for i in range(n)])


def tp_sum(p):
    count, width = p.shape
    core = lax.axis_index("tp") % 2
    halves = p.reshape(2, count // 2, width)
    keep = lax.dynamic_index_in_dim(halves, core, 0, keepdims=False)
    send = lax.dynamic_index_in_dim(halves, 1 - core, 0, keepdims=False)
    s = (keep.astype(F32) + swap(send, "tp", 1).astype(F32)).astype(BF16)
    t = (s.astype(F32) + swap(s, "tp", 2).astype(F32)).astype(BF16)
    o = swap(t, "tp", 1)
    low = jnp.where(core == 0, t, o)
    high = jnp.where(core == 0, o, t)
    return jnp.concatenate([low, high], axis=0)


def tp_gather(x):
    me = lax.axis_index("tp")
    two = jnp.stack([x, swap(x, "tp", 2)])
    four = jnp.concatenate([two, swap(two, "tp", 1)])
    order = jnp.array([0, 2, 1, 3])
    return jnp.stack(
        [lax.dynamic_index_in_dim(four, order[g ^ me], 0, keepdims=False) for g in range(4)]
    )


def rows_scatter(g):
    size = lax.axis_size("rows")
    me = lax.axis_index("rows")
    width, n = g.shape
    cur = g.reshape(size, width // size, n)
    bit = 1
    while bit < size:
        pairs = cur.reshape(cur.shape[0] // 2, 2, *cur.shape[1:])
        mine = (me // bit) % 2
        keep = lax.dynamic_index_in_dim(pairs, mine, 1, keepdims=False)
        send = lax.dynamic_index_in_dim(pairs, 1 - mine, 1, keepdims=False)
        got = swap(send.astype(BF16), "rows", bit)
        cur = keep.astype(F32) + got.astype(F32)
        bit *= 2
    return cur[0]


def rows_sum(v):
    size = lax.axis_size("rows")
    bit = 1
    while bit < size:
        v = v + swap(v, "rows", bit)
        bit *= 2
    return v


def layer_norm(values, gain, shift):
    center = values - jnp.mean(values, axis=-1, keepdims=True)
    spread = jnp.mean(center * center, axis=-1, keepdims=True)
    return center * lax.rsqrt(spread + EPSILON) * gain + shift


def norm_parts(values):
    center = values - jnp.mean(values, axis=-1, keepdims=True)
    spread = jnp.mean(center * center, axis=-1, keepdims=True)
    inv = lax.rsqrt(spread + EPSILON)
    return center * inv, inv


def norm_back(values, gain, cot):
    hat, inv = norm_parts(values)
    w = cot * gain
    mean_w = jnp.mean(w, axis=-1, keepdims=True)
    mean_wh = jnp.mean(w * hat, axis=-1, keepdims=True)
    return inv * (w - mean_w - hat * mean_wh), cot * hat


def masked_scores(q, k, seg):
    scores = jnp.einsum("qhd,khd->hqk", q, k, preferred_element_type=F32) * HD ** (-0.5)
    return jnp.where((seg[:, None] == seg[None, :])[None], scores, NEGATIVE)


def attend(q, k, v, seg):
    scores = masked_scores(q, k, seg)
    top = jnp.max(scores, axis=-1, keepdims=True)
    expo = jnp.exp(scores - top)
    total = jnp.sum(expo, axis=-1, keepdims=True)
    probs = (expo / total).astype(BF16)
    mixed = jnp.einsum("hqk,khd->qhd", probs, v, preferred_element_type=F32)
    return mixed, (top + jnp.log(total))[..., 0]


def attend_back(q, k, v, seg, lse, grad):
    probs = jnp.exp(masked_scores(q, k, seg) - lse[..., None])
    grad_probs = jnp.einsum("qhd,khd->hqk", grad, v, preferred_element_type=F32)
    gv = jnp.einsum("hqk,qhd->khd", probs.astype(BF16), grad, preferred_element_type=F32)
    inner = jnp.sum(probs * grad_probs, axis=-1, keepdims=True)
    gs = (probs * (grad_probs - inner)).astype(BF16)
    gq = jnp.einsum("hqk,khd->qhd", gs, k, preferred_element_type=F32) * HD ** (-0.5)
    gk = jnp.einsum("hqk,qhd->khd", gs, q, preferred_element_type=F32) * HD ** (-0.5)
    return gq, gk, gv


def gelu_both(u):
    phi = 0.5 * (1.0 + lax.erf(u * (0.5**0.5)))
    return u * phi, phi + u * jnp.exp(-0.5 * u * u) * 0.3989422804014327


def dot(a, b):
    return jnp.dot(a, b, preferred_element_type=F32)


def dot_t(a, b):
    return lax.dot_general(a, b, (((1,), (1,)), ((), ())), preferred_element_type=F32)


def t_dot(a, b):
    return lax.dot_general(a, b, (((0,), (0,)), ((), ())), preferred_element_type=F32)


def per_device(
    patches,
    segment_ids,
    mask_flags,
    upstream,
    mask_embed,
    norm_gain,
    norm_shift,
    in_weight,
    in_bias,
    out_weight,
    out_bias,
    up_weight,
    up_bias,
    down_weight,
    slow_mask_embed,
    slow_norm_gain,
    slow_norm_shift,
    slow_in_weight,
    slow_in_bias,
    slow_out_weight,
    slow_out_bias,
    slow_up_weight,
    slow_up_bias,
    slow_down_weight,
):
    rows_here, length, width = patches.shape
    count = rows_here * length
    cols = in_weight.shape[3]
    heads_here = cols // HD
    seg = segment_ids.reshape(count)
    flags = mask_flags.reshape(count, 1) > 0
    hidden = jnp.where(flags, mask_embed[None, :], patches.reshape(count, width).astype(F32))
    top_grad = upstream.reshape(count, width)
    out_full = tp_gather(out_weight)
    out_full = [out_full[:, l].reshape(-1, width) for l in range(LAYERS)]
    weights_in = [in_weight[l].reshape(width, 3 * cols) for l in range(LAYERS)]

    kept = []
    for l in range(LAYERS):
        normed = layer_norm(hidden, norm_gain[l, 0], norm_shift[l, 0]).astype(BF16)
        bias_in = jnp.concatenate([in_bias[l, 0], jnp.zeros_like(in_bias[l, 0]), in_bias[l, 1]])
        projected = (dot(normed, weights_in[l]) + bias_in).astype(BF16)
        q, k, v = (
            projected[:, c * cols : (c + 1) * cols].reshape(count, heads_here, HD) for c in range(3)
        )
        mixed, lse = attend(q, k, v, seg)
        mixed = mixed.reshape(count, cols).astype(BF16)
        gathered = tp_gather(mixed)
        after = hidden + out_bias[l, 0]
        after = after + dot(jnp.concatenate([gathered[g] for g in range(4)], axis=1), out_full[l])
        normed_two = layer_norm(after, norm_gain[l, 1], norm_shift[l, 1]).astype(BF16)
        upward = dot(normed_two, up_weight[l]) + up_bias[l]
        active, slope = gelu_both(upward)
        active = active.astype(BF16)
        feed = tp_sum(dot(active, down_weight[l]).astype(BF16))
        kept.append((hidden, normed, q, k, v, lse, mixed, after, normed_two, active, slope.astype(BF16)))
        hidden = after + feed.astype(F32) + out_bias[l, 1]
    layer_out = hidden.astype(BF16).reshape(patches.shape)

    grad_hidden = top_grad.astype(F32)
    sums = {}
    scattered = [None] * LAYERS
    for l in reversed(range(LAYERS)):
        entry, normed, q, k, v, lse, mixed, after, normed_two, active, slope = kept[l]
        sums["down_bias", l] = jnp.sum(grad_hidden, axis=0)
        branch = grad_hidden.astype(BF16)
        grad_upward = (dot_t(branch, down_weight[l]) * slope.astype(F32)).astype(BF16)
        sums["up_bias", l] = jnp.sum(grad_upward, axis=0, dtype=F32)
        share = dot_t(grad_upward, up_weight[l]).astype(BF16)
        grad_two = tp_sum(share).astype(F32)
        first = jnp.concatenate([t_dot(branch, active), t_dot(normed_two, grad_upward)], axis=1)
        scat_one = rows_scatter(first)
        pulled, prod = norm_back(after, norm_gain[l, 1], grad_two)
        sums["gain", l, 1] = jnp.sum(prod, axis=0)
        sums["shift", l, 1] = jnp.sum(grad_two, axis=0)
        grad_after = pulled + grad_hidden
        sums["out_bias", l] = jnp.sum(grad_after, axis=0)
        attn = grad_after.astype(BF16)
        grad_mixed = dot_t(attn, out_weight[l]).astype(BF16)
        gq, gk, gv = attend_back(q, k, v, seg, lse, grad_mixed.reshape(count, heads_here, HD))
        grad_proj = jnp.concatenate([g.reshape(count, cols) for g in (gq, gk, gv)], axis=1).astype(BF16)
        col = jnp.sum(grad_proj, axis=0, dtype=F32)
        sums["in_bias", l] = jnp.stack([col[:cols], col[2 * cols :]])
        share = dot_t(grad_proj, weights_in[l]).astype(BF16)
        second = jnp.concatenate([t_dot(normed, grad_proj), t_dot(attn, mixed)], axis=1)
        scat_two = rows_scatter(second)
        scattered[l] = (scat_one, scat_two)
        pulled, prod = norm_back(entry, norm_gain[l, 0], share.astype(F32))
        sums["gain", l, 0] = jnp.sum(prod, axis=0)
        sums["shift", l, 0] = jnp.sum(share, axis=0, dtype=F32)
        if l == 0:
            both = pulled + 0.25 * grad_after
            sums["embed"] = jnp.sum(jnp.where(flags, both, 0.0), axis=0)
        grad_one = tp_sum(share).astype(F32)
        grad_hidden = norm_back(entry, norm_gain[l, 0], grad_one)[0] + grad_after
    grad_patches = jnp.where(flags, 0.0, grad_hidden).astype(BF16).reshape(patches.shape)

    quarter = 0.25
    vec = [sums["embed"]]
    for l in range(LAYERS):
        vec += [sums["gain", l, 0], quarter * sums["gain", l, 1]]
    for l in range(LAYERS):
        vec += [sums["shift", l, 0], quarter * sums["shift", l, 1]]
    for l in range(LAYERS):
        vec += [quarter * sums["out_bias", l], quarter * sums["down_bias", l]]
    vec = jnp.stack(vec)
    vec = vec + swap(vec, "tp", 1)
    vec = vec + swap(vec, "tp", 2)
    own = jnp.stack(
        [sums["up_bias", l] for l in range(LAYERS)]
        + [jnp.concatenate([sums["in_bias", l].reshape(-1) for l in range(LAYERS)])]
    )
    vec = rows_sum(jnp.concatenate([vec, own]))
    grad_mask_embed = vec[0]
    grad_norm_gain = vec[1:5].reshape(LAYERS, 2, width)
    grad_norm_shift = vec[5:9].reshape(LAYERS, 2, width)
    grad_out_bias = vec[9:13].reshape(LAYERS, 2, width)
    grad_up_bias = vec[13:15]
    grad_in_bias = vec[15].reshape(LAYERS, 2, cols)

    ff = down_weight.shape[1]
    grad_in_weight = jnp.stack([s[1][:, : 3 * cols].reshape(-1, 3, cols) for s in scattered])
    grad_out_weight = jnp.stack([s[1][:, 3 * cols :].T for s in scattered])
    grad_up_weight = jnp.stack([s[0][:, ff:] for s in scattered])
    grad_down_weight = jnp.stack([s[0][:, :ff].T for s in scattered])

    piece = width // lax.axis_size("rows")
    start = lax.axis_index("rows") * piece

    def blend(slow, weight):
        return DECAY * slow + (1.0 - DECAY) * weight.astype(F32)

    return (
        layer_out,
        grad_patches,
        grad_mask_embed,
        grad_norm_gain,
        grad_norm_shift,
        grad_in_weight,
        grad_in_bias,
        grad_out_weight,
        grad_out_bias,
        grad_up_weight,
        grad_up_bias,
        grad_down_weight,
        blend(slow_mask_embed, mask_embed),
        blend(slow_norm_gain, norm_gain),
        blend(slow_norm_shift, norm_shift),
        blend(slow_in_weight, lax.dynamic_slice_in_dim(in_weight, start, piece, 1)),
        blend(slow_in_bias, in_bias),
        blend(slow_out_weight, lax.dynamic_slice_in_dim(out_weight, start, piece, 2)),
        blend(slow_out_bias, out_bias),
        blend(slow_up_weight, lax.dynamic_slice_in_dim(up_weight, start, piece, 1)),
        blend(slow_up_bias, up_bias),
        blend(slow_down_weight, lax.dynamic_slice_in_dim(down_weight, start, piece, 2)),
    )


def solution(mesh):
    placed = (
        P("rows", None, None),
        P("rows", None),
        P("rows", None),
        P("rows", None, None),
        P(),
        P(),
        P(),
        P(None, None, None, "tp"),
        P(None, None, "tp"),
        P(None, "tp", None),
        P(),
        P(None, None, "tp"),
        P(None, "tp"),
        P(None, "tp", None),
        P(),
        P(),
        P(),
        P(None, "rows", None, "tp"),
        P(None, None, "tp"),
        P(None, "tp", "rows"),
        P(),
        P(None, "rows", "tp"),
        P(None, "tp"),
        P(None, "tp", "rows"),
    )
    return jax.shard_map(
        per_device,
        mesh=mesh,
        in_specs=placed,
        out_specs=(
            P("rows", None, None),
            P("rows", None, None),
            P(),
            P(),
            P(),
            P(None, "rows", None, "tp"),
            P(None, None, "tp"),
            P(None, "tp", "rows"),
            P(),
            P(None, "rows", "tp"),
            P(None, "tp"),
            P(None, "tp", "rows"),
            P(),
            P(),
            P(),
            P(None, "rows", None, "tp"),
            P(None, None, "tp"),
            P(None, "tp", "rows"),
            P(),
            P(None, "rows", "tp"),
            P(None, "tp"),
            P(None, "tp", "rows"),
        ),
        check_vma=False,
    )
```

```python
import functools

import jax
import jax.numpy as jnp
from jax import lax
from jax.experimental import pallas as pl
from jax.experimental.pallas import tpu as pltpu
from jax.sharding import PartitionSpec as P

HD = 64
LAYERS = 2
EPSILON = 1e-06
DECAY = 0.8
NEGATIVE = -1e30
F32 = jnp.float32
BF16 = jnp.bfloat16


def swap(x, axis, bit):
    n = lax.axis_size(axis)
    return lax.ppermute(x, axis, [(i, i ^ bit) for i in range(n)])


def shape(dims, dtype=BF16):
    return jax.ShapeDtypeStruct(tuple(dims), dtype)


def run(body, outs, args, after=(), scratch=(), flops=0, vmem=16):
    n_in, n_after = len(args), len(after)

    def kernel(*refs):
        me = lax.axis_index("tp")
        body((me % 2, me, lax.axis_index("rows")), *refs[:n_in], *refs[n_in + n_after :])

    moved = sum(a.size * a.dtype.itemsize for a in list(args) + list(outs))
    return pl.pallas_call(
        kernel,
        in_specs=[pl.BlockSpec(memory_space=pltpu.VMEM)] * n_in + [pl.BlockSpec(memory_space=pl.ANY)] * n_after,
        out_specs=[pl.BlockSpec(memory_space=pltpu.VMEM)] * len(outs),
        out_shape=outs,
        scratch_shapes=scratch,
        name=body.__name__,
        compiler_params=pltpu.CompilerParams(vmem_limit_bytes=vmem * 1024 * 1024),
        cost_estimate=pl.CostEstimate(flops=flops, bytes_accessed=moved, transcendentals=0),
    )(*args, *after)


def dot(a, b):
    return jnp.dot(a, b, preferred_element_type=F32)


def dot_t(a, b):
    return lax.dot_general(a, b, (((1,), (1,)), ((), ())), preferred_element_type=F32)


def t_dot(a, b):
    return lax.dot_general(a, b, (((0,), (0,)), ((), ())), preferred_element_type=F32)


GAIN, SHIFT, OUT_BIAS, UP_BIAS, EMBED, SEG, FLAG, IN_BIAS, PACKED = 0, 4, 8, 12, 14, 15, 16, 17, 24
V_EMBED, V_GAIN, V_SHIFT, V_OUT, OWN, V_UP, V_IN, SUMMED = 0, 1, 5, 9, 13, 13, 15, 24


def norm_parts(values):
    center = values - jnp.mean(values, axis=-1, keepdims=True)
    spread = jnp.mean(center * center, axis=-1, keepdims=True)
    inv = lax.rsqrt(spread + EPSILON)
    return center * inv, inv


def norm_back(values, gain, cot):
    hat, inv = norm_parts(values)
    w = cot * gain
    mean_w = jnp.mean(w, axis=-1, keepdims=True)
    mean_wh = jnp.mean(w * hat, axis=-1, keepdims=True)
    return inv * (w - mean_w - hat * mean_wh), cot * hat


def column(row, lanes=128):
    return jnp.transpose(jnp.broadcast_to(row, (lanes, row.shape[1])))


def split_three(v):
    one = v.astype(BF16).astype(F32)
    two = (v - one).astype(BF16).astype(F32)
    return one, two, v - one - two


def halves_of(ref):
    half = ref.shape[0] // 2
    return [slice(i * half, i * half + half) for i in range(2)]


def row_of(pack, i):
    return pack[i : i + 1, :]


def add_rows(ref, i, rows):
    if i == 0:
        ref[...] = jnp.zeros_like(ref)
    for n, r in enumerate(rows):
        ref[n : n + 1, :] += jnp.sum(r, axis=0, keepdims=True)


def share_out(at, held, send_ref, keep_ref):
    send_ref[...] = held[1 - at[0]]
    keep_ref[...] = held[at[0]]


def joined(at, i, own_ref, other_ref):
    return jnp.where(at[0] == i, own_ref[...].astype(F32), other_ref[...].astype(F32))


def entry_of(patches_ref, pack, at):
    on = column(pack[FLAG : FLAG + 1, at])[:, :1] > 0.0
    return jnp.where(on, row_of(pack, EMBED), patches_ref[at, :].astype(F32)), on


def project(x, l, pack, weight_ref, normed_ref, qkv_ref, at):
    hat, _ = norm_parts(x)
    normed = (hat * row_of(pack, GAIN + 2 * l) + row_of(pack, SHIFT + 2 * l)).astype(BF16)
    normed_ref[at, :] = normed
    bias = row_of(pack, IN_BIAS + l)
    part, cols = qkv_ref.shape[1] // 3, weight_ref.shape[2]
    for c in range(3):
        first = c * part
        out = (dot_t(normed, weight_ref[l, c]) + bias[:, first : first + cols]).astype(BF16)
        if c == 0:
            out = out * jnp.asarray(HD**-0.5, BF16)
        qkv_ref[at, first : first + cols] = out
        qkv_ref[at, first + cols : first + part] = jnp.zeros((out.shape[0], part - cols), BF16)


def pack_kernel(_, gain, shift, out_bias, up_bias, embed, seg, flags, in_bias, pack):
    pack[...] = jnp.zeros_like(pack)
    for l in range(LAYERS):
        for base, ref in ((GAIN, gain), (SHIFT, shift), (OUT_BIAS, out_bias)):
            pack[base + 2 * l : base + 2 * l + 2, :] = ref[l]
        cols = in_bias.shape[2]
        last = pack.shape[1] // 3 * 2
        pack[IN_BIAS + l : IN_BIAS + l + 1, :cols] = in_bias[l, 0:1]
        pack[IN_BIAS + l : IN_BIAS + l + 1, last : last + cols] = in_bias[l, 1:2]
    pack[UP_BIAS : UP_BIAS + LAYERS, :] = up_bias[...]
    pack[EMBED : EMBED + 1, :] = embed[...].reshape(1, pack.shape[1])
    pack[SEG : SEG + 1, :] = seg[...].astype(F32)
    pack[FLAG : FLAG + 1, :] = flags[...].astype(F32)


def first_project_kernel(_, patches, pack, weight, normed, qkv):
    for at in halves_of(patches):
        x, _on = entry_of(patches, pack, at)
        project(x, 0, pack, weight, normed, qkv, at)


def next_project_kernel(at, after, own, other, pack, weight, x_ref, normed, qkv):
    for i, rows in enumerate(halves_of(after)):
        x = after[rows, :] + joined(at, i, own, other) + row_of(pack, OUT_BIAS + 1)
        x_ref[rows, :] = x
        project(x, 1, pack, weight, normed, qkv, rows)


def head_lanes(rows, h):
    lane = lax.broadcasted_iota(jnp.int32, (rows, 128), 1)
    upper = lane >= 64
    mine = upper if h % 2 else jnp.logical_not(upper)
    return mine, lane % 64


def attend_kernel(_, qkv, pack, mixed_ref, held_ref):
    length, part = qkv.shape[0], qkv.shape[1] // 3
    heads, width = held_ref.shape[1] // 128, mixed_ref.shape[1]
    seg = column(row_of(pack, SEG)).astype(jnp.int32)
    step = 256
    for h in range(heads):
        lanes = h // 2 * 128
        mine, place = head_lanes(length, h)
        apart = jnp.where((place < 4) & (place != seg), NEGATIVE, 0.0)
        keys = jnp.where(mine, qkv[:, part + lanes : part + lanes + 128].astype(F32), apart).astype(BF16)
        size = min(128, width - lanes)
        mine, place = mine[:step], place[:step]
        for q0 in range(0, length, step):
            at = slice(q0, q0 + step)
            marks = (place == seg[at]).astype(F32)
            q = qkv[at, lanes : lanes + 128].astype(F32)
            scores = dot_t(jnp.where(mine, q, marks).astype(BF16), keys)
            top = jnp.max(scores, axis=-1, keepdims=True)
            expo = jnp.exp(scores - top)
            total = jnp.sum(expo, axis=-1, keepdims=True)
            out = dot(expo.astype(BF16), qkv[:, 2 * part + lanes : 2 * part + lanes + 128]) / total
            one, two, three = split_three(-(top + jnp.log(total)))
            marks = marks + jnp.where(
                place == 4, one, jnp.where(place == 5, two, jnp.where(place == 6, three, 0.0))
            )
            held_ref[at, h * 128 : h * 128 + 128] = jnp.where(mine, q, marks).astype(BF16)
            if h % 2:
                out = jnp.where(mine, out, mixed_ref[at, lanes : lanes + 128].astype(F32))
            mixed_ref[at, lanes : lanes + size] = out[:, :size].astype(BF16)


def gelu_both(u):
    phi = 0.5 * (1.0 + lax.erf(u * (0.5**0.5)))
    return u * phi, phi + u * jnp.exp(-0.5 * u * u) * 0.3989422804014327


def in_order(me, own, far, near, last):
    core, chip = me % 2 == 1, me // 2 == 1

    def pick(on, one, two):
        return jnp.where(on, two, one), jnp.where(on, one, two)

    own, far = pick(chip, own, far)
    near, last = pick(chip, near, last)
    own, near = pick(core, own, near)
    far, last = pick(core, far, last)
    return own, near, far, last


def order_kernel(at, own, far, near, last, out):
    for l in range(own.shape[0]):
        for g, w in enumerate(in_order(at[1], own[l], far[l], near[l], last[l])):
            out[l, g * w.shape[0] : g * w.shape[0] + w.shape[0], :] = w


def feed_front(at, l, x, rows, mixed, weights, pack, up, after_ref, normed_ref):
    after = x + row_of(pack, OUT_BIAS + 2 * l)
    size = mixed[0].shape[1]
    for g, m in enumerate(in_order(at[1], *[m[rows, :] for m in mixed])):
        after = after + dot(m, weights[l, g * size : g * size + size, :])
    after_ref[rows, :] = after
    hat, _ = norm_parts(after)
    normed = (hat * row_of(pack, GAIN + 2 * l + 1) + row_of(pack, SHIFT + 2 * l + 1)).astype(BF16)
    normed_ref[rows, :] = normed
    return gelu_both(dot(normed, up[l]) + row_of(pack, UP_BIAS + l))


def first_feed_kernel(
    at, patches, m0, m1, m2, m3, weights, pack, up, down,
    after_ref, normed_ref, active_ref, slope_ref, send_ref, keep_ref, held,
):
    for i, rows in enumerate(halves_of(patches)):
        x, _ = entry_of(patches, pack, rows)
        active, slope = feed_front(at, 0, x, rows, (m0, m1, m2, m3), weights, pack, up, after_ref, normed_ref)
        active = active.astype(BF16)
        active_ref[rows, :] = active
        slope_ref[rows, :] = slope.astype(BF16)
        held[i] = dot(active, down[0]).astype(BF16)
    share_out(at, held, send_ref, keep_ref)


def last_feed_kernel(
    at, x, m0, m1, m2, m3, weights, pack, up, down, top,
    after_ref, normed_ref, active_ref, dup_ref, send_ref, keep_ref, sums_ref, held,
):
    for i, rows in enumerate(halves_of(x)):
        active, slope = feed_front(
            at, 1, x[rows, :], rows, (m0, m1, m2, m3), weights, pack, up, after_ref, normed_ref
        )
        active_ref[rows, :] = active.astype(BF16)
        dup = (dot_t(top[rows, :], down[1]) * slope).astype(BF16)
        dup_ref[rows, :] = dup
        add_rows(sums_ref, i, [dup.astype(F32), top[rows, :].astype(F32)])
        held[i] = dot_t(dup, up[1]).astype(BF16)
    share_out(at, held, send_ref, keep_ref)


def down_kernel(at, active, down, send_ref, keep_ref, held):
    for i, rows in enumerate(halves_of(active)):
        held[i] = dot(active[rows, :], down[1]).astype(BF16)
    share_out(at, held, send_ref, keep_ref)


def output_kernel(at, after, own, other, pack, out_ref):
    for i, rows in enumerate(halves_of(after)):
        out_ref[rows, :] = (after[rows, :] + joined(at, i, own, other) + row_of(pack, OUT_BIAS + 3)).astype(BF16)


def attn_front(l, at, after, own, other, above, pack, out_w, mixed, grad_ref, attn_ref, held_ref, sums_ref):
    width = mixed.shape[1]
    for i, rows in enumerate(halves_of(after)):
        cot = joined(at, i, own, other)
        pulled, prod = norm_back(after[rows, :], row_of(pack, GAIN + 2 * l + 1), cot)
        grad = pulled + above[rows, :].astype(F32)
        grad_ref[rows, :] = grad
        attn = grad.astype(BF16)
        attn_ref[rows, :] = attn
        add_rows(sums_ref, i, [prod, cot, grad])
        mixed_grad = dot_t(attn, out_w[l]).astype(BF16).astype(F32)
        count = attn.shape[0]
        for h in range(width // HD):
            lanes = h // 2 * 128
            mine, place = head_lanes(count, h)
            size = min(128, width - lanes)
            mix = mixed[rows, lanes : lanes + size].astype(F32)
            grads = mixed_grad[:, lanes : lanes + size]
            if size < 128:
                fill = jnp.zeros((count, 128 - size), F32)
                mix, grads = (jnp.concatenate([v, fill], axis=1) for v in (mix, grads))
            inner = jnp.sum(jnp.where(mine, mix * grads, 0.0), axis=-1, keepdims=True)
            one, two, three = split_three(-inner)
            marks = jnp.where(
                place == 4, one, jnp.where(place == 5, two, jnp.where(place == 6, three, 0.0))
            )
            held_ref[rows, h * 128 : h * 128 + 128] = jnp.where(mine, grads, marks).astype(BF16)


def attend_back(l, at, qkv, pack, q_held, g_held, weight, dproj_ref, send_ref, keep_ref, sums_ref, turned, held):
    length, width = qkv.shape
    part = width // 3
    heads = q_held.shape[1] // 128
    step = 256
    seg = column(row_of(pack, SEG)).astype(jnp.int32)
    for h in range(heads):
        lanes = h // 2 * 128
        mine, place = head_lanes(length, h)
        mine_step = mine[:step]
        ones = ((place >= 4) & (place < 7)).astype(F32)
        apart = jnp.where((place < 4) & (place != seg), NEGATIVE, ones)
        keys = jnp.where(mine, qkv[:, part + lanes : part + lanes + 128].astype(F32), apart).astype(BF16)
        values = jnp.where(mine, qkv[:, 2 * part + lanes : 2 * part + lanes + 128].astype(F32), ones).astype(BF16)
        qh = q_held[:, h * 128 : h * 128 + 128]
        gh = g_held[:, h * 128 : h * 128 + 128]
        for k0 in range(0, length, step):
            rows = slice(k0, k0 + step)
            probs = jnp.exp(dot_t(keys[rows], qh))
            ds = (probs * dot_t(values[rows], gh)).astype(BF16)
            gv = dot(probs.astype(BF16), gh).astype(BF16)
            gk = dot(ds, qh).astype(BF16)
            for base, g in ((part, gk), (2 * part, gv)):
                cols = slice(base + lanes, base + lanes + 128)
                if h % 2:
                    g = jnp.where(mine_step, g.astype(F32), dproj_ref[rows, cols].astype(F32)).astype(BF16)
                elif h == heads - 1:
                    g = jnp.where(mine_step, g.astype(F32), 0.0).astype(BF16)
                dproj_ref[rows, cols] = g
            dq = t_dot(qkv[rows, part + lanes : part + lanes + 128], ds)
            if k0 == 0:
                turned[...] = dq
            else:
                turned[...] += dq
        dq = jnp.transpose(turned[...]) * HD**-0.5
        cols = slice(lanes, lanes + 128)
        if h % 2:
            dq = jnp.where(mine, dq, dproj_ref[:, cols].astype(F32))
        elif h == heads - 1:
            dq = jnp.where(mine, dq, 0.0)
        dproj_ref[:, cols] = dq.astype(BF16)
    for i, rows in enumerate(halves_of(dproj_ref)):
        dproj = dproj_ref[rows, :]
        add_rows(sums_ref, i, [dproj.astype(F32)])
        cols = weight.shape[2]
        held[i] = sum(dot(dproj[:, c * part : c * part + cols], weight[l, c]) for c in range(3)).astype(BF16)
    share_out(at, held, send_ref, keep_ref)


def feed_back_kernel(
    at, x, own, other, above, pack, down, slope, up, grad_ref, branch_ref, dup_ref, send_ref, keep_ref, sums_ref, held
):
    for i, rows in enumerate(halves_of(x)):
        cot = joined(at, i, own, other)
        pulled, prod = norm_back(x[rows, :], row_of(pack, GAIN + 2), cot)
        grad = pulled + above[rows, :]
        grad_ref[rows, :] = grad
        branch = grad.astype(BF16)
        branch_ref[rows, :] = branch
        dup = (dot_t(branch, down[0]) * slope[rows, :].astype(F32)).astype(BF16)
        dup_ref[rows, :] = dup
        add_rows(sums_ref, i, [prod, cot, grad, dup.astype(F32)])
        held[i] = dot_t(dup, up[0]).astype(BF16)
    share_out(at, held, send_ref, keep_ref)


def tail_sums_kernel(
    at, patches, pack, own, other, above, feed_one, front_one, back_one, feed_zero, front_zero, back_zero, out
):
    out[...] = jnp.zeros_like(out)
    for i, rows in enumerate(halves_of(patches)):
        cot = joined(at, i, own, other)
        x, on = entry_of(patches, pack, rows)
        pulled, prod = norm_back(x, row_of(pack, GAIN), cot)
        both = jnp.where(on, pulled + 0.25 * above[rows, :], 0.0)
        for base, v in ((V_EMBED, both), (V_GAIN, prod), (V_SHIFT, cot)):
            out[base : base + 1, :] += jnp.sum(v, axis=0, keepdims=True)
    for base, v in (
        (V_GAIN + 1, front_zero[0:1, :]),
        (V_GAIN + 2, feed_zero[0:1, :]),
        (V_GAIN + 3, front_one[0:1, :]),
        (V_SHIFT + 1, front_zero[1:2, :]),
        (V_SHIFT + 2, feed_zero[1:2, :]),
        (V_SHIFT + 3, front_one[1:2, :]),
        (V_OUT, front_zero[2:3, :]),
        (V_OUT + 1, feed_zero[2:3, :]),
        (V_OUT + 2, front_one[2:3, :]),
        (V_OUT + 3, feed_one[1:2, :]),
    ):
        out[base : base + 1, :] = 0.25 * v
    out[V_UP : V_UP + 1, :] = feed_zero[3:4, :]
    out[V_UP + 1 : V_UP + 2, :] = feed_one[0:1, :]
    out[V_IN : V_IN + 1, :] = back_zero[0:1, :]
    out[V_IN + 1 : V_IN + 2, :] = back_one[0:1, :]


def add_shared_kernel(_, mine, got, out):
    row = lax.broadcasted_iota(jnp.int32, mine.shape, 0)
    out[...] = mine[...] + jnp.where(row < OWN, got[...], 0.0)


def add_kernel(_, mine, got, out):
    out[...] = mine[...] + got[...]


def unpack_kernel(_, mine, got, embed, gain, shift, in_bias, out_bias, up_bias):
    v = mine[...] + got[...]
    embed[...] = v[V_EMBED]
    cols = in_bias.shape[2]
    last = v.shape[1] // 3 * 2
    for l in range(LAYERS):
        for base, ref in ((V_GAIN, gain), (V_SHIFT, shift), (V_OUT, out_bias)):
            ref[l] = v[base + 2 * l : base + 2 * l + 2]
        in_bias[l, 0:1, :] = v[V_IN + l : V_IN + l + 1, :cols]
        in_bias[l, 1:2, :] = v[V_IN + l : V_IN + l + 1, last : last + cols]
    up_bias[...] = v[V_UP : V_UP + LAYERS]


def patches_kernel(at, patches, pack, own, other, above, out_ref):
    for i, rows in enumerate(halves_of(patches)):
        x, on = entry_of(patches, pack, rows)
        pulled, _ = norm_back(x, row_of(pack, GAIN), joined(at, i, own, other))
        out_ref[rows, :] = jnp.where(on, 0.0, pulled + above[rows, :]).astype(BF16)


def split_rows(value, held, size):
    rows = value.shape[0] // size
    for b in range(size):
        held[b % 2, b // 2] = value[b * rows : b * rows + rows].astype(BF16)


def feed_grads_kernel(at, branch, active, normed, dup, send_ref, keep_ref, held):
    size, width = held.shape[1] * 2, active.shape[1]
    for i, (a, b) in enumerate(((branch, active), (normed, dup))):
        split_rows(t_dot(a[...], b[...]), held, size)
        cols = slice(i * width, i * width + width)
        send_ref[:, :, cols] = held[1 - at[2] % 2]
        keep_ref[:, :, cols] = held[at[2] % 2]


def attn_grads_kernel(at, normed, dproj, attn, mixed, send_ref, keep_ref, held):
    size, cols = held.shape[1] * 2, mixed.shape[1]
    part = dproj.shape[1] // 3
    g = t_dot(normed[...], dproj[...])
    o = t_dot(attn[...], mixed[...])
    pieces = [g[:, c * part : c * part + cols] for c in range(3)] + [o]
    whole_lanes = [p[:, :128] for p in pieces]
    rest = [
        jnp.concatenate([pieces[i][:, 128:], pieces[i + 1][:, 128:]], axis=1) for i in range(0, 4, 2)
    ]
    split_rows(jnp.concatenate(whole_lanes + rest, axis=1), held, size)
    send_ref[...] = held[1 - at[2] % 2]
    keep_ref[...] = held[at[2] % 2]


def halve(bit, at, keep, got, send_ref, keep_ref):
    mine = (at[2] // bit) % 2
    for i in range(send_ref.shape[0]):
        for ref, j in ((send_ref, 2 * i + 1 - mine), (keep_ref, 2 * i + mine)):
            ref[i] = (keep[j].astype(F32) + got[j].astype(F32)).astype(BF16)


def split_pairs(cur, mine):
    pairs = cur.reshape(cur.shape[0] // 2, 2, *cur.shape[1:])
    return (
        lax.dynamic_index_in_dim(pairs, 1 - mine, 1, keepdims=False),
        lax.dynamic_index_in_dim(pairs, mine, 1, keepdims=False),
    )


def add_halves_kernel(_, mine, got, out):
    out[...] = (mine[...].astype(F32) + got[...].astype(F32)).astype(BF16)


def named(body, *first):
    kernel = functools.partial(body, *first)
    kernel.__name__ = body.__name__ + "_" + "_".join(map(str, first))
    return kernel


def finish_feed_kernel(_, keep_zero, got_zero, keep_one, got_one, down, up):
    width = up.shape[2]
    for l, (keep, got) in enumerate(((keep_zero, got_zero), (keep_one, got_one))):
        v = keep[0].astype(F32) + got[0].astype(F32)
        down[l], up[l] = v[:, :width], v[:, width:]


def finish_attn_kernel(_, keep_zero, got_zero, keep_one, got_one, in_ref, out_ref):
    cols = in_ref.shape[3]
    rest = cols - 128
    for l, (keep, got) in enumerate(((keep_zero, got_zero), (keep_one, got_one))):
        v = keep[0].astype(F32) + got[0].astype(F32)
        for c in range(4):
            first, last = v[:, c * 128 : c * 128 + 128], v[:, 512 + c * rest : 512 + c * rest + rest]
            if c < 3:
                in_ref[l, c, :, :128] = first
                in_ref[l, c, :, 128:] = last
            else:
                out_ref[l] = jnp.transpose(jnp.concatenate([first, last], axis=1))


def blend(slow, weight):
    return DECAY * slow + (1.0 - DECAY) * weight.astype(F32)


def own_lanes(at, rows, width):
    place = lax.broadcasted_iota(jnp.int32, (rows, width), 0) + at[2] * rows
    return (lax.broadcasted_iota(jnp.int32, (rows, width), 1) == place).astype(BF16)


def average_up_kernel(at, in_w, up_w, slow_in, slow_up, fresh_in, fresh_up):
    rows, width = slow_up.shape[1:]
    pick = own_lanes(at, rows, width)
    for l in range(LAYERS):
        for c in range(3):
            fresh_in[l, c] = blend(slow_in[l, c], dot_t(pick, in_w[l, c]))
        fresh_up[l] = blend(slow_up[l], up_w[l, pl.ds(pl.multiple_of(at[2] * rows, 16), rows), :])


def average_down_kernel(at, out_w, down_w, slow_out, slow_down, fresh_out, fresh_down):
    rows, width = slow_down.shape[1:]
    pick = own_lanes(at, rows, down_w.shape[2])
    for l in range(LAYERS):
        fresh_out[l] = blend(slow_out[l], dot_t(out_w[l], pick))
        fresh_down[l] = blend(slow_down[l], dot_t(pick, down_w[l]))


def average_small_kernel(_, *refs):
    n = len(refs) // 3
    for slow, weight, fresh in zip(refs[:n], refs[n : 2 * n], refs[2 * n :]):
        fresh[...] = blend(slow[...], weight[...])


def per_device(
    patches,
    segment_ids,
    mask_flags,
    upstream,
    mask_embed,
    norm_gain,
    norm_shift,
    in_weight,
    in_bias,
    out_weight,
    out_bias,
    up_weight,
    up_bias,
    down_weight,
    slow_mask_embed,
    slow_norm_gain,
    slow_norm_shift,
    slow_in_weight,
    slow_in_bias,
    slow_out_weight,
    slow_out_bias,
    slow_up_weight,
    slow_up_bias,
    slow_down_weight,
):
    rows_here, length, width = patches.shape
    count = rows_here * length
    cols = in_weight.shape[3]
    ff = down_weight.shape[1]
    size = lax.axis_size("rows")
    piece = width // size
    aligned = piece % 16 == 0
    half = count // 2
    tokens = patches.reshape(count, width)
    top = upstream.reshape(count, width)
    weight_in = in_weight.transpose(0, 2, 3, 1)
    part = 3 * 128 * -(-cols // 128)
    heads = cols // HD
    unit = 2 * count * width * width
    act, act32 = shape((count, width)), shape((count, width), F32)
    hid, wide, held = shape((count, ff)), shape((count, part)), shape((count, heads * 128))
    split = [shape((half, width))] * 2
    eight = shape((8, width), F32)
    both = [pltpu.VMEM((2, half, width), BF16)]
    last = []

    def call(body, outs, args, **kwargs):
        result = run(body, outs, args, after=tuple(last), **kwargs)
        last[:] = [min(result, key=lambda r: r.size)]
        return result

    def add(keep, got):
        return call(add_halves_kernel, [shape(keep.shape)], (keep, got))[0]

    def terms(kernel, args):
        n = width if kernel is attn_grads_kernel else 2 * ff
        if aligned:
            return call(
                kernel, [shape((size // 2, piece, n))] * 2, args,
                scratch=[pltpu.VMEM((2, size // 2, piece, width), BF16)], flops=2 * unit,
            )
        if kernel is attn_grads_kernel:
            normed_in, dproj_in, attn_in, mixed_in = args
            g = t_dot(normed_in, dproj_in)
            pieces = [g[:, c * part // 3 : c * part // 3 + cols] for c in range(3)] + [t_dot(attn_in, mixed_in)]
            sums = [p[:, :128] for p in pieces] + [p[:, 128:] for p in pieces]
        else:
            sums = [t_dot(args[0], args[1]), t_dot(args[2], args[3])]
        sums = jnp.concatenate(sums, axis=1).astype(BF16).reshape(size, piece, n)
        return split_pairs(sums, lax.axis_index("rows") % 2)

    def step(keep, got, bit):
        m, rows, n = keep.shape
        if aligned:
            return call(named(halve, bit), [shape((m // 2, rows, n))] * 2, (keep, got))
        cur = (keep.astype(F32) + got.astype(F32)).astype(BF16)
        return split_pairs(cur, (lax.axis_index("rows") // bit) % 2)

    class Scatter:
        def __init__(self, send, keep):
            self.bit, self.keep, self.got = 1, keep, swap(send, "rows", 1)

        def advance(self):
            self.bit *= 2
            send, self.keep = step(self.keep, self.got, self.bit)
            self.got = swap(send, "rows", self.bit)

        def finish(self):
            while 2 * self.bit < size:
                self.advance()
            return self.keep, self.got

    def attend(l):
        mixed[l], q_held[l] = call(
            attend_kernel, [shape((count, cols)), held], (qkv[l], pack), flops=heads * count * count * 1024
        )
        far = swap(mixed[l], "tp", 2)
        return mixed[l], far, swap(mixed[l], "tp", 1), swap(far, "tp", 1)

    def front(l, own, other, above):
        return call(
            named(attn_front, l), [act32, act, held, eight], (after[l], own, other, above, pack, out_weight, mixed[l]),
            flops=unit // 3,
        )

    def back(l):
        return call(
            named(attend_back, l), [wide] + split + [shape((8, part), F32)],
            (qkv[l], pack, q_held[l], g_held, weight_in), scratch=[pltpu.VMEM((128, count), F32)] + both, flops=4 * unit,
        )

    normed, qkv, mixed, q_held, after, normed_two, active = {}, {}, {}, {}, {}, {}, {}
    far = swap(out_weight, "tp", 2)
    weight_blocks = (out_weight, far, swap(out_weight, "tp", 1), swap(far, "tp", 1))

    pack = call(
        pack_kernel, [shape((PACKED, width), F32)],
        (norm_gain, norm_shift, out_bias, up_bias, mask_embed, segment_ids, mask_flags, in_bias),
    )[0]
    normed[0], qkv[0] = call(first_project_kernel, [act, wide], (tokens, pack, weight_in), flops=unit)
    blocks = attend(0)
    out_full = call(order_kernel, [shape((LAYERS, 4 * cols, width))], weight_blocks)[0]
    small = (slow_mask_embed, slow_norm_gain, slow_norm_shift, slow_in_bias, slow_out_bias, slow_up_bias)
    fresh_small = call(
        average_small_kernel, [shape(v.shape, F32) for v in small],
        small + (mask_embed, norm_gain, norm_shift, in_bias, out_bias, up_bias),
    )
    after[0], normed_two[0], active[0], slope, send, keep = call(
        first_feed_kernel, [act32, act, hid, hid] + split,
        (tokens, *blocks, out_full, pack, up_weight, down_weight), scratch=both, flops=4 * unit,
    )
    s = add(keep, swap(send, "tp", 1))
    got = swap(s, "tp", 2)
    if aligned:
        slow_down = slow_down_weight.transpose(0, 2, 1)
        slow_in = slow_in_weight.transpose(0, 2, 1, 3)
        fresh_out_weight, fresh_down = call(
            average_down_kernel, [shape(slow_out_weight.shape, F32), shape(slow_down.shape, F32)],
            (out_weight, down_weight, slow_out_weight, slow_down),
        )
        fresh_in, fresh_up_weight = call(
            average_up_kernel, [shape(slow_in.shape, F32), shape(slow_up_weight.shape, F32)],
            (weight_in, up_weight, slow_in, slow_up_weight),
        )
        fresh_in_weight, fresh_down_weight = fresh_in.transpose(0, 2, 1, 3), fresh_down.transpose(0, 2, 1)
    else:
        start = lax.axis_index("rows") * piece
        fresh_in_weight, fresh_out_weight, fresh_up_weight, fresh_down_weight = (
            blend(slow, lax.dynamic_slice_in_dim(weight, start, piece, dim))
            for slow, weight, dim in (
                (slow_in_weight, in_weight, 1),
                (slow_out_weight, out_weight, 2),
                (slow_up_weight, up_weight, 1),
                (slow_down_weight, down_weight, 2),
            )
        )
    own = add(s, got)
    x_next, normed[1], qkv[1] = call(
        next_project_kernel, [act32, act, wide], (after[0], own, swap(own, "tp", 1), pack, weight_in), flops=unit
    )
    blocks = attend(1)
    after[1], normed_two[1], active[1], dup, send, keep, feed_one = call(
        last_feed_kernel, [act32, act, hid, hid] + split + [eight],
        (x_next, *blocks, out_full, pack, up_weight, down_weight, top), scratch=both, flops=5 * unit,
    )
    s = add(keep, swap(send, "tp", 1))
    got = swap(s, "tp", 2)
    feed_scatter = {1: Scatter(*terms(feed_grads_kernel, (top, active[1], normed_two[1], dup)))}
    send_out, keep_out = call(down_kernel, split, (active[1], down_weight), scratch=both, flops=unit)
    got_out = swap(send_out, "tp", 1)
    own = add(s, got)
    other = swap(own, "tp", 1)
    s_out = add(keep_out, got_out)
    got_out = swap(s_out, "tp", 2)

    grad_after, attn, g_held, front_one = front(1, own, other, top)
    dproj, send, keep, back_one = back(1)
    s = add(keep, swap(send, "tp", 1))
    got = swap(s, "tp", 2)
    attn_scatter = {1: Scatter(*terms(attn_grads_kernel, (normed[1], dproj, attn, mixed[1])))}
    feed_scatter[1].advance()
    own_out = add(s_out, got_out)
    other_out = swap(own_out, "tp", 1)
    own = add(s, got)

    above, branch, dup, send, keep, feed_zero = call(
        feed_back_kernel, [act32, act, hid] + split + [eight],
        (x_next, own, swap(own, "tp", 1), grad_after, pack, down_weight, slope, up_weight), scratch=both, flops=2 * unit,
    )
    s = add(keep, swap(send, "tp", 1))
    got = swap(s, "tp", 2)
    feed_scatter[0] = Scatter(*terms(feed_grads_kernel, (branch, active[0], normed_two[0], dup)))
    attn_scatter[1].advance()
    feed_scatter[1].advance()
    layer_out = call(output_kernel, [act], (after[1], own_out, other_out, pack))[0].reshape(patches.shape)
    own = add(s, got)
    grad_after, attn, g_held, front_zero = front(0, own, swap(own, "tp", 1), above)
    dproj, send, keep, back_zero = back(0)
    got = swap(send, "tp", 1)
    attn_scatter[0] = Scatter(*terms(attn_grads_kernel, (normed[0], dproj, attn, mixed[0])))
    s = add(keep, got)
    got = swap(s, "tp", 2)
    feed_scatter[0].advance()
    attn_scatter[1].advance()
    sums = call(
        tail_sums_kernel, [shape((SUMMED, width), F32)],
        (tokens, pack, keep, send, grad_after, feed_one, front_one, back_one, feed_zero, front_zero, back_zero),
    )[0]
    vector = [shape(sums.shape, F32)]
    sums = call(add_shared_kernel, vector, (sums, swap(sums, "tp", 1)))[0]
    sums = call(add_shared_kernel, vector, (sums, swap(sums, "tp", 2)))[0]
    got_sums = swap(sums, "rows", 1)
    own = add(s, got)
    other = swap(own, "tp", 1)
    feed_scatter[0].advance()
    attn_scatter[0].advance()
    grad_patches = call(patches_kernel, [act], (tokens, pack, own, other, grad_after))[0].reshape(patches.shape)
    bit = 2
    while bit < size:
        sums = call(add_kernel, vector, (sums, got_sums))[0]
        got_sums = swap(sums, "rows", bit)
        bit *= 2
        if bit == 4:
            attn_scatter[0].advance()
    pair = shape((LAYERS, 2, width), F32)
    grad_mask_embed, grad_norm_gain, grad_norm_shift, grad_in_bias, grad_out_bias, grad_up_bias = call(
        unpack_kernel,
        [shape((width,), F32), pair, pair, shape(in_bias.shape, F32), pair, shape(up_bias.shape, F32)],
        (sums, got_sums),
    )
    grad_down, grad_up_weight = call(
        finish_feed_kernel, [shape((LAYERS, piece, ff), F32)] * 2, feed_scatter[0].finish() + feed_scatter[1].finish()
    )
    grad_in, grad_out_weight = call(
        finish_attn_kernel, [shape((LAYERS, 3, piece, cols), F32), shape((LAYERS, cols, piece), F32)],
        attn_scatter[0].finish() + attn_scatter[1].finish(),
    )
    return (
        layer_out,
        grad_patches,
        grad_mask_embed,
        grad_norm_gain,
        grad_norm_shift,
        grad_in.transpose(0, 2, 1, 3),
        grad_in_bias,
        grad_out_weight,
        grad_out_bias,
        grad_up_weight,
        grad_up_bias,
        grad_down.transpose(0, 2, 1),
        fresh_small[0],
        fresh_small[1],
        fresh_small[2],
        fresh_in_weight,
        fresh_small[3],
        fresh_out_weight,
        fresh_small[4],
        fresh_up_weight,
        fresh_small[5],
        fresh_down_weight,
    )


def solution(mesh):
    placed = (
        P("rows", None, None),
        P("rows", None),
        P("rows", None),
        P("rows", None, None),
        P(),
        P(),
        P(),
        P(None, None, None, "tp"),
        P(None, None, "tp"),
        P(None, "tp", None),
        P(),
        P(None, None, "tp"),
        P(None, "tp"),
        P(None, "tp", None),
        P(),
        P(),
        P(),
        P(None, "rows", None, "tp"),
        P(None, None, "tp"),
        P(None, "tp", "rows"),
        P(),
        P(None, "rows", "tp"),
        P(None, "tp"),
        P(None, "tp", "rows"),
    )
    return jax.shard_map(
        per_device,
        mesh=mesh,
        in_specs=placed,
        out_specs=(
            P("rows", None, None),
            P("rows", None, None),
            P(),
            P(),
            P(),
            P(None, "rows", None, "tp"),
            P(None, None, "tp"),
            P(None, "tp", "rows"),
            P(),
            P(None, "rows", "tp"),
            P(None, "tp"),
            P(None, "tp", "rows"),
            P(),
            P(),
            P(),
            P(None, "rows", None, "tp"),
            P(None, None, "tp"),
            P(None, "tp", "rows"),
            P(),
            P(None, "rows", "tp"),
            P(None, "tp"),
            P(None, "tp", "rows"),
        ),
        check_vma=False,
    )
```

```python
import functools

import jax
import jax.numpy as jnp
from jax import lax
from jax.experimental import pallas as pl
from jax.experimental.pallas import tpu as pltpu
from jax.sharding import PartitionSpec as P

HD = 64
LAYERS = 2
EPSILON = 1e-06
DECAY = 0.8
NEGATIVE = -1e30
F32 = jnp.float32
BF16 = jnp.bfloat16


def swap(x, axis, bit):
    n = lax.axis_size(axis)
    return lax.ppermute(x, axis, [(i, i ^ bit) for i in range(n)])


def shape(dims, dtype=BF16):
    return jax.ShapeDtypeStruct(tuple(dims), dtype)


def run(body, outs, args, after=(), scratch=(), vmem=16, far=0):
    n_in, n_after = len(args), len(after)

    def kernel(*refs):
        me = lax.axis_index("tp")
        body((me % 2, me, lax.axis_index("rows")), *refs[:n_in], *refs[n_in + n_after :])

    near = pl.BlockSpec(memory_space=pltpu.VMEM)
    anywhere = pl.BlockSpec(memory_space=pl.ANY)
    return pl.pallas_call(
        kernel,
        in_specs=[near] * (n_in - far) + [anywhere] * (far + n_after),
        out_specs=[near] * len(outs),
        out_shape=outs,
        scratch_shapes=scratch,
        name=body.__name__,
        compiler_params=pltpu.CompilerParams(vmem_limit_bytes=vmem * 1024 * 1024),
        cost_estimate=pl.CostEstimate(flops=1, bytes_accessed=1, transcendentals=0),
    )(*args, *after)


def named(body, *first):
    kernel = functools.partial(body, *first)
    kernel.__name__ = body.__name__ + "_" + "_".join(map(str, first))
    return kernel


def dot(a, b):
    return jnp.dot(a, b, preferred_element_type=F32)


def dot_t(a, b):
    return lax.dot_general(a, b, (((1,), (1,)), ((), ())), preferred_element_type=F32)


def t_dot(a, b):
    return lax.dot_general(a, b, (((0,), (0,)), ((), ())), preferred_element_type=F32)


GAIN, SHIFT, OUT_BIAS, UP_BIAS, EMBED, SEG, FLAG, IN_BIAS, PACKED = 0, 4, 8, 12, 14, 15, 16, 17, 24
V_EMBED, V_GAIN, V_SHIFT, V_OUT, OWN, V_UP, V_IN, SUMMED = 0, 1, 5, 9, 13, 13, 15, 24


def norm_parts(values):
    center = values - jnp.mean(values, axis=-1, keepdims=True)
    spread = jnp.mean(center * center, axis=-1, keepdims=True)
    inv = lax.rsqrt(spread + EPSILON)
    return center * inv, inv


def norm_back(values, gain, cot):
    hat, inv = norm_parts(values)
    w = cot * gain
    mean_w = jnp.mean(w, axis=-1, keepdims=True)
    mean_wh = jnp.mean(w * hat, axis=-1, keepdims=True)
    return inv * (w - mean_w - hat * mean_wh), cot * hat


def column(row, lanes=128):
    return jnp.transpose(jnp.broadcast_to(row, (lanes, row.shape[1])))


def split_three(v):
    one = v.astype(BF16).astype(F32)
    two = (v - one).astype(BF16).astype(F32)
    return one, two, v - one - two


def chunk(i, half):
    return slice(i * half, i * half + half)


def row_of(pack, i):
    return pack[i : i + 1, :]


def add_rows(ref, first, rows):
    if first:
        ref[...] = jnp.zeros_like(ref)
    for n, r in enumerate(rows):
        ref[n : n + 1, :] += jnp.sum(r, axis=0, keepdims=True)


def share_out(at, value, held, sends, keep):
    half = value.shape[0] // 2
    for c in range(2):
        held[c] = value[c * half : c * half + half].astype(BF16)
    keep[...] = held[at[0]]
    if len(sends) == 1:
        sends[0][...] = held[1 - at[0]]
        return
    first = 0
    for s in sends:
        n = s.shape[0]
        s[...] = held[1 - at[0], first : first + n]
        first += n


def joined(at, own, others):
    own = own[...].astype(F32)
    other = jnp.concatenate([o[...].astype(F32) for o in others], axis=0)
    low = at[0] == 0
    return jnp.concatenate([jnp.where(low, own, other), jnp.where(low, other, own)], axis=0)


def entry_of(patches, pack, rows):
    on = column(pack[FLAG : FLAG + 1, rows])[:, :1] > 0.0
    return jnp.where(on, row_of(pack, EMBED), patches.astype(F32)), on


def project(x, l, pack, weight, normed_ref, qkv_ref):
    hat, _ = norm_parts(x)
    normed = (hat * row_of(pack, GAIN + 2 * l) + row_of(pack, SHIFT + 2 * l)).astype(BF16)
    normed_ref[...] = normed
    bias = row_of(pack, IN_BIAS + l)
    part, cols = qkv_ref.shape[1] // 3, weight.shape[1]
    for c in range(3):
        first = c * part
        out = (dot_t(normed, weight[c]) + bias[:, first : first + cols]).astype(BF16)
        if c == 0:
            out = out * jnp.asarray(HD**-0.5, BF16)
        qkv_ref[:, first : first + cols] = out
        qkv_ref[:, first + cols : first + part] = jnp.zeros((out.shape[0], part - cols), BF16)


def take_kernel(_, weights, out, sem):
    copy = pltpu.make_async_copy(weights.at[0], out, sem.at[0])
    copy.start()
    copy.wait()


def first_project_kernel(_, *refs):
    far, outs, held, sem = refs[:10], refs[10:15], refs[15:25], refs[25]
    pack, normed, qkv = outs[0], outs[1:3], outs[3:5]
    gain, shift, out_bias, up_bias, embed, seg, flags, in_bias, tokens, weight = far
    sources = [gain, shift, out_bias, up_bias, embed, seg, flags, in_bias, tokens, weight.at[0]]
    copies = [pltpu.make_async_copy(src, dst, sem.at[i]) for i, (src, dst) in enumerate(zip(sources, held))]
    for c in copies:
        c.start()
    for c in copies[:8]:
        c.wait()
    gain, shift, out_bias, up_bias, embed, seg, flags, in_bias, tokens, weight = held[:10]
    pack[...] = jnp.zeros_like(pack)
    for l in range(LAYERS):
        for base, ref in ((GAIN, gain), (SHIFT, shift), (OUT_BIAS, out_bias)):
            pack[base + 2 * l : base + 2 * l + 2, :] = ref[l]
        cols = in_bias.shape[2]
        last = pack.shape[1] // 3 * 2
        pack[IN_BIAS + l : IN_BIAS + l + 1, :cols] = in_bias[l, 0:1]
        pack[IN_BIAS + l : IN_BIAS + l + 1, last : last + cols] = in_bias[l, 1:2]
    pack[UP_BIAS : UP_BIAS + LAYERS, :] = up_bias[...]
    pack[EMBED : EMBED + 1, :] = embed[...].reshape(1, pack.shape[1])
    pack[SEG : SEG + 1, :] = seg[...].astype(F32)
    pack[FLAG : FLAG + 1, :] = flags[...].astype(F32)
    for c in copies[8:10]:
        c.wait()
    for i in range(2):
        rows = chunk(i, normed[i].shape[0])
        x, _on = entry_of(tokens[rows, :], pack, rows)
        project(x, 0, pack, weight, normed[i], qkv[i])


def next_project_kernel(at, after, own, low, high, pack, weight, x_ref, normed, qkv):
    x = after[...] + joined(at, own, (low, high)) + row_of(pack, OUT_BIAS + 1)
    x_ref[...] = x
    project(x, 1, pack, weight.at[1], normed, qkv)


def head_lanes(rows, h):
    lane = lax.broadcasted_iota(jnp.int32, (rows, 128), 1)
    upper = lane >= 64
    mine = upper if h % 2 else jnp.logical_not(upper)
    return mine, lane % 64


def two(refs, cols):
    return jnp.concatenate([r[:, cols] for r in refs], axis=0)


def attend(l, i, _, qkv_a, qkv_b, pack, mixed_ref, packed_ref, held_ref):
    qkv = (qkv_a, qkv_b)
    half, part = qkv_a.shape[0], qkv_a.shape[1] // 3
    heads, width = held_ref.shape[1] // 128, mixed_ref.shape[1]
    seg = column(row_of(pack, SEG)).astype(jnp.int32)
    for h in range(heads):
        lanes = h // 2 * 128
        mine, place = head_lanes(2 * half, h)
        apart = jnp.where((place < 4) & (place != seg), NEGATIVE, 0.0)
        keys = two(qkv, slice(part + lanes, part + lanes + 128))
        keys = jnp.where(mine, keys.astype(F32), apart).astype(BF16)
        values = two(qkv, slice(2 * part + lanes, 2 * part + lanes + 128))
        size = min(128, width - lanes)
        mine, place = mine[:half], place[:half]
        marks = (place == seg[chunk(i, half)]).astype(F32)
        q = qkv[i][:, lanes : lanes + 128].astype(F32)
        scores = dot_t(jnp.where(mine, q, marks).astype(BF16), keys)
        top = jnp.max(scores, axis=-1, keepdims=True)
        expo = jnp.exp(scores - top)
        total = jnp.sum(expo, axis=-1, keepdims=True)
        out = dot(expo.astype(BF16), values) / total
        one, twice, three = split_three(-(top + jnp.log(total)))
        marks = marks + jnp.where(
            place == 4, one, jnp.where(place == 5, twice, jnp.where(place == 6, three, 0.0))
        )
        held_ref[:, h * 128 : h * 128 + 128] = jnp.where(mine, q, marks).astype(BF16)
        if h % 2:
            out = jnp.where(mine, out, mixed_ref[:, lanes : lanes + 128].astype(F32))
        out = out[:, :size].astype(BF16)
        mixed_ref[:, lanes : lanes + size] = out
        if size == 128:
            packed_ref[:half, :] = out
        else:
            packed_ref[half:, :size] = out[: half // 2]
            packed_ref[half:, size:] = out[half // 2 :]


def gelu_both(u):
    phi = 0.5 * (1.0 + lax.erf(u * (0.5**0.5)))
    return u * phi, phi + u * jnp.exp(-0.5 * u * u) * 0.3989422804014327


def in_order(me, own, far, near, last):
    core, chip = me % 2 == 1, me // 2 == 1

    def pick(on, one, other):
        return jnp.where(on, other, one), jnp.where(on, one, other)

    own, far = pick(chip, own, far)
    near, last = pick(chip, near, last)
    own, near = pick(core, own, near)
    far, last = pick(core, far, last)
    return own, near, far, last


def copy_kernel(_, x, *outs):
    n = outs[0].shape[0]
    for i, o in enumerate(outs):
        o[...] = x[i * n : i * n + n]


def order_weights(at, own, far, near, last, out):
    rest = out.shape[0] - 512
    blocks = own[...], far[...], near[...], jnp.concatenate([p[...] for p in last], axis=0)
    for g, w in enumerate(in_order(at[1], *blocks)):
        out[g * 128 : g * 128 + 128, :] = w[:128]
        out[512 + g * rest // 4 : 512 + (g + 1) * rest // 4, :] = w[128:]


def order_kernel(at, own, far, near, one, twice, three, four, out):
    order_weights(at, own, far, near, (one, twice, three, four), out)


def take_last_kernel(_, weights, out):
    out[...] = weights[LAYERS - 1]


def mixed_rows(at, mixed):
    half = mixed[0].shape[0] * 2 // 3
    mixed = [m[...] for m in mixed[:3]] + [jnp.concatenate([m[...] for m in mixed[3:]], axis=0)]
    blocks = in_order(at[1], *[m[:half, :] for m in mixed])
    rest = in_order(at[1], *[m[half:, :] for m in mixed])
    rest = [jnp.concatenate([r[:, :64], r[:, 64:]], axis=0) for r in rest]
    pairs = [jnp.concatenate(rest[g : g + 2], axis=1) for g in (0, 2)]
    return jnp.concatenate([*blocks, *pairs], axis=1)


def feed_front(at, l, x, mixed, weights, pack, up, after_ref, normed_ref):
    after = x + row_of(pack, OUT_BIAS + 2 * l) + dot(mixed_rows(at, mixed), weights[...])
    after_ref[...] = after
    hat, _ = norm_parts(after)
    normed = (hat * row_of(pack, GAIN + 2 * l + 1) + row_of(pack, SHIFT + 2 * l + 1)).astype(BF16)
    normed_ref[...] = normed
    return gelu_both(dot(normed, up[l]) + row_of(pack, UP_BIAS + l))


def first_feed(i, at, patches, weights, pack, up, down, *refs):
    *mixed, after, normed, active_ref, slope_ref, keep, low, high, held = refs
    rows = chunk(i, after.shape[0])
    x, _ = entry_of(patches[rows, :], pack, rows)
    active, slope = feed_front(at, 0, x, mixed, weights, pack, up, after, normed)
    active = active.astype(BF16)
    active_ref[...] = active
    slope_ref[...] = slope.astype(BF16)
    share_out(at, dot(active, down[0]), held, (low, high), keep)


def last_feed(i, at, x, weights, pack, up, down, top, *refs):
    *mixed, after, normed, active_ref, dup_ref, sums_ref, keep, low, high, held = refs
    active, slope = feed_front(at, 1, x[...], mixed, weights, pack, up, after, normed)
    active_ref[...] = active.astype(BF16)
    branch = top[chunk(i, after.shape[0]), :]
    dup = (dot_t(branch, down[1]) * slope).astype(BF16)
    dup_ref[...] = dup
    add_rows(sums_ref, True, [dup.astype(F32), branch.astype(F32)])
    share_out(at, dot_t(dup, up[1]), held, (low, high), keep)


def down_kernel(at, active_a, active_b, down, keep, send, held):
    for i, active in enumerate((active_a, active_b)):
        share_out(at, dot(active[...], down[1]), held, (send.at[i],), keep.at[i])


def output_kernel(at, after_a, after_b, pack, own, other, out_ref):
    half = after_a.shape[0]
    for i, after in enumerate((after_a, after_b)):
        y = after[...] + joined(at, own.at[i], (other.at[i],)) + row_of(pack, OUT_BIAS + 3)
        out_ref[chunk(i, half), :] = y.astype(BF16)


def attn_front(l, i, at, after, above, pack, out_w, mixed, own, *refs):
    *others, grad_ref, attn_ref, held_ref, sums_ref = refs
    width = mixed.shape[1]
    half = after.shape[0]
    cot = joined(at, own, others)
    pulled, prod = norm_back(after[...], row_of(pack, GAIN + 2 * l + 1), cot)
    above = above[chunk(i, half), :] if above.shape[0] > half else above[...]
    grad = pulled + above.astype(F32)
    grad_ref[...] = grad
    attn = grad.astype(BF16)
    attn_ref[...] = attn
    add_rows(sums_ref, True, [prod, cot, grad])
    mixed_grad = dot_t(attn, out_w[l]).astype(BF16).astype(F32)
    for h in range(width // HD):
        lanes = h // 2 * 128
        mine, place = head_lanes(half, h)
        size = min(128, width - lanes)
        mix = mixed[:, lanes : lanes + size].astype(F32)
        grads = mixed_grad[:, lanes : lanes + size]
        if size < 128:
            fill = jnp.zeros((half, 128 - size), F32)
            mix, grads = (jnp.concatenate([v, fill], axis=1) for v in (mix, grads))
        inner = jnp.sum(jnp.where(mine, mix * grads, 0.0), axis=-1, keepdims=True)
        one, twice, three = split_three(-inner)
        marks = jnp.where(place == 4, one, jnp.where(place == 5, twice, jnp.where(place == 6, three, 0.0)))
        held_ref[:, h * 128 : h * 128 + 128] = jnp.where(mine, grads, marks).astype(BF16)


def attend_back(l, at, qkv_a, qkv_b, pack, q_a, q_b, g_a, g_b, weight, dproj_ref, sums_ref, *refs):
    *refs, turned, held = refs
    if l:
        keeps, sends = refs[:2], (refs[2:4], refs[4:])
    else:
        keeps, sends = [refs[0].at[i] for i in range(2)], [(r,) for r in refs[1:]]
    qkv, q_held, g_held = (qkv_a, qkv_b), (q_a, q_b), (g_a, g_b)
    half, width = qkv_a.shape
    length = 2 * half
    part = width // 3
    heads = q_a.shape[1] // 128
    seg = column(row_of(pack, SEG)).astype(jnp.int32)
    for h in range(heads):
        lanes = h // 2 * 128
        mine, place = head_lanes(half, h)
        ones = ((place >= 4) & (place < 7)).astype(F32)
        qh = two(q_held, slice(h * 128, h * 128 + 128))
        gh = two(g_held, slice(h * 128, h * 128 + 128))
        for i in range(2):
            rows = chunk(i, half)
            apart = jnp.where((place < 4) & (place != seg[rows]), NEGATIVE, ones)
            bare = qkv[i][:, part + lanes : part + lanes + 128]
            keys = jnp.where(mine, bare.astype(F32), apart).astype(BF16)
            values = qkv[i][:, 2 * part + lanes : 2 * part + lanes + 128].astype(F32)
            values = jnp.where(mine, values, ones).astype(BF16)
            probs = jnp.exp(dot_t(keys, qh))
            ds = (probs * dot_t(values, gh)).astype(BF16)
            gv = dot(probs.astype(BF16), gh).astype(BF16)
            gk = dot(ds, qh).astype(BF16)
            for base, g in ((part, gk), (2 * part, gv)):
                cols = slice(base + lanes, base + lanes + 128)
                if h % 2:
                    g = jnp.where(mine, g.astype(F32), dproj_ref[rows, cols].astype(F32)).astype(BF16)
                elif h == heads - 1:
                    g = jnp.where(mine, g.astype(F32), 0.0).astype(BF16)
                dproj_ref[rows, cols] = g
            dq = t_dot(bare, ds)
            if i == 0:
                turned[...] = dq
            else:
                turned[...] += dq
        dq = jnp.transpose(turned[...]) * HD**-0.5
        cols = slice(lanes, lanes + 128)
        mine, _ = head_lanes(length, h)
        if h % 2:
            dq = jnp.where(mine, dq, dproj_ref[:, cols].astype(F32))
        elif h == heads - 1:
            dq = jnp.where(mine, dq, 0.0)
        dproj_ref[:, cols] = dq.astype(BF16)
    cols = weight.shape[2]
    for i in range(2):
        dproj = dproj_ref[chunk(i, half), :]
        add_rows(sums_ref, i == 0, [dproj.astype(F32)])
        share = sum(dot(dproj[:, c * part : c * part + cols], weight[l, c]) for c in range(3))
        share_out(at, share, held, sends[i], keeps[i])


def feed_back(
    i, at, x, own, low, high, above, pack, down, slope, up, grad_ref, branch_ref, dup_ref, sums_ref, keep, *sends
):
    *sends, held = sends
    cot = joined(at, own, (low, high))
    pulled, prod = norm_back(x[...], row_of(pack, GAIN + 2), cot)
    grad = pulled + above[...]
    grad_ref[...] = grad
    branch = grad.astype(BF16)
    branch_ref[...] = branch
    dup = (dot_t(branch, down[0]) * slope[...].astype(F32)).astype(BF16)
    dup_ref[...] = dup
    add_rows(sums_ref, True, [prod, cot, grad, dup.astype(F32)])
    share_out(at, dot_t(dup, up[0]), held, sends, keep)


def tail_sums_kernel(
    at, patches, pack, above_a, above_b, feed_one_a, feed_one_b, feed_zero_a, feed_zero_b,
    front_one_a, front_one_b, front_zero_a, front_zero_b, back_one, back_zero, keep, send_a, send_b, out,
):
    out[...] = jnp.zeros_like(out)
    half = above_a.shape[0]
    for i, above in enumerate((above_a, above_b)):
        rows = chunk(i, half)
        cot = joined(at, keep.at[i], ((send_a, send_b)[i],))
        x, on = entry_of(patches[rows, :], pack, rows)
        pulled, prod = norm_back(x, row_of(pack, GAIN), cot)
        embed = jnp.where(on, pulled + 0.25 * above[...], 0.0)
        for base, v in ((V_EMBED, embed), (V_GAIN, prod), (V_SHIFT, cot)):
            out[base : base + 1, :] += jnp.sum(v, axis=0, keepdims=True)
    feed_one = feed_one_a[...] + feed_one_b[...]
    feed_zero = feed_zero_a[...] + feed_zero_b[...]
    front_zero = front_zero_a[...] + front_zero_b[...]
    front_one = front_one_a[...] + front_one_b[...]
    for base, v, n in (
        (V_GAIN + 1, front_zero, 0),
        (V_GAIN + 2, feed_zero, 0),
        (V_GAIN + 3, front_one, 0),
        (V_SHIFT + 1, front_zero, 1),
        (V_SHIFT + 2, feed_zero, 1),
        (V_SHIFT + 3, front_one, 1),
        (V_OUT, front_zero, 2),
        (V_OUT + 1, feed_zero, 2),
        (V_OUT + 2, front_one, 2),
        (V_OUT + 3, feed_one, 1),
    ):
        out[base : base + 1, :] = 0.25 * v[n : n + 1, :]
    out[V_UP : V_UP + 1, :] = feed_zero[3:4, :]
    out[V_UP + 1 : V_UP + 2, :] = feed_one[0:1, :]
    out[V_IN : V_IN + 1, :] = back_zero[0:1, :]
    out[V_IN + 1 : V_IN + 2, :] = back_one[0:1, :]


def add_shared_kernel(_, mine, got, out):
    row = lax.broadcasted_iota(jnp.int32, mine.shape, 0)
    out[...] = mine[...] + jnp.where(row < OWN, got[...], 0.0)


def add_kernel(_, mine, got, out):
    out[...] = mine[...] + got[...]


def unpack_kernel(_, mine, got, embed, gain, shift, in_bias, out_bias, up_bias):
    v = mine[...] + got[...]
    embed[...] = v[V_EMBED]
    cols = in_bias.shape[2]
    last = v.shape[1] // 3 * 2
    for l in range(LAYERS):
        for base, ref in ((V_GAIN, gain), (V_SHIFT, shift), (V_OUT, out_bias)):
            ref[l] = v[base + 2 * l : base + 2 * l + 2]
        in_bias[l, 0:1, :] = v[V_IN + l : V_IN + l + 1, :cols]
        in_bias[l, 1:2, :] = v[V_IN + l : V_IN + l + 1, last : last + cols]
    up_bias[...] = v[V_UP : V_UP + LAYERS]


def patches_kernel(at, patches, pack, above_a, above_b, own, other_a, other_b, out_ref):
    half = above_a.shape[0]
    for i, (above, other) in enumerate(((above_a, other_a), (above_b, other_b))):
        rows = chunk(i, half)
        x, on = entry_of(patches[rows, :], pack, rows)
        pulled, _ = norm_back(x, row_of(pack, GAIN), joined(at, own.at[i], (other,)))
        out_ref[rows, :] = jnp.where(on, 0.0, pulled + above[...]).astype(BF16)


def split_rows(value, held, bit):
    size = 2 * held.shape[1]
    rows = value.shape[0] // size
    for n in range(size):
        held[n // bit % 2, n // (2 * bit) * bit + n % bit] = value[n * rows : n * rows + rows].astype(BF16)


def spread(refs, n):
    if len(refs) == n:
        return [r[...] for r in refs]
    half = refs[0].shape[0] // n
    return [refs[0][chunk(i, half), :] for i in range(n)]


def cut_terms(at, bit, value, refs):
    *pieces, held = refs
    split_rows(value, held, bit)
    mine = at[2] // bit
    n = pieces[0].shape[2]
    for i, ref in enumerate(pieces):
        cols = slice(i // 2 * n, i // 2 * n + n)
        ref[...] = held[(mine + 1 + i) % 2, :, :, cols]


def feed_grads(parts, bit, at, *refs):
    cuts = refs[-2 * parts - 1 :]
    *args, right_a, right_b = refs[: -2 * parts - 1]
    left = spread(args, 2)
    cut_terms(at, bit, t_dot(left[0], right_a[...]) + t_dot(left[1], right_b[...]), cuts)


def attn_grads(parts, bit, at, normed_a, normed_b, dproj, attn_a, attn_b, mixed_a, mixed_b, *refs):
    cols = mixed_a.shape[1]
    half, part = normed_a.shape[0], dproj.shape[1] // 3
    g = t_dot(normed_a[...], dproj[:half, :]) + t_dot(normed_b[...], dproj[half:, :])
    o = t_dot(attn_a[...], mixed_a[...]) + t_dot(attn_b[...], mixed_b[...])
    pieces = [g[:, c * part : c * part + cols] for c in range(3)] + [o]
    whole_lanes = [p[:, :128] for p in pieces]
    rest = [
        jnp.concatenate([pieces[i][:, 128:], pieces[i + 1][:, 128:]], axis=1) for i in range(0, 4, 2)
    ]
    cut_terms(at, bit, jnp.concatenate(whole_lanes + rest, axis=1), refs)


def halve(bit, under, n_out, at, *refs):
    pairs, outs = refs[: len(refs) - 2 * n_out], refs[len(refs) - 2 * n_out :]
    mine = (at[2] // bit) % 2
    n = outs[0].shape[2]
    first = 0
    for held, got in zip(pairs[::2], pairs[1::2]):
        last = first + held.shape[2]
        for p in range(n_out):
            low, high = max(first, p * n), min(last, p * n + n)
            if low >= high:
                continue
            source, target = slice(low - first, high - first), slice(low - p * n, high - p * n)
            for i in range(outs[0].shape[0]):
                for ref, side in ((outs[2 * p], 1 - mine), (outs[2 * p + 1], mine)):
                    j = i // under * 2 * under + side * under + i % under
                    both = held[j, :, source].astype(F32) + got[j, :, source].astype(F32)
                    ref[i, :, target] = both.astype(BF16)
        first = last


def split_pairs(cur, low, mine):
    pairs = cur.reshape(cur.shape[0] // (2 * low), 2, low, *cur.shape[1:])
    return [
        lax.dynamic_index_in_dim(pairs, side, 1, keepdims=False).reshape(-1, *cur.shape[1:]) for side in (1 - mine, mine)
    ]


def add_bf16(mine, got):
    return (mine[...].astype(F32) + got[...].astype(F32)).astype(BF16)


def add_bf16_kernel(_, mine, *refs):
    *gots, out = refs
    first = 0
    for g in gots:
        rows = slice(first, first + g.shape[0])
        out[rows] = add_bf16(mine.at[rows], g)
        first += g.shape[0]


def add_whole_kernel(_, mine, got, out):
    out[...] = add_bf16(mine, got)


def add_pieces_kernel(_, mine, got, out, *pieces):
    s = add_bf16(mine, got)
    out[...] = s
    n = pieces[0].shape[0]
    for i, p in enumerate(pieces):
        p[...] = s[i * n : i * n + n]


def add_pair_kernel(_, mine, got_a, got_b, out):
    for i, got in enumerate((got_a, got_b)):
        out[i] = add_bf16(mine.at[i], got)


def add_halves_kernel(_, mine, got, out, low, high):
    v = add_bf16(mine, got)
    out[...] = v
    low[...], high[...] = v[0], v[1]


def totals(refs):
    return jnp.concatenate(
        [k[0].astype(F32) + g[0].astype(F32) for k, g in zip(refs[::2], refs[1::2])], axis=1
    )


def finish_feed(n_zero, _, *refs):
    *refs, down, up = refs
    ff = up.shape[2]
    for l, part in enumerate((refs[:n_zero], refs[n_zero:])):
        v = totals(part)
        down[l], up[l] = v[:, :ff], v[:, ff:]


def finish_attn_kernel(_, *refs):
    *refs, in_ref, out_ref = refs
    cols = in_ref.shape[3]
    rest = cols - 128
    both = totals(refs)
    width = both.shape[1] // LAYERS
    for n in range(LAYERS):
        l = LAYERS - 1 - n
        v = both[:, n * width : n * width + width]
        for c in range(4):
            first, last = v[:, c * 128 : c * 128 + 128], v[:, 512 + c * rest : 512 + c * rest + rest]
            if c < 3:
                in_ref[l, c, :, :128] = first
                in_ref[l, c, :, 128:] = last
            else:
                out_ref[l] = jnp.transpose(jnp.concatenate([first, last], axis=1))


def blend(slow, weight):
    return DECAY * slow + (1.0 - DECAY) * weight.astype(F32)


def own_lanes(at, rows, width):
    place = lax.broadcasted_iota(jnp.int32, (rows, width), 0) + at[2] * rows
    return (lax.broadcasted_iota(jnp.int32, (rows, width), 1) == place).astype(BF16)


def average_up_kernel(at, in_w, up_w, slow_in, slow_up, fresh_in, fresh_up):
    rows, width = slow_up.shape[1:]
    pick = own_lanes(at, rows, width)
    for l in range(LAYERS):
        for c in range(3):
            fresh_in[l, c] = blend(slow_in[l, c], dot_t(pick, in_w[l, c]))
        fresh_up[l] = blend(slow_up[l], up_w[l, pl.ds(pl.multiple_of(at[2] * rows, 16), rows), :])


def average_down_kernel(at, out_w, down_w, slow_out, slow_down, fresh_out, fresh_down):
    rows, width = slow_down.shape[1:]
    pick = own_lanes(at, rows, down_w.shape[2])
    for l in range(LAYERS):
        fresh_out[l] = blend(slow_out[l], dot_t(out_w[l], pick))
        fresh_down[l] = blend(slow_down[l], dot_t(pick, down_w[l]))


def average_small_kernel(_, *refs):
    n = len(refs) // 3
    for slow, weight, fresh in zip(refs[:n], refs[n : 2 * n], refs[2 * n :]):
        fresh[...] = blend(slow[...], weight[...])


def per_device(
    patches,
    segment_ids,
    mask_flags,
    upstream,
    mask_embed,
    norm_gain,
    norm_shift,
    in_weight,
    in_bias,
    out_weight,
    out_bias,
    up_weight,
    up_bias,
    down_weight,
    slow_mask_embed,
    slow_norm_gain,
    slow_norm_shift,
    slow_in_weight,
    slow_in_bias,
    slow_out_weight,
    slow_out_bias,
    slow_up_weight,
    slow_up_bias,
    slow_down_weight,
):
    rows_here, length, width = patches.shape
    count = rows_here * length
    cols = in_weight.shape[3]
    ff = down_weight.shape[1]
    size = lax.axis_size("rows")
    piece = width // size
    aligned = piece % 16 == 0
    half = count // 2
    quarter = half // 2
    tokens = patches.reshape(count, width)
    top = upstream.reshape(count, width)
    weight_in = in_weight.transpose(0, 2, 3, 1)
    part = 3 * 128 * -(-cols // 128)
    heads = cols // HD
    act, act32, wide = shape((half, width)), shape((half, width), F32), shape((half, part))
    hid, held = shape((half, ff)), shape((half, heads * 128))
    small, pair = shape((quarter, width)), shape((2, quarter, width))
    eight, eighth, bit_of = shape((8, width), F32), shape((quarter // 2, width)), shape((quarter // 4, width))
    two_cores = [pltpu.VMEM((2, quarter, width), BF16)]
    last = []

    def call(body, outs, args, touch=(), free=False, **kwargs):
        if free:
            return run(body, outs, args, **kwargs)
        result = run(body, outs, args, after=tuple(last) + tuple(touch), **kwargs)
        last[:] = [min(result, key=lambda r: r.size)]
        return result

    def add(keep, gots, **kwargs):
        return call(add_bf16_kernel, [shape(keep.shape)], (keep, *gots), **kwargs)[0]

    def add_own(keep, got, parts=2, **kwargs):
        out = [shape((quarter // parts, width))] * parts
        own, *pieces = call(add_pieces_kernel, [small] + out, (keep, got), **kwargs)
        return (own, *(swap(p, "tp", 1) for p in pieces))

    def exchange(keep, sends, **kwargs):
        s = add(keep, [swap(s, "tp", 1) for s in sends], **kwargs)
        return s, swap(s, "tp", 2)

    def terms(kernel, parts, bit, args, **kwargs):
        n = width // parts
        if aligned:
            return call(
                named(kernel, parts, bit), [shape((size // 2, piece, n))] * (2 * parts), args,
                scratch=[pltpu.VMEM((2, size // 2, piece, width), BF16)], **kwargs,
            )
        if kernel is attn_grads:
            normed_a, normed_b, dproj_in, attn_a, attn_b, *mixed_in = args
            g = t_dot(jnp.concatenate([normed_a, normed_b]), dproj_in)
            o = t_dot(jnp.concatenate([attn_a, attn_b]), jnp.concatenate(mixed_in))
            pieces = [g[:, c * part // 3 : c * part // 3 + cols] for c in range(3)] + [o]
            sums = jnp.concatenate([p[:, :128] for p in pieces] + [p[:, 128:] for p in pieces], axis=1)
        else:
            sums = t_dot(jnp.concatenate(args[:-2]), jnp.concatenate(args[-2:]))
        sums = sums.astype(BF16).reshape(size, piece, width)
        mine = lax.axis_index("rows") // bit % 2
        return [x for i in range(parts) for x in split_pairs(sums[:, :, i * n : i * n + n], bit, mine)]

    def step(pieces, bit, low, parts, **kwargs):
        count_in, rows, _ = pieces[0].shape
        n = sum(p.shape[2] for p in pieces[::2]) // parts
        if aligned:
            return call(
                named(halve, bit, low, parts), [shape((count_in // 2, rows, n))] * (2 * parts), pieces, **kwargs
            )
        cur = [(k.astype(F32) + g.astype(F32)).astype(BF16) for k, g in zip(pieces[::2], pieces[1::2])]
        cur, mine = jnp.concatenate(cur, axis=2), lax.axis_index("rows") // bit % 2
        return [x for i in range(parts) for x in split_pairs(cur[:, :, i * n : i * n + n], low, mine)]

    bits = [1 << i for i in range(size.bit_length() - 1)]
    later = bits[1:] + bits[:1]

    class Scatter:
        def __init__(self, order):
            self.order, self.done, self.pieces = order, 0, ()

        def take(self, cuts):
            for send, keep in zip(cuts[::2], cuts[1::2]):
                self.pieces += (keep, swap(send, "rows", self.order[self.done]))

        def add(self, kernel, parts, args, **kwargs):
            self.take(terms(kernel, parts, self.order[0], args, **kwargs))

        def advance(self, parts=1, **kwargs):
            self.done += 1
            bit = self.order[self.done]
            low = 1 << sum(x < bit for x in self.order[self.done :])
            cuts = step(self.pieces, bit, low, parts, **kwargs)
            self.pieces = ()
            self.take(cuts)

        def came(self):
            return self.pieces[1::2]

        def finish(self):
            while self.done + 1 < len(self.order):
                self.advance()
            return self.pieces

    def mix(l):
        parts, blocks = [], []
        for i in range(2):
            m, packed, q = call(
                named(attend, l, i), [shape((half, cols)), shape((half + quarter, 128)), held], (*qkv[l], pack)
            )
            parts.append((m, q))
            blocks.append((packed, swap(packed, "tp", 2), swap(packed, "tp", 1)))
        mixed[l], q_held[l] = zip(*parts)
        return blocks

    def last_blocks(far, i):
        pieces = (far,)
        if i == 0:
            pieces = call(copy_kernel, [shape((far.shape[0] // 2, 128))] * 2, (far,))
        return [swap(p, "tp", 1) for p in pieces]

    def front(l, above, sums, parts, touch=()):
        results = []
        for i, (s, got) in enumerate(sums):
            own = add_own(s, got, parts, touch=() if i else touch)
            results.append(
                call(
                    named(attn_front, l, i), [act32, act, held, eight],
                    (after[l][i], above[i], pack, out_weight, mixed[l][i], *own),
                )
            )
        return zip(*results)

    def back(l, shares, **kwargs):
        dproj, sums, *shares = call(
            named(attend_back, l), [shape((count, part)), shape((8, part), F32)] + shares,
            (*qkv[l], pack, *q_held[l], *g_held, weight_in), scratch=[pltpu.VMEM((128, count), F32)] + two_cores, **kwargs,
        )
        return dproj, sums, shares

    normed, qkv, mixed, q_held, after, normed_two, active = {}, {}, {}, {}, {}, {}, {}

    far_args = (norm_gain, norm_shift, out_bias, up_bias, mask_embed, segment_ids, mask_flags, in_bias, tokens, weight_in)
    *far_args, far_weight = [pltpu.with_memory_space_constraint(a, pltpu.HBM) for a in far_args + (out_weight,)]
    block = (cols, width)
    own = call(
        take_kernel, [shape(block)], (far_weight,), scratch=[pltpu.SemaphoreType.DMA((1,))], far=1
    )[0]
    far, near = swap(own, "tp", 2), swap(own, "tp", 1)
    scratch = [pltpu.VMEM(a.shape, a.dtype) for a in far_args[:9]]
    scratch += [pltpu.VMEM(weight_in.shape[1:], BF16), pltpu.SemaphoreType.DMA((10,))]
    pack, *rest = call(
        first_project_kernel, [shape((PACKED, width), F32), act, act, wide, wide], far_args,
        scratch=scratch, far=len(far_args),
    )
    normed[0], qkv[0] = rest[:2], rest[2:]
    blocks = mix(0)
    pieces = call(copy_kernel, [shape((cols // 4, width))] * 4, (far,))
    out_zero = call(
        order_kernel, [shape((4 * cols, width))], (own, far, near, *(swap(p, "tp", 1) for p in pieces))
    )[0]
    slows = (slow_mask_embed, slow_norm_gain, slow_norm_shift, slow_in_bias, slow_out_bias, slow_up_bias)
    fresh_small = call(
        average_small_kernel, [shape(v.shape, F32) for v in slows],
        slows + (mask_embed, norm_gain, norm_shift, in_bias, out_bias, up_bias),
    )
    parts = []
    for i in range(2):
        packed, far, near = blocks[i]
        parts.append(
            call(
                named(first_feed, i), [act32, act, hid, hid, small, eighth, eighth],
                (tokens, out_zero, pack, up_weight, down_weight, packed, far, near, *last_blocks(far, i)), scratch=two_cores,
            )
        )
    after[0], normed_two[0], active[0], slope, keeps, *sends = zip(*parts)
    sums = [exchange(keeps[i], [s[i] for s in sends]) for i in range(2)]
    own = call(take_last_kernel, [shape(block)], (out_weight,))[0]
    far, near = swap(own, "tp", 2), swap(own, "tp", 1)
    if aligned:
        slow_down = slow_down_weight.transpose(0, 2, 1)
        slow_in = slow_in_weight.transpose(0, 2, 1, 3)
        fresh_out_weight, fresh_down = call(
            average_down_kernel, [shape(slow_out_weight.shape, F32), shape(slow_down.shape, F32)],
            (out_weight, down_weight, slow_out_weight, slow_down),
        )
        fresh_in, fresh_up_weight = call(
            average_up_kernel, [shape(slow_in.shape, F32), shape(slow_up_weight.shape, F32)],
            (weight_in, up_weight, slow_in, slow_up_weight),
        )
        fresh_in_weight, fresh_down_weight = fresh_in.transpose(0, 2, 1, 3), fresh_down.transpose(0, 2, 1)
    else:
        start = lax.axis_index("rows") * piece
        fresh_in_weight, fresh_out_weight, fresh_up_weight, fresh_down_weight = (
            blend(slow, lax.dynamic_slice_in_dim(weight, start, piece, dim))
            for slow, weight, dim in (
                (slow_in_weight, in_weight, 1),
                (slow_out_weight, out_weight, 2),
                (slow_up_weight, up_weight, 1),
                (slow_down_weight, down_weight, 2),
            )
        )
    parts = []
    for i, (s, got) in enumerate(sums):
        parts.append(call(next_project_kernel, [act32, act, wide], (after[0][i], *add_own(s, got), pack, weight_in)))
    x_next, normed[1], qkv[1] = zip(*parts)
    blocks = mix(1)
    pieces = call(copy_kernel, [shape((cols // 4, width))] * 4, (far,))
    out_one = call(
        order_kernel, [shape((4 * cols, width))], (own, far, near, *(swap(p, "tp", 1) for p in pieces))
    )[0]
    parts = []
    for i in range(2):
        packed, far, near = blocks[i]
        parts.append(
            call(
                named(last_feed, i), [act32, act, hid, hid, eight, small, eighth, eighth],
                (x_next[i], out_one, pack, up_weight, down_weight, top, packed, far, near, *last_blocks(far, i)),
                scratch=two_cores,
            )
        )
    after[1], normed_two[1], active[1], dup, feed_one, keeps, *sends = zip(*parts)
    sums = [exchange(keeps[i], [s[i] for s in sends]) for i in range(2)]
    feed_scatter, attn_scatter = {1: Scatter(bits)}, {0: Scatter(bits), 1: Scatter(bits)}
    feed_scatter[1].add(feed_grads, 1, (top, *active[1]), free=True)
    feed_scatter[1].add(feed_grads, 1, (*normed_two[1], *dup))

    grad_after, attn, g_held, front_one = front(1, (top, top), sums, 2)
    dproj, back_one, (keep_a, keep_b, *sends) = back(1, [small] * 2 + [eighth] * 4)
    out_keep, out_send = call(down_kernel, [pair, pair], (*active[1], down_weight), scratch=two_cores)
    out_came = swap(out_send, "tp", 1)
    sums = [exchange(keep_a, sends[:2], touch=feed_scatter[1].came()[:1]), exchange(keep_b, sends[2:])]
    attn_scatter[1].add(attn_grads, 1, (*normed[1], dproj, *attn, *mixed[1]))
    feed_scatter[1].advance()

    parts = []
    for i, (s, got) in enumerate(sums):
        own = add_own(s, got)
        parts.append(
            call(
                named(feed_back, i), [act32, act, hid, eight, small, small],
                (x_next[i], *own, grad_after[i], pack, down_weight, slope[i], up_weight), scratch=two_cores,
            )
        )
        if i == 0:
            out_sum = call(add_whole_kernel, [pair], (out_keep, out_came))[0]
            out_came = swap(out_sum, "tp", 2)
    sends = [x[5:] for x in parts]
    above, branch, dup, feed_zero, keeps = zip(*(x[:5] for x in parts))
    touch = (*attn_scatter[1].came(), *feed_scatter[1].came())
    sums = [exchange(keeps[i], sends[i], touch=touch if i else ()) for i in range(2)]
    feed_scatter[0] = Scatter(bits)
    feed_scatter[0].add(feed_grads, 1, (*branch, *active[0]), free=True)
    feed_scatter[0].add(feed_grads, 1, (*normed_two[0], *dup))
    grad_after, attn, g_held, front_zero = front(0, above, sums, 2)
    dproj, back_zero, (keep, *sends) = back(0, [pair, small, small], touch=feed_scatter[0].came()[:1])
    s = call(
        add_pair_kernel, [pair], (keep, *(swap(x, "tp", 1) for x in sends)), touch=(out_came, *feed_scatter[0].came()[1:])
    )[0]
    got = swap(s, "tp", 2)
    out_sum = call(add_whole_kernel, [pair], (out_sum, out_came))[0]
    out_came = swap(out_sum, "tp", 1)
    feed_scatter[0].advance()
    attn_scatter[1].add(attn_grads, 1, (*normed[0], dproj, *attn, *mixed[0]))
    feed_scatter[1].advance()
    total = call(
        tail_sums_kernel, [shape((SUMMED, width), F32)],
        (tokens, pack, *grad_after, *feed_one, *feed_zero, *front_one, *front_zero, back_one, back_zero, keep, *sends),
    )[0]
    layer_out = call(
        output_kernel, [shape((count, width))], (*after[1], pack, out_sum, out_came), touch=feed_scatter[0].came()
    )[0].reshape(patches.shape)
    vector = [shape(total.shape, F32)]
    total = call(add_shared_kernel, vector, (total, swap(total, "tp", 1)))[0]
    got_total = swap(total, "tp", 2)
    attn_scatter[1].advance()
    feed_scatter[0].advance()
    own, *other = call(add_halves_kernel, [pair, small, small], (s, got), touch=feed_scatter[1].came())
    other = [swap(x, "tp", 1) for x in other]
    total = call(add_shared_kernel, vector, (total, got_total))[0]
    order = bits[-1:] + bits[:-1]
    got_total = swap(total, "rows", order[0])
    grad_patches = call(
        patches_kernel, [shape((count, width))], (tokens, pack, *grad_after, own, *other)
    )[0].reshape(patches.shape)
    for n, bit in enumerate(order[1:]):
        total = call(add_kernel, vector, (total, got_total))[0]
        got_total = swap(total, "rows", bit)
        if n == 0:
            attn_scatter[1].advance(touch=feed_scatter[0].came())
    zero, one = feed_scatter[0].finish(), feed_scatter[1].finish()
    grad_down, grad_up_weight = call(
        named(finish_feed, len(zero)), [shape((LAYERS, piece, ff), F32)] * 2, zero + one
    )
    both = shape((LAYERS, 2, width), F32)
    grad_mask_embed, grad_norm_gain, grad_norm_shift, grad_in_bias, grad_out_bias, grad_up_bias = call(
        unpack_kernel,
        [shape((width,), F32), both, both, shape(in_bias.shape, F32), both, shape(up_bias.shape, F32)],
        (total, got_total),
    )
    one = attn_scatter[1].finish()
    grad_in, grad_out_weight = call(
        finish_attn_kernel, [shape((LAYERS, 3, piece, cols), F32), shape((LAYERS, cols, piece), F32)], one
    )
    return (
        layer_out,
        grad_patches,
        grad_mask_embed,
        grad_norm_gain,
        grad_norm_shift,
        grad_in.transpose(0, 2, 1, 3),
        grad_in_bias,
        grad_out_weight,
        grad_out_bias,
        grad_up_weight,
        grad_up_bias,
        grad_down.transpose(0, 2, 1),
        fresh_small[0],
        fresh_small[1],
        fresh_small[2],
        fresh_in_weight,
        fresh_small[3],
        fresh_out_weight,
        fresh_small[4],
        fresh_up_weight,
        fresh_small[5],
        fresh_down_weight,
    )


def solution(mesh):
    placed = (
        P("rows", None, None),
        P("rows", None),
        P("rows", None),
        P("rows", None, None),
        P(),
        P(),
        P(),
        P(None, None, None, "tp"),
        P(None, None, "tp"),
        P(None, "tp", None),
        P(),
        P(None, None, "tp"),
        P(None, "tp"),
        P(None, "tp", None),
        P(),
        P(),
        P(),
        P(None, "rows", None, "tp"),
        P(None, None, "tp"),
        P(None, "tp", "rows"),
        P(),
        P(None, "rows", "tp"),
        P(None, "tp"),
        P(None, "tp", "rows"),
    )
    return jax.shard_map(
        per_device,
        mesh=mesh,
        in_specs=placed,
        out_specs=(
            P("rows", None, None),
            P("rows", None, None),
            P(),
            P(),
            P(),
            P(None, "rows", None, "tp"),
            P(None, None, "tp"),
            P(None, "tp", "rows"),
            P(),
            P(None, "rows", "tp"),
            P(None, "tp"),
            P(None, "tp", "rows"),
            P(),
            P(),
            P(),
            P(None, "rows", None, "tp"),
            P(None, None, "tp"),
            P(None, "tp", "rows"),
            P(),
            P(None, "rows", "tp"),
            P(None, "tp"),
            P(None, "tp", "rows"),
        ),
        check_vma=False,
    )
```

```python
import functools

import jax
import jax.numpy as jnp
from jax import lax
from jax.experimental import pallas as pl
from jax.experimental.pallas import tpu as pltpu
from jax.sharding import PartitionSpec as P

HD = 64
LAYERS = 2
EPSILON = 1e-06
DECAY = 0.8
NEGATIVE = -1e30
F32 = jnp.float32
BF16 = jnp.bfloat16


def swap(x, axis, bit):
    n = lax.axis_size(axis)
    return lax.ppermute(x, axis, [(i, i ^ bit) for i in range(n)])


def shape(dims, dtype=BF16):
    return jax.ShapeDtypeStruct(tuple(dims), dtype)


def run(body, outs, args, after=(), scratch=(), vmem=16, far=0):
    n_in, n_after = len(args), len(after)

    def kernel(*refs):
        me = lax.axis_index("tp")
        body((me % 2, me, lax.axis_index("rows")), *refs[:n_in], *refs[n_in + n_after :])

    near = pl.BlockSpec(memory_space=pltpu.VMEM)
    anywhere = pl.BlockSpec(memory_space=pl.ANY)
    return pl.pallas_call(
        kernel,
        in_specs=[near] * (n_in - far) + [anywhere] * (far + n_after),
        out_specs=[near] * len(outs),
        out_shape=outs,
        scratch_shapes=scratch,
        name=body.__name__,
        compiler_params=pltpu.CompilerParams(vmem_limit_bytes=vmem * 1024 * 1024),
        cost_estimate=pl.CostEstimate(flops=1, bytes_accessed=1, transcendentals=0),
    )(*args, *after)


def named(body, *first):
    kernel = functools.partial(body, *first)
    kernel.__name__ = body.__name__ + "_" + "_".join(map(str, first))
    return kernel


def dot(a, b):
    return jnp.dot(a, b, preferred_element_type=F32)


def dot_t(a, b):
    return lax.dot_general(a, b, (((1,), (1,)), ((), ())), preferred_element_type=F32)


def t_dot(a, b):
    return lax.dot_general(a, b, (((0,), (0,)), ((), ())), preferred_element_type=F32)


GAIN, SHIFT, OUT_BIAS, UP_BIAS, EMBED, SEG, FLAG, IN_BIAS, PACKED = 0, 4, 8, 12, 14, 15, 16, 17, 24
V_EMBED, V_GAIN, V_SHIFT, V_OUT, OWN, V_UP, V_IN, SUMMED = 0, 1, 5, 9, 13, 13, 15, 24


def norm_parts(values):
    center = values - jnp.mean(values, axis=-1, keepdims=True)
    spread = jnp.mean(center * center, axis=-1, keepdims=True)
    inv = lax.rsqrt(spread + EPSILON)
    return center * inv, inv


def norm_back(values, gain, cot):
    hat, inv = norm_parts(values)
    w = cot * gain
    mean_w = jnp.mean(w, axis=-1, keepdims=True)
    mean_wh = jnp.mean(w * hat, axis=-1, keepdims=True)
    return inv * (w - mean_w - hat * mean_wh), cot * hat


def column(row, lanes=128):
    return jnp.transpose(jnp.broadcast_to(row, (lanes, row.shape[1])))


def split_three(v):
    one = v.astype(BF16).astype(F32)
    two = (v - one).astype(BF16).astype(F32)
    return one, two, v - one - two


def chunk(i, half):
    return slice(i * half, i * half + half)


def row_of(pack, i):
    return pack[i : i + 1, :]


def add_rows(ref, first, rows):
    if first:
        ref[...] = jnp.zeros_like(ref)
    for n, r in enumerate(rows):
        ref[n : n + 1, :] += jnp.sum(r, axis=0, keepdims=True)


def share_out(at, value, held, sends, keep):
    half = value.shape[0] // 2
    for c in range(2):
        held[c] = value[c * half : c * half + half].astype(BF16)
    keep[...] = held[at[0]]
    if len(sends) == 1:
        sends[0][...] = held[1 - at[0]]
        return
    first = 0
    for s in sends:
        n = s.shape[0]
        s[...] = held[1 - at[0], first : first + n]
        first += n


def joined(at, own, others):
    own = own[...].astype(F32)
    other = jnp.concatenate([o[...].astype(F32) for o in others], axis=0)
    low = at[0] == 0
    return jnp.concatenate([jnp.where(low, own, other), jnp.where(low, other, own)], axis=0)


def entry_of(patches, pack, rows):
    on = column(pack[FLAG : FLAG + 1, rows])[:, :1] > 0.0
    return jnp.where(on, row_of(pack, EMBED), patches.astype(F32)), on


def project(x, l, pack, weight, normed_ref, qkv_ref):
    hat, _ = norm_parts(x)
    normed = (hat * row_of(pack, GAIN + 2 * l) + row_of(pack, SHIFT + 2 * l)).astype(BF16)
    normed_ref[...] = normed
    bias = row_of(pack, IN_BIAS + l)
    part, cols = qkv_ref.shape[1] // 3, weight.shape[1]
    for c in range(3):
        first = c * part
        out = (dot_t(normed, weight[c]) + bias[:, first : first + cols]).astype(BF16)
        if c == 0:
            out = out * jnp.asarray(HD**-0.5, BF16)
        qkv_ref[:, first : first + cols] = out
        qkv_ref[:, first + cols : first + part] = jnp.zeros((out.shape[0], part - cols), BF16)


def take_kernel(_, weights, out, sem):
    copy = pltpu.make_async_copy(weights.at[0], out, sem.at[0])
    copy.start()
    copy.wait()


def first_project_kernel(_, *refs):
    far, outs, held, sem = refs[:10], refs[10:15], refs[15:25], refs[25]
    pack, normed, qkv = outs[0], outs[1:3], outs[3:5]
    gain, shift, out_bias, up_bias, embed, seg, flags, in_bias, tokens, weight = far
    sources = [gain, shift, out_bias, up_bias, embed, seg, flags, in_bias, tokens, weight.at[0]]
    copies = [pltpu.make_async_copy(src, dst, sem.at[i]) for i, (src, dst) in enumerate(zip(sources, held))]
    for c in copies:
        c.start()
    for c in copies[:8]:
        c.wait()
    gain, shift, out_bias, up_bias, embed, seg, flags, in_bias, tokens, weight = held[:10]
    pack[...] = jnp.zeros_like(pack)
    for l in range(LAYERS):
        for base, ref in ((GAIN, gain), (SHIFT, shift), (OUT_BIAS, out_bias)):
            pack[base + 2 * l : base + 2 * l + 2, :] = ref[l]
        cols = in_bias.shape[2]
        last = pack.shape[1] // 3 * 2
        pack[IN_BIAS + l : IN_BIAS + l + 1, :cols] = in_bias[l, 0:1]
        pack[IN_BIAS + l : IN_BIAS + l + 1, last : last + cols] = in_bias[l, 1:2]
    pack[UP_BIAS : UP_BIAS + LAYERS, :] = up_bias[...]
    pack[EMBED : EMBED + 1, :] = embed[...].reshape(1, pack.shape[1])
    pack[SEG : SEG + 1, :] = seg[...].astype(F32)
    pack[FLAG : FLAG + 1, :] = flags[...].astype(F32)
    for c in copies[8:10]:
        c.wait()
    for i in range(2):
        rows = chunk(i, normed[i].shape[0])
        x, _on = entry_of(tokens[rows, :], pack, rows)
        project(x, 0, pack, weight, normed[i], qkv[i])


def next_project_kernel(at, after, own, low, high, pack, weight, x_ref, normed, qkv):
    x = after[...] + joined(at, own, (low, high)) + row_of(pack, OUT_BIAS + 1)
    x_ref[...] = x
    project(x, 1, pack, weight.at[1], normed, qkv)


def head_lanes(rows, h):
    lane = lax.broadcasted_iota(jnp.int32, (rows, 128), 1)
    upper = lane >= 64
    mine = upper if h % 2 else jnp.logical_not(upper)
    return mine, lane % 64


def two(refs, cols):
    return jnp.concatenate([r[:, cols] for r in refs], axis=0)


def attend(l, i, _, qkv_a, qkv_b, pack, mixed_ref, packed_ref, held_ref):
    qkv = (qkv_a, qkv_b)
    half, part = qkv_a.shape[0], qkv_a.shape[1] // 3
    heads, width = held_ref.shape[1] // 128, mixed_ref.shape[1]
    seg = column(row_of(pack, SEG)).astype(jnp.int32)
    for h in range(heads):
        lanes = h // 2 * 128
        mine, place = head_lanes(2 * half, h)
        apart = jnp.where((place < 4) & (place != seg), NEGATIVE, 0.0)
        keys = two(qkv, slice(part + lanes, part + lanes + 128))
        keys = jnp.where(mine, keys.astype(F32), apart).astype(BF16)
        values = two(qkv, slice(2 * part + lanes, 2 * part + lanes + 128))
        size = min(128, width - lanes)
        mine, place = mine[:half], place[:half]
        marks = (place == seg[chunk(i, half)]).astype(F32)
        q = qkv[i][:, lanes : lanes + 128].astype(F32)
        scores = dot_t(jnp.where(mine, q, marks).astype(BF16), keys)
        top = jnp.max(scores, axis=-1, keepdims=True)
        expo = jnp.exp(scores - top)
        total = jnp.sum(expo, axis=-1, keepdims=True)
        out = dot(expo.astype(BF16), values) / total
        one, twice, three = split_three(-(top + jnp.log(total)))
        marks = marks + jnp.where(
            place == 4, one, jnp.where(place == 5, twice, jnp.where(place == 6, three, 0.0))
        )
        held_ref[:, h * 128 : h * 128 + 128] = jnp.where(mine, q, marks).astype(BF16)
        if h % 2:
            out = jnp.where(mine, out, mixed_ref[:, lanes : lanes + 128].astype(F32))
        out = out[:, :size].astype(BF16)
        mixed_ref[:, lanes : lanes + size] = out
        if size == 128:
            packed_ref[:half, :] = out
        else:
            packed_ref[half:, :size] = out[: half // 2]
            packed_ref[half:, size:] = out[half // 2 :]


def gelu_both(u):
    phi = 0.5 * (1.0 + lax.erf(u * (0.5**0.5)))
    return u * phi, phi + u * jnp.exp(-0.5 * u * u) * 0.3989422804014327


def in_order(me, own, far, near, last):
    core, chip = me % 2 == 1, me // 2 == 1

    def pick(on, one, other):
        return jnp.where(on, other, one), jnp.where(on, one, other)

    own, far = pick(chip, own, far)
    near, last = pick(chip, near, last)
    own, near = pick(core, own, near)
    far, last = pick(core, far, last)
    return own, near, far, last


def copy_kernel(_, x, *outs):
    n = outs[0].shape[0]
    for i, o in enumerate(outs):
        o[...] = x[i * n : i * n + n]


def order_weights(at, own, far, near, last, out):
    rest = out.shape[0] - 512
    blocks = own[...], far[...], near[...], jnp.concatenate([p[...] for p in last], axis=0)
    for g, w in enumerate(in_order(at[1], *blocks)):
        out[g * 128 : g * 128 + 128, :] = w[:128]
        out[512 + g * rest // 4 : 512 + (g + 1) * rest // 4, :] = w[128:]


def order_kernel(at, own, far, near, one, twice, three, four, out):
    order_weights(at, own, far, near, (one, twice, three, four), out)


def take_last_kernel(_, weights, out):
    out[...] = weights[LAYERS - 1]


def mixed_rows(at, mixed):
    half = mixed[0].shape[0] * 2 // 3
    mixed = [m[...] for m in mixed[:3]] + [jnp.concatenate([m[...] for m in mixed[3:]], axis=0)]
    blocks = in_order(at[1], *[m[:half, :] for m in mixed])
    rest = in_order(at[1], *[m[half:, :] for m in mixed])
    rest = [jnp.concatenate([r[:, :64], r[:, 64:]], axis=0) for r in rest]
    pairs = [jnp.concatenate(rest[g : g + 2], axis=1) for g in (0, 2)]
    return jnp.concatenate([*blocks, *pairs], axis=1)


def feed_front(at, l, x, mixed, weights, pack, up, after_ref, normed_ref):
    after = x + row_of(pack, OUT_BIAS + 2 * l) + dot(mixed_rows(at, mixed), weights[...])
    after_ref[...] = after
    hat, _ = norm_parts(after)
    normed = (hat * row_of(pack, GAIN + 2 * l + 1) + row_of(pack, SHIFT + 2 * l + 1)).astype(BF16)
    normed_ref[...] = normed
    return gelu_both(dot(normed, up[l]) + row_of(pack, UP_BIAS + l))


def first_feed(i, at, patches, weights, pack, up, down, *refs):
    *mixed, after, normed, active_ref, slope_ref, keep, low, high, held = refs
    rows = chunk(i, after.shape[0])
    x, _ = entry_of(patches[rows, :], pack, rows)
    active, slope = feed_front(at, 0, x, mixed, weights, pack, up, after, normed)
    active = active.astype(BF16)
    active_ref[...] = active
    slope_ref[...] = slope.astype(BF16)
    share_out(at, dot(active, down[0]), held, (low, high), keep)


def last_feed(i, at, x, weights, pack, up, down, top, *refs):
    *mixed, after, normed, active_ref, dup_ref, sums_ref, keep, low, high, held = refs
    active, slope = feed_front(at, 1, x[...], mixed, weights, pack, up, after, normed)
    active_ref[...] = active.astype(BF16)
    branch = top[chunk(i, after.shape[0]), :]
    dup = (dot_t(branch, down[1]) * slope).astype(BF16)
    dup_ref[...] = dup
    add_rows(sums_ref, True, [dup.astype(F32), branch.astype(F32)])
    share_out(at, dot_t(dup, up[1]), held, (low, high), keep)


def down_kernel(at, active_a, active_b, down, keep, send, held):
    for i, active in enumerate((active_a, active_b)):
        share_out(at, dot(active[...], down[1]), held, (send.at[i],), keep.at[i])


def output_kernel(at, after_a, after_b, pack, own, one, two_, three, out_ref):
    half = after_a.shape[0]
    for i, after in enumerate((after_a, after_b)):
        y = after[...] + joined(at, own.at[i], chunk_of(i, (one, two_, three))) + row_of(pack, OUT_BIAS + 3)
        out_ref[chunk(i, half), :] = y.astype(BF16)


def attn_front(l, i, at, after, above, pack, out_w, mixed, own, *refs):
    *others, grad_ref, attn_ref, held_ref, sums_ref = refs
    width = mixed.shape[1]
    half = after.shape[0]
    cot = joined(at, own, others)
    pulled, prod = norm_back(after[...], row_of(pack, GAIN + 2 * l + 1), cot)
    above = above[chunk(i, half), :] if above.shape[0] > half else above[...]
    grad = pulled + above.astype(F32)
    grad_ref[...] = grad
    attn = grad.astype(BF16)
    attn_ref[...] = attn
    add_rows(sums_ref, True, [prod, cot, grad])
    mixed_grad = dot_t(attn, out_w[l]).astype(BF16).astype(F32)
    for h in range(width // HD):
        lanes = h // 2 * 128
        mine, place = head_lanes(half, h)
        size = min(128, width - lanes)
        mix = mixed[:, lanes : lanes + size].astype(F32)
        grads = mixed_grad[:, lanes : lanes + size]
        if size < 128:
            fill = jnp.zeros((half, 128 - size), F32)
            mix, grads = (jnp.concatenate([v, fill], axis=1) for v in (mix, grads))
        inner = jnp.sum(jnp.where(mine, mix * grads, 0.0), axis=-1, keepdims=True)
        one, twice, three = split_three(-inner)
        marks = jnp.where(place == 4, one, jnp.where(place == 5, twice, jnp.where(place == 6, three, 0.0)))
        held_ref[:, h * 128 : h * 128 + 128] = jnp.where(mine, grads, marks).astype(BF16)


def attend_back(l, at, qkv_a, qkv_b, pack, q_a, q_b, g_a, g_b, weight, dproj_ref, sums_ref, *refs):
    *refs, turned, held = refs
    if l:
        keeps, sends = refs[:2], (refs[2:4], refs[4:])
    else:
        *refs, stacked = refs
        n = stacked.shape[0] // 2
        keeps, sends = [refs[0].at[i] for i in range(2)], [(stacked.at[pl.ds(i * n, n)],) for i in range(2)]
    qkv, q_held, g_held = (qkv_a, qkv_b), (q_a, q_b), (g_a, g_b)
    half, width = qkv_a.shape
    length = 2 * half
    part = width // 3
    heads = q_a.shape[1] // 128
    seg = column(row_of(pack, SEG)).astype(jnp.int32)
    for h in range(heads):
        lanes = h // 2 * 128
        mine, place = head_lanes(half, h)
        ones = ((place >= 4) & (place < 7)).astype(F32)
        qh = two(q_held, slice(h * 128, h * 128 + 128))
        gh = two(g_held, slice(h * 128, h * 128 + 128))
        for i in range(2):
            rows = chunk(i, half)
            apart = jnp.where((place < 4) & (place != seg[rows]), NEGATIVE, ones)
            bare = qkv[i][:, part + lanes : part + lanes + 128]
            keys = jnp.where(mine, bare.astype(F32), apart).astype(BF16)
            values = qkv[i][:, 2 * part + lanes : 2 * part + lanes + 128].astype(F32)
            values = jnp.where(mine, values, ones).astype(BF16)
            probs = jnp.exp(dot_t(keys, qh))
            ds = (probs * dot_t(values, gh)).astype(BF16)
            gv = dot(probs.astype(BF16), gh).astype(BF16)
            gk = dot(ds, qh).astype(BF16)
            for base, g in ((part, gk), (2 * part, gv)):
                cols = slice(base + lanes, base + lanes + 128)
                if h % 2:
                    g = jnp.where(mine, g.astype(F32), dproj_ref[rows, cols].astype(F32)).astype(BF16)
                elif h == heads - 1:
                    g = jnp.where(mine, g.astype(F32), 0.0).astype(BF16)
                dproj_ref[rows, cols] = g
            dq = t_dot(bare, ds)
            if i == 0:
                turned[...] = dq
            else:
                turned[...] += dq
        dq = jnp.transpose(turned[...]) * HD**-0.5
        cols = slice(lanes, lanes + 128)
        mine, _ = head_lanes(length, h)
        if h % 2:
            dq = jnp.where(mine, dq, dproj_ref[:, cols].astype(F32))
        elif h == heads - 1:
            dq = jnp.where(mine, dq, 0.0)
        dproj_ref[:, cols] = dq.astype(BF16)
    cols = weight.shape[2]
    for i in range(2):
        dproj = dproj_ref[chunk(i, half), :]
        add_rows(sums_ref, i == 0, [dproj.astype(F32)])
        share = sum(dot(dproj[:, c * part : c * part + cols], weight[l, c]) for c in range(3))
        share_out(at, share, held, sends[i], keeps[i])
    if not l:
        n = refs[1].shape[0]
        for i, piece in enumerate(refs[1:]):
            piece[...] = stacked[i * n : i * n + n]


def feed_back(
    i, at, x, own, low, high, above, pack, down, slope, up, grad_ref, branch_ref, dup_ref, sums_ref, keep, *sends
):
    *sends, held = sends
    cot = joined(at, own, (low, high))
    pulled, prod = norm_back(x[...], row_of(pack, GAIN + 2), cot)
    grad = pulled + above[...]
    grad_ref[...] = grad
    branch = grad.astype(BF16)
    branch_ref[...] = branch
    dup = (dot_t(branch, down[0]) * slope[...].astype(F32)).astype(BF16)
    dup_ref[...] = dup
    add_rows(sums_ref, True, [prod, cot, grad, dup.astype(F32)])
    share_out(at, dot_t(dup, up[0]), held, sends, keep)


def tail_sums_kernel(
    at, patches, pack, above_a, above_b, feed_one_a, feed_one_b, feed_zero_a, feed_zero_b,
    front_one_a, front_one_b, front_zero_a, front_zero_b, back_one, back_zero, keep, *refs,
):
    *sends, out = refs
    out[...] = jnp.zeros_like(out)
    half = above_a.shape[0]
    for i, above in enumerate((above_a, above_b)):
        rows = chunk(i, half)
        cot = joined(at, keep.at[i], chunk_of(i, sends))
        x, on = entry_of(patches[rows, :], pack, rows)
        pulled, prod = norm_back(x, row_of(pack, GAIN), cot)
        embed = jnp.where(on, pulled + 0.25 * above[...], 0.0)
        for base, v in ((V_EMBED, embed), (V_GAIN, prod), (V_SHIFT, cot)):
            out[base : base + 1, :] += jnp.sum(v, axis=0, keepdims=True)
    feed_one = feed_one_a[...] + feed_one_b[...]
    feed_zero = feed_zero_a[...] + feed_zero_b[...]
    front_zero = front_zero_a[...] + front_zero_b[...]
    front_one = front_one_a[...] + front_one_b[...]
    for base, v, n in (
        (V_GAIN + 1, front_zero, 0),
        (V_GAIN + 2, feed_zero, 0),
        (V_GAIN + 3, front_one, 0),
        (V_SHIFT + 1, front_zero, 1),
        (V_SHIFT + 2, feed_zero, 1),
        (V_SHIFT + 3, front_one, 1),
        (V_OUT, front_zero, 2),
        (V_OUT + 1, feed_zero, 2),
        (V_OUT + 2, front_one, 2),
        (V_OUT + 3, feed_one, 1),
    ):
        out[base : base + 1, :] = 0.25 * v[n : n + 1, :]
    out[V_UP : V_UP + 1, :] = feed_zero[3:4, :]
    out[V_UP + 1 : V_UP + 2, :] = feed_one[0:1, :]
    out[V_IN : V_IN + 1, :] = back_zero[0:1, :]
    out[V_IN + 1 : V_IN + 2, :] = back_one[0:1, :]


def add_shared_kernel(_, mine, got, out):
    row = lax.broadcasted_iota(jnp.int32, mine.shape, 0)
    out[...] = mine[...] + jnp.where(row < OWN, got[...], 0.0)


def add_kernel(_, mine, got, out):
    out[...] = mine[...] + got[...]


def unpack_kernel(_, mine, got, embed, gain, shift, in_bias, out_bias, up_bias):
    v = mine[...] + got[...]
    embed[...] = v[V_EMBED]
    cols = in_bias.shape[2]
    last = v.shape[1] // 3 * 2
    for l in range(LAYERS):
        for base, ref in ((V_GAIN, gain), (V_SHIFT, shift), (V_OUT, out_bias)):
            ref[l] = v[base + 2 * l : base + 2 * l + 2]
        in_bias[l, 0:1, :] = v[V_IN + l : V_IN + l + 1, :cols]
        in_bias[l, 1:2, :] = v[V_IN + l : V_IN + l + 1, last : last + cols]
    up_bias[...] = v[V_UP : V_UP + LAYERS]


def patches_kernel(at, patches, pack, above_a, above_b, own, other_a, other_b, out_ref):
    half = above_a.shape[0]
    for i, (above, other) in enumerate(((above_a, other_a), (above_b, other_b))):
        rows = chunk(i, half)
        x, on = entry_of(patches[rows, :], pack, rows)
        pulled, _ = norm_back(x, row_of(pack, GAIN), joined(at, own.at[i], (other,)))
        out_ref[rows, :] = jnp.where(on, 0.0, pulled + above[...]).astype(BF16)


def split_rows(value, held, bit):
    size = 2 * held.shape[1]
    rows = value.shape[0] // size
    for n in range(size):
        held[n // bit % 2, n // (2 * bit) * bit + n % bit] = value[n * rows : n * rows + rows].astype(BF16)


def spread(refs, n):
    if len(refs) == n:
        return [r[...] for r in refs]
    half = refs[0].shape[0] // n
    return [refs[0][chunk(i, half), :] for i in range(n)]


def cut_terms(at, bit, value, refs):
    *pieces, held = refs
    split_rows(value, held, bit)
    mine = at[2] // bit
    n = pieces[0].shape[2]
    for i, ref in enumerate(pieces):
        cols = slice(i // 2 * n, i // 2 * n + n)
        ref[...] = held[(mine + 1 + i) % 2, :, :, cols]


def feed_grads(parts, bit, at, *refs):
    cuts = refs[-2 * parts - 1 :]
    *args, right_a, right_b = refs[: -2 * parts - 1]
    left = spread(args, 2)
    cut_terms(at, bit, t_dot(left[0], right_a[...]) + t_dot(left[1], right_b[...]), cuts)


def attn_grads(parts, bit, at, normed_a, normed_b, dproj, attn_a, attn_b, mixed_a, mixed_b, *refs):
    cols = mixed_a.shape[1]
    half, part = normed_a.shape[0], dproj.shape[1] // 3
    g = t_dot(normed_a[...], dproj[:half, :]) + t_dot(normed_b[...], dproj[half:, :])
    o = t_dot(attn_a[...], mixed_a[...]) + t_dot(attn_b[...], mixed_b[...])
    pieces = [g[:, c * part : c * part + cols] for c in range(3)] + [o]
    whole_lanes = [p[:, :128] for p in pieces]
    rest = [
        jnp.concatenate([pieces[i][:, 128:], pieces[i + 1][:, 128:]], axis=1) for i in range(0, 4, 2)
    ]
    cut_terms(at, bit, jnp.concatenate(whole_lanes + rest, axis=1), refs)


def halve(bit, under, n_out, at, *refs):
    pairs, outs = refs[: len(refs) - 2 * n_out], refs[len(refs) - 2 * n_out :]
    mine = (at[2] // bit) % 2
    n = outs[0].shape[2]
    first = 0
    for held, got in zip(pairs[::2], pairs[1::2]):
        last = first + held.shape[2]
        for p in range(n_out):
            low, high = max(first, p * n), min(last, p * n + n)
            if low >= high:
                continue
            source, target = slice(low - first, high - first), slice(low - p * n, high - p * n)
            for i in range(outs[0].shape[0]):
                for ref, side in ((outs[2 * p], 1 - mine), (outs[2 * p + 1], mine)):
                    j = i // under * 2 * under + side * under + i % under
                    both = held[j, :, source].astype(F32) + got[j, :, source].astype(F32)
                    ref[i, :, target] = both.astype(BF16)
        first = last


def split_pairs(cur, low, mine):
    pairs = cur.reshape(cur.shape[0] // (2 * low), 2, low, *cur.shape[1:])
    return [
        lax.dynamic_index_in_dim(pairs, side, 1, keepdims=False).reshape(-1, *cur.shape[1:]) for side in (1 - mine, mine)
    ]


def add_bf16(mine, got):
    return (mine[...].astype(F32) + got[...].astype(F32)).astype(BF16)


def add_bf16_kernel(_, mine, *refs):
    *gots, out = refs
    first = 0
    for g in gots:
        rows = slice(first, first + g.shape[0])
        out[rows] = add_bf16(mine.at[rows], g)
        first += g.shape[0]


def add_whole_kernel(_, mine, got, out):
    out[...] = add_bf16(mine, got)


def add_pieces_kernel(_, mine, got, out, *pieces):
    s = add_bf16(mine, got)
    out[...] = s
    n = pieces[0].shape[0]
    for i, p in enumerate(pieces):
        p[...] = s[i * n : i * n + n]


def chunk_of(i, pieces):
    n = pieces[1].shape[0] // 2
    return (pieces[0], pieces[1].at[pl.ds(0, n)]) if i == 0 else (pieces[1].at[pl.ds(n, n)], pieces[2])


def add_pair_kernel(_, mine, *refs):
    *gots, out = refs
    for i in range(2):
        first = 0
        for piece in chunk_of(i, gots):
            rows = slice(first, first + piece.shape[0])
            out[i, rows] = add_bf16(mine.at[i, rows], piece)
            first += piece.shape[0]


def add_chunks_kernel(_, mine, got, out_a, out_b):
    v = add_bf16(mine, got)
    out_a[...], out_b[...] = v[0], v[1]


def add_cut_kernel(_, mine_a, mine_b, got_a, got_b, out, one, two_, three):
    a, b = add_bf16(mine_a, got_a), add_bf16(mine_b, got_b)
    out[0], out[1] = a, b
    n = one.shape[0]
    one[...], three[...] = a[:n], b[-n:]
    two_[: n // 2], two_[n // 2 :] = a[n:], b[: n // 2]


def add_halves_kernel(_, mine, got, out, low, high):
    v = add_bf16(mine, got)
    out[...] = v
    low[...], high[...] = v[0], v[1]


def totals(refs):
    return jnp.concatenate(
        [k[0].astype(F32) + g[0].astype(F32) for k, g in zip(refs[::2], refs[1::2])], axis=1
    )


def finish_feed(n_zero, _, *refs):
    *refs, down, up = refs
    ff = up.shape[2]
    for l, part in enumerate((refs[:n_zero], refs[n_zero:])):
        v = totals(part)
        down[l], up[l] = v[:, :ff], v[:, ff:]


def finish_attn_kernel(_, *refs):
    *refs, in_ref, out_ref = refs
    cols = in_ref.shape[3]
    rest = cols - 128
    both = totals(refs)
    width = both.shape[1] // LAYERS
    for n in range(LAYERS):
        l = LAYERS - 1 - n
        v = both[:, n * width : n * width + width]
        for c in range(4):
            first, last = v[:, c * 128 : c * 128 + 128], v[:, 512 + c * rest : 512 + c * rest + rest]
            if c < 3:
                in_ref[l, c, :, :128] = first
                in_ref[l, c, :, 128:] = last
            else:
                out_ref[l] = jnp.transpose(jnp.concatenate([first, last], axis=1))


def blend(slow, weight):
    return DECAY * slow + (1.0 - DECAY) * weight.astype(F32)


def own_lanes(at, rows, width):
    place = lax.broadcasted_iota(jnp.int32, (rows, width), 0) + at[2] * rows
    return (lax.broadcasted_iota(jnp.int32, (rows, width), 1) == place).astype(BF16)


def average_up_kernel(at, in_w, up_w, slow_in, slow_up, fresh_in, fresh_up):
    rows, width = slow_up.shape[1:]
    pick = own_lanes(at, rows, width)
    for l in range(LAYERS):
        for c in range(3):
            fresh_in[l, c] = blend(slow_in[l, c], dot_t(pick, in_w[l, c]))
        fresh_up[l] = blend(slow_up[l], up_w[l, pl.ds(pl.multiple_of(at[2] * rows, 16), rows), :])


def average_down_kernel(at, out_w, down_w, slow_out, slow_down, fresh_out, fresh_down):
    rows, width = slow_down.shape[1:]
    pick = own_lanes(at, rows, down_w.shape[2])
    for l in range(LAYERS):
        fresh_out[l] = blend(slow_out[l], dot_t(out_w[l], pick))
        fresh_down[l] = blend(slow_down[l], dot_t(pick, down_w[l]))


def average_small_kernel(_, *refs):
    n = len(refs) // 3
    for slow, weight, fresh in zip(refs[:n], refs[n : 2 * n], refs[2 * n :]):
        fresh[...] = blend(slow[...], weight[...])


def per_device(
    patches,
    segment_ids,
    mask_flags,
    upstream,
    mask_embed,
    norm_gain,
    norm_shift,
    in_weight,
    in_bias,
    out_weight,
    out_bias,
    up_weight,
    up_bias,
    down_weight,
    slow_mask_embed,
    slow_norm_gain,
    slow_norm_shift,
    slow_in_weight,
    slow_in_bias,
    slow_out_weight,
    slow_out_bias,
    slow_up_weight,
    slow_up_bias,
    slow_down_weight,
):
    rows_here, length, width = patches.shape
    count = rows_here * length
    cols = in_weight.shape[3]
    ff = down_weight.shape[1]
    size = lax.axis_size("rows")
    piece = width // size
    aligned = piece % 16 == 0
    half = count // 2
    quarter = half // 2
    tokens = patches.reshape(count, width)
    top = upstream.reshape(count, width)
    weight_in = in_weight.transpose(0, 2, 3, 1)
    part = 3 * 128 * -(-cols // 128)
    heads = cols // HD
    act, act32, wide = shape((half, width)), shape((half, width), F32), shape((half, part))
    hid, held = shape((half, ff)), shape((half, heads * 128))
    small, pair = shape((quarter, width)), shape((2, quarter, width))
    eight, eighth, bit_of = shape((8, width), F32), shape((quarter // 2, width)), shape((quarter // 4, width))
    two_cores = [pltpu.VMEM((2, quarter, width), BF16)]
    last = []

    def call(body, outs, args, touch=(), free=False, **kwargs):
        if free:
            return run(body, outs, args, **kwargs)
        result = run(body, outs, args, after=tuple(last) + tuple(touch), **kwargs)
        last[:] = [min(result, key=lambda r: r.size)]
        return result

    def add(keep, gots, **kwargs):
        return call(add_bf16_kernel, [shape(keep.shape)], (keep, *gots), **kwargs)[0]

    def add_own(keep, got, parts=2, **kwargs):
        out = [shape((quarter // parts, width))] * parts
        own, *pieces = call(add_pieces_kernel, [small] + out, (keep, got), **kwargs)
        return (own, *(swap(p, "tp", 1) for p in pieces))

    def exchange(keep, sends, **kwargs):
        s = add(keep, [swap(s, "tp", 1) for s in sends], **kwargs)
        return s, swap(s, "tp", 2)

    def terms(kernel, parts, bit, args, **kwargs):
        n = width // parts
        if aligned:
            return call(
                named(kernel, parts, bit), [shape((size // 2, piece, n))] * (2 * parts), args,
                scratch=[pltpu.VMEM((2, size // 2, piece, width), BF16)], **kwargs,
            )
        if kernel is attn_grads:
            normed_a, normed_b, dproj_in, attn_a, attn_b, *mixed_in = args
            g = t_dot(jnp.concatenate([normed_a, normed_b]), dproj_in)
            o = t_dot(jnp.concatenate([attn_a, attn_b]), jnp.concatenate(mixed_in))
            pieces = [g[:, c * part // 3 : c * part // 3 + cols] for c in range(3)] + [o]
            sums = jnp.concatenate([p[:, :128] for p in pieces] + [p[:, 128:] for p in pieces], axis=1)
        else:
            sums = t_dot(jnp.concatenate(args[:-2]), jnp.concatenate(args[-2:]))
        sums = sums.astype(BF16).reshape(size, piece, width)
        mine = lax.axis_index("rows") // bit % 2
        return [x for i in range(parts) for x in split_pairs(sums[:, :, i * n : i * n + n], bit, mine)]

    def step(pieces, bit, low, parts, **kwargs):
        count_in, rows, _ = pieces[0].shape
        n = sum(p.shape[2] for p in pieces[::2]) // parts
        if aligned:
            return call(
                named(halve, bit, low, parts), [shape((count_in // 2, rows, n))] * (2 * parts), pieces, **kwargs
            )
        cur = [(k.astype(F32) + g.astype(F32)).astype(BF16) for k, g in zip(pieces[::2], pieces[1::2])]
        cur, mine = jnp.concatenate(cur, axis=2), lax.axis_index("rows") // bit % 2
        return [x for i in range(parts) for x in split_pairs(cur[:, :, i * n : i * n + n], low, mine)]

    bits = [1 << i for i in range(size.bit_length() - 1)]
    later = bits[1:] + bits[:1]

    class Scatter:
        def __init__(self, order):
            self.order, self.done, self.pieces = order, 0, ()

        def take(self, cuts):
            for send, keep in zip(cuts[::2], cuts[1::2]):
                self.pieces += (keep, swap(send, "rows", self.order[self.done]))

        def add(self, kernel, parts, args, **kwargs):
            self.take(terms(kernel, parts, self.order[0], args, **kwargs))

        def advance(self, parts=1, **kwargs):
            self.done += 1
            bit = self.order[self.done]
            low = 1 << sum(x < bit for x in self.order[self.done :])
            cuts = step(self.pieces, bit, low, parts, **kwargs)
            self.pieces = ()
            self.take(cuts)

        def came(self):
            return self.pieces[1::2]

        def finish(self):
            while self.done + 1 < len(self.order):
                self.advance()
            return self.pieces

    def mix(l):
        parts, blocks = [], []
        for i in range(2):
            m, packed, q = call(
                named(attend, l, i), [shape((half, cols)), shape((half + quarter, 128)), held], (*qkv[l], pack)
            )
            parts.append((m, q))
            blocks.append((packed, swap(packed, "tp", 2), swap(packed, "tp", 1)))
        mixed[l], q_held[l] = zip(*parts)
        return blocks

    def last_blocks(far, i):
        pieces = (far,)
        if i == 0:
            pieces = call(copy_kernel, [shape((far.shape[0] // 2, 128))] * 2, (far,))
        return [swap(p, "tp", 1) for p in pieces]

    def front(l, above, sums, parts, between=lambda: None):
        results = []
        for i, (s, got) in enumerate(sums):
            own = add_own(s, got, parts)
            results.append(
                call(
                    named(attn_front, l, i), [act32, act, held, eight],
                    (after[l][i], above[i], pack, out_weight, mixed[l][i], *own),
                )
            )
            if i == 0:
                between()
        return zip(*results)

    def back(l, shares, **kwargs):
        extra = [] if l else [pltpu.VMEM((half, width), BF16)]
        dproj, sums, *shares = call(
            named(attend_back, l), [shape((count, part)), shape((8, part), F32)] + shares,
            (*qkv[l], pack, *q_held[l], *g_held, weight_in), scratch=extra + [pltpu.VMEM((128, count), F32)] + two_cores, **kwargs,
        )
        return dproj, sums, shares

    normed, qkv, mixed, q_held, after, normed_two, active = {}, {}, {}, {}, {}, {}, {}

    far_args = (norm_gain, norm_shift, out_bias, up_bias, mask_embed, segment_ids, mask_flags, in_bias, tokens, weight_in)
    *far_args, far_weight = [pltpu.with_memory_space_constraint(a, pltpu.HBM) for a in far_args + (out_weight,)]
    block = (cols, width)
    own = call(
        take_kernel, [shape(block)], (far_weight,), scratch=[pltpu.SemaphoreType.DMA((1,))], far=1
    )[0]
    far, near = swap(own, "tp", 2), swap(own, "tp", 1)
    scratch = [pltpu.VMEM(a.shape, a.dtype) for a in far_args[:9]]
    scratch += [pltpu.VMEM(weight_in.shape[1:], BF16), pltpu.SemaphoreType.DMA((10,))]
    pack, *rest = call(
        first_project_kernel, [shape((PACKED, width), F32), act, act, wide, wide], far_args,
        scratch=scratch, far=len(far_args),
    )
    normed[0], qkv[0] = rest[:2], rest[2:]
    blocks = mix(0)
    pieces = call(copy_kernel, [shape((cols // 4, width))] * 4, (far,))
    out_zero = call(
        order_kernel, [shape((4 * cols, width))], (own, far, near, *(swap(p, "tp", 1) for p in pieces))
    )[0]
    slows = (slow_mask_embed, slow_norm_gain, slow_norm_shift, slow_in_bias, slow_out_bias, slow_up_bias)
    fresh_small = call(
        average_small_kernel, [shape(v.shape, F32) for v in slows],
        slows + (mask_embed, norm_gain, norm_shift, in_bias, out_bias, up_bias),
    )
    parts = []
    for i in range(2):
        packed, far, near = blocks[i]
        parts.append(
            call(
                named(first_feed, i), [act32, act, hid, hid, small, eighth, eighth],
                (tokens, out_zero, pack, up_weight, down_weight, packed, far, near, *last_blocks(far, i)), scratch=two_cores,
            )
        )
    after[0], normed_two[0], active[0], slope, keeps, *sends = zip(*parts)
    sums = [exchange(keeps[i], [s[i] for s in sends]) for i in range(2)]
    own = call(take_last_kernel, [shape(block)], (out_weight,))[0]
    far, near = swap(own, "tp", 2), swap(own, "tp", 1)
    if aligned:
        slow_down = slow_down_weight.transpose(0, 2, 1)
        slow_in = slow_in_weight.transpose(0, 2, 1, 3)
        fresh_out_weight, fresh_down = call(
            average_down_kernel, [shape(slow_out_weight.shape, F32), shape(slow_down.shape, F32)],
            (out_weight, down_weight, slow_out_weight, slow_down),
        )
        fresh_in, fresh_up_weight = call(
            average_up_kernel, [shape(slow_in.shape, F32), shape(slow_up_weight.shape, F32)],
            (weight_in, up_weight, slow_in, slow_up_weight),
        )
        fresh_in_weight, fresh_down_weight = fresh_in.transpose(0, 2, 1, 3), fresh_down.transpose(0, 2, 1)
    else:
        start = lax.axis_index("rows") * piece
        fresh_in_weight, fresh_out_weight, fresh_up_weight, fresh_down_weight = (
            blend(slow, lax.dynamic_slice_in_dim(weight, start, piece, dim))
            for slow, weight, dim in (
                (slow_in_weight, in_weight, 1),
                (slow_out_weight, out_weight, 2),
                (slow_up_weight, up_weight, 1),
                (slow_down_weight, down_weight, 2),
            )
        )
    parts = []
    for i, (s, got) in enumerate(sums):
        parts.append(call(next_project_kernel, [act32, act, wide], (after[0][i], *add_own(s, got), pack, weight_in)))
    x_next, normed[1], qkv[1] = zip(*parts)
    blocks = mix(1)
    pieces = call(copy_kernel, [shape((cols // 4, width))] * 4, (far,))
    out_one = call(
        order_kernel, [shape((4 * cols, width))], (own, far, near, *(swap(p, "tp", 1) for p in pieces))
    )[0]
    parts = []
    for i in range(2):
        packed, far, near = blocks[i]
        parts.append(
            call(
                named(last_feed, i), [act32, act, hid, hid, eight, small, eighth, eighth],
                (x_next[i], out_one, pack, up_weight, down_weight, top, packed, far, near, *last_blocks(far, i)),
                scratch=two_cores,
            )
        )
    after[1], normed_two[1], active[1], dup, feed_one, keeps, *sends = zip(*parts)
    sums = [exchange(keeps[i], [s[i] for s in sends]) for i in range(2)]
    feed_scatter, attn_scatter = {1: Scatter(bits)}, {0: Scatter(bits), 1: Scatter(bits)}
    feed_scatter[1].add(feed_grads, 1, (top, *active[1]), free=True)
    feed_scatter[1].add(feed_grads, 1, (*normed_two[1], *dup))

    grad_after, attn, g_held, front_one = front(1, (top, top), sums, 2)
    dproj, back_one, (keep_a, keep_b, *sends) = back(1, [small] * 2 + [eighth] * 4)
    sums = [exchange(keep_a, sends[:2], touch=feed_scatter[1].came()[:1]), exchange(keep_b, sends[2:])]
    attn_scatter[1].add(attn_grads, 1, (*normed[1], dproj, *attn, *mixed[1]))
    feed_scatter[1].advance()

    parts = []
    for i, (s, got) in enumerate(sums):
        own = add_own(s, got)
        parts.append(
            call(
                named(feed_back, i), [act32, act, hid, eight, small, small],
                (x_next[i], *own, grad_after[i], pack, down_weight, slope[i], up_weight), scratch=two_cores,
            )
        )
    sends = [x[5:] for x in parts]
    above, branch, dup, feed_zero, keeps = zip(*(x[:5] for x in parts))
    touch = (*attn_scatter[1].came(), *feed_scatter[1].came())
    sums = [exchange(keeps[i], sends[i], touch=touch if i else ()) for i in range(2)]
    feed_scatter[0] = Scatter(bits)
    feed_scatter[0].add(feed_grads, 1, (*branch, *active[0]), free=True)
    feed_scatter[0].add(feed_grads, 1, (*normed_two[0], *dup))
    grad_after, attn, g_held, front_zero = front(0, above, sums, 2, feed_scatter[1].advance)
    dproj, back_zero, (keep, *sends) = back(0, [pair] + [shape((half // 3, width))] * 3, touch=feed_scatter[0].came()[:1])
    attn_scatter[1].add(attn_grads, 1, (*normed[0], dproj, *attn, *mixed[0]))
    feed_scatter[0].advance()
    s = call(
        add_pair_kernel, [pair], (keep, *(swap(x, "tp", 1) for x in sends)), touch=feed_scatter[1].came()
    )[0]
    got = swap(s, "tp", 2)
    total = call(
        tail_sums_kernel, [shape((SUMMED, width), F32)],
        (tokens, pack, *grad_after, *feed_one, *feed_zero, *front_one, *front_zero, back_one, back_zero, keep, *sends),
    )[0]
    out_keep, out_send = call(down_kernel, [pair, pair], (*active[1], down_weight), scratch=two_cores)
    out_came = swap(out_send, "tp", 1)
    vector = [shape(total.shape, F32)]
    total = call(add_shared_kernel, vector, (total, swap(total, "tp", 1)))[0]
    got_total = swap(total, "tp", 2)
    attn_scatter[1].advance()
    feed_scatter[0].advance()
    own, *other = call(add_halves_kernel, [pair, small, small], (s, got))
    other = [swap(x, "tp", 1) for x in other]
    grad_patches = call(
        patches_kernel, [shape((count, width))], (tokens, pack, *grad_after, own, *other)
    )[0].reshape(patches.shape)
    total = call(add_shared_kernel, vector, (total, got_total))[0]
    order = bits[-1:] + bits[:-1]
    got_total = swap(total, "rows", order[0])
    out_sums = call(add_chunks_kernel, [small, small], (out_keep, out_came))
    out_came = [swap(x, "tp", 2) for x in out_sums]
    for n, bit in enumerate(order[1:]):
        total = call(add_kernel, vector, (total, got_total))[0]
        got_total = swap(total, "rows", bit)
        if n == 0:
            attn_scatter[1].advance(touch=feed_scatter[0].came())
    out_sum, *pieces = call(
        add_cut_kernel, [pair] + [shape((half // 3, width))] * 3, (*out_sums, *out_came)
    )
    pieces = [swap(x, "tp", 1) for x in pieces]
    zero, one = feed_scatter[0].finish(), feed_scatter[1].finish()
    grad_down, grad_up_weight = call(
        named(finish_feed, len(zero)), [shape((LAYERS, piece, ff), F32)] * 2, zero + one
    )
    both = shape((LAYERS, 2, width), F32)
    layer_out = call(output_kernel, [shape((count, width))], (*after[1], pack, out_sum, *pieces))[0]
    layer_out = layer_out.reshape(patches.shape)
    grad_mask_embed, grad_norm_gain, grad_norm_shift, grad_in_bias, grad_out_bias, grad_up_bias = call(
        unpack_kernel,
        [shape((width,), F32), both, both, shape(in_bias.shape, F32), both, shape(up_bias.shape, F32)],
        (total, got_total),
    )
    one = attn_scatter[1].finish()
    grad_in, grad_out_weight = call(
        finish_attn_kernel, [shape((LAYERS, 3, piece, cols), F32), shape((LAYERS, cols, piece), F32)], one
    )
    return (
        layer_out,
        grad_patches,
        grad_mask_embed,
        grad_norm_gain,
        grad_norm_shift,
        grad_in.transpose(0, 2, 1, 3),
        grad_in_bias,
        grad_out_weight,
        grad_out_bias,
        grad_up_weight,
        grad_up_bias,
        grad_down.transpose(0, 2, 1),
        fresh_small[0],
        fresh_small[1],
        fresh_small[2],
        fresh_in_weight,
        fresh_small[3],
        fresh_out_weight,
        fresh_small[4],
        fresh_up_weight,
        fresh_small[5],
        fresh_down_weight,
    )


def solution(mesh):
    placed = (
        P("rows", None, None),
        P("rows", None),
        P("rows", None),
        P("rows", None, None),
        P(),
        P(),
        P(),
        P(None, None, None, "tp"),
        P(None, None, "tp"),
        P(None, "tp", None),
        P(),
        P(None, None, "tp"),
        P(None, "tp"),
        P(None, "tp", None),
        P(),
        P(),
        P(),
        P(None, "rows", None, "tp"),
        P(None, None, "tp"),
        P(None, "tp", "rows"),
        P(),
        P(None, "rows", "tp"),
        P(None, "tp"),
        P(None, "tp", "rows"),
    )
    return jax.shard_map(
        per_device,
        mesh=mesh,
        in_specs=placed,
        out_specs=(
            P("rows", None, None),
            P("rows", None, None),
            P(),
            P(),
            P(),
            P(None, "rows", None, "tp"),
            P(None, None, "tp"),
            P(None, "tp", "rows"),
            P(),
            P(None, "rows", "tp"),
            P(None, "tp"),
            P(None, "tp", "rows"),
            P(),
            P(),
            P(),
            P(None, "rows", None, "tp"),
            P(None, None, "tp"),
            P(None, "tp", "rows"),
            P(),
            P(None, "rows", "tp"),
            P(None, "tp"),
            P(None, "tp", "rows"),
        ),
        check_vma=False,
    )
```

```python
import functools

import jax
import jax.numpy as jnp
from jax import lax
from jax.experimental import pallas as pl
from jax.experimental.pallas import tpu as pltpu
from jax.sharding import PartitionSpec as P

HD = 64
LAYERS = 2
EPSILON = 1e-06
DECAY = 0.8
NEGATIVE = -1e30
F32 = jnp.float32
BF16 = jnp.bfloat16


def swap(x, axis, bit):
    n = lax.axis_size(axis)
    return lax.ppermute(x, axis, [(i, i ^ bit) for i in range(n)])


def shape(dims, dtype=BF16):
    return jax.ShapeDtypeStruct(tuple(dims), dtype)


def run(body, outs, args, after=(), scratch=(), vmem=16, far=0):
    n_in, n_after = len(args), len(after)

    def kernel(*refs):
        me = lax.axis_index("tp")
        body((me % 2, me, lax.axis_index("rows")), *refs[:n_in], *refs[n_in + n_after :])

    near = pl.BlockSpec(memory_space=pltpu.VMEM)
    anywhere = pl.BlockSpec(memory_space=pl.ANY)
    return pl.pallas_call(
        kernel,
        in_specs=[near] * (n_in - far) + [anywhere] * (far + n_after),
        out_specs=[near] * len(outs),
        out_shape=outs,
        scratch_shapes=scratch,
        name=body.__name__,
        compiler_params=pltpu.CompilerParams(vmem_limit_bytes=vmem * 1024 * 1024),
        cost_estimate=pl.CostEstimate(flops=1, bytes_accessed=1, transcendentals=0),
    )(*args, *after)


def named(body, *first):
    kernel = functools.partial(body, *first)
    kernel.__name__ = body.__name__ + "_" + "_".join(map(str, first))
    return kernel


def dot(a, b):
    return jnp.dot(a, b, preferred_element_type=F32)


def dot_t(a, b):
    return lax.dot_general(a, b, (((1,), (1,)), ((), ())), preferred_element_type=F32)


def t_dot(a, b):
    return lax.dot_general(a, b, (((0,), (0,)), ((), ())), preferred_element_type=F32)


GAIN, SHIFT, OUT_BIAS, UP_BIAS, EMBED, SEG, FLAG, IN_BIAS, PACKED = 0, 4, 8, 12, 14, 15, 16, 17, 24
V_EMBED, V_GAIN, V_SHIFT, V_OUT, OWN, V_UP, V_IN, SUMMED = 0, 1, 5, 9, 13, 13, 15, 24


def norm_parts(values):
    center = values - jnp.mean(values, axis=-1, keepdims=True)
    spread = jnp.mean(center * center, axis=-1, keepdims=True)
    inv = lax.rsqrt(spread + EPSILON)
    return center * inv, inv


def norm_back(values, gain, cot):
    hat, inv = norm_parts(values)
    w = cot * gain
    mean_w = jnp.mean(w, axis=-1, keepdims=True)
    mean_wh = jnp.mean(w * hat, axis=-1, keepdims=True)
    return inv * (w - mean_w - hat * mean_wh), cot * hat


def column(row, lanes=128):
    return jnp.transpose(jnp.broadcast_to(row, (lanes, row.shape[1])))


def split_three(v):
    one = v.astype(BF16).astype(F32)
    two = (v - one).astype(BF16).astype(F32)
    return one, two, v - one - two


def chunk(i, half):
    return slice(i * half, i * half + half)


def row_of(pack, i):
    return pack[i : i + 1, :]


def add_rows(ref, first, rows):
    if first:
        ref[...] = jnp.zeros_like(ref)
    for n, r in enumerate(rows):
        ref[n : n + 1, :] += jnp.sum(r, axis=0, keepdims=True)


def share_out(at, value, held, sends, keep):
    half = value.shape[0] // 2
    for c in range(2):
        held[c] = value[c * half : c * half + half].astype(BF16)
    keep[...] = held[at[0]]
    if len(sends) == 1:
        sends[0][...] = held[1 - at[0]]
        return
    first = 0
    for s in sends:
        n = s.shape[0]
        s[...] = held[1 - at[0], first : first + n]
        first += n


def joined(at, own, others):
    own = own[...].astype(F32)
    other = jnp.concatenate([o[...].astype(F32) for o in others], axis=0)
    low = at[0] == 0
    return jnp.concatenate([jnp.where(low, own, other), jnp.where(low, other, own)], axis=0)


def entry_of(patches, pack, rows):
    on = column(pack[FLAG : FLAG + 1, rows])[:, :1] > 0.0
    return jnp.where(on, row_of(pack, EMBED), patches.astype(F32)), on


def project(x, l, pack, weight, normed_ref, qkv_ref):
    hat, _ = norm_parts(x)
    normed = (hat * row_of(pack, GAIN + 2 * l) + row_of(pack, SHIFT + 2 * l)).astype(BF16)
    normed_ref[...] = normed
    bias = row_of(pack, IN_BIAS + l)
    part, cols = qkv_ref.shape[1] // 3, weight.shape[1]
    for c in range(3):
        first = c * part
        out = (dot_t(normed, weight[c]) + bias[:, first : first + cols]).astype(BF16)
        if c == 0:
            out = out * jnp.asarray(HD**-0.5, BF16)
        qkv_ref[:, first : first + cols] = out
        qkv_ref[:, first + cols : first + part] = jnp.zeros((out.shape[0], part - cols), BF16)


def take_kernel(_, weights, out, sem):
    copy = pltpu.make_async_copy(weights.at[0], out, sem.at[0])
    copy.start()
    copy.wait()


def first_project_kernel(_, *refs):
    far, outs, held, sem = refs[:10], refs[10:15], refs[15:25], refs[25]
    pack, normed, qkv = outs[0], outs[1:3], outs[3:5]
    gain, shift, out_bias, up_bias, embed, seg, flags, in_bias, tokens, weight = far
    sources = [gain, shift, out_bias, up_bias, embed, seg, flags, in_bias, tokens, weight.at[0]]
    copies = [pltpu.make_async_copy(src, dst, sem.at[i]) for i, (src, dst) in enumerate(zip(sources, held))]
    for c in copies:
        c.start()
    for c in copies[:8]:
        c.wait()
    gain, shift, out_bias, up_bias, embed, seg, flags, in_bias, tokens, weight = held[:10]
    pack[...] = jnp.zeros_like(pack)
    for l in range(LAYERS):
        for base, ref in ((GAIN, gain), (SHIFT, shift), (OUT_BIAS, out_bias)):
            pack[base + 2 * l : base + 2 * l + 2, :] = ref[l]
        cols = in_bias.shape[2]
        last = pack.shape[1] // 3 * 2
        pack[IN_BIAS + l : IN_BIAS + l + 1, :cols] = in_bias[l, 0:1]
        pack[IN_BIAS + l : IN_BIAS + l + 1, last : last + cols] = in_bias[l, 1:2]
    pack[UP_BIAS : UP_BIAS + LAYERS, :] = up_bias[...]
    pack[EMBED : EMBED + 1, :] = embed[...].reshape(1, pack.shape[1])
    pack[SEG : SEG + 1, :] = seg[...].astype(F32)
    pack[FLAG : FLAG + 1, :] = flags[...].astype(F32)
    for c in copies[8:10]:
        c.wait()
    for i in range(2):
        rows = chunk(i, normed[i].shape[0])
        x, _on = entry_of(tokens[rows, :], pack, rows)
        project(x, 0, pack, weight, normed[i], qkv[i])


def next_project_kernel(at, after, own, low, high, pack, weight, x_ref, normed, qkv):
    x = after[...] + joined(at, own, (low, high)) + row_of(pack, OUT_BIAS + 1)
    x_ref[...] = x
    project(x, 1, pack, weight.at[1], normed, qkv)


def head_lanes(rows, h):
    lane = lax.broadcasted_iota(jnp.int32, (rows, 128), 1)
    upper = lane >= 64
    mine = upper if h % 2 else jnp.logical_not(upper)
    return mine, lane % 64


def two(refs, cols):
    return jnp.concatenate([r[:, cols] for r in refs], axis=0)


def attend(l, i, _, qkv_a, qkv_b, pack, mixed_ref, packed_ref, held_ref):
    qkv = (qkv_a, qkv_b)
    half, part = qkv_a.shape[0], qkv_a.shape[1] // 3
    heads, width = held_ref.shape[1] // 128, mixed_ref.shape[1]
    seg = column(row_of(pack, SEG)).astype(jnp.int32)
    for h in range(heads):
        lanes = h // 2 * 128
        mine, place = head_lanes(2 * half, h)
        apart = jnp.where((place < 4) & (place != seg), NEGATIVE, 0.0)
        keys = two(qkv, slice(part + lanes, part + lanes + 128))
        keys = jnp.where(mine, keys.astype(F32), apart).astype(BF16)
        values = two(qkv, slice(2 * part + lanes, 2 * part + lanes + 128))
        size = min(128, width - lanes)
        mine, place = mine[:half], place[:half]
        marks = (place == seg[chunk(i, half)]).astype(F32)
        q = qkv[i][:, lanes : lanes + 128].astype(F32)
        scores = dot_t(jnp.where(mine, q, marks).astype(BF16), keys)
        top = jnp.max(scores, axis=-1, keepdims=True)
        expo = jnp.exp(scores - top)
        total = jnp.sum(expo, axis=-1, keepdims=True)
        out = dot(expo.astype(BF16), values) / total
        one, twice, three = split_three(-(top + jnp.log(total)))
        marks = marks + jnp.where(
            place == 4, one, jnp.where(place == 5, twice, jnp.where(place == 6, three, 0.0))
        )
        held_ref[:, h * 128 : h * 128 + 128] = jnp.where(mine, q, marks).astype(BF16)
        if h % 2:
            out = jnp.where(mine, out, mixed_ref[:, lanes : lanes + 128].astype(F32))
        out = out[:, :size].astype(BF16)
        mixed_ref[:, lanes : lanes + size] = out
        if size == 128:
            packed_ref[:half, :] = out
        else:
            packed_ref[half:, :size] = out[: half // 2]
            packed_ref[half:, size:] = out[half // 2 :]


def gelu_both(u):
    phi = 0.5 * (1.0 + lax.erf(u * (0.5**0.5)))
    return u * phi, phi + u * jnp.exp(-0.5 * u * u) * 0.3989422804014327


def in_order(me, own, far, near, last):
    core, chip = me % 2 == 1, me // 2 == 1

    def pick(on, one, other):
        return jnp.where(on, other, one), jnp.where(on, one, other)

    own, far = pick(chip, own, far)
    near, last = pick(chip, near, last)
    own, near = pick(core, own, near)
    far, last = pick(core, far, last)
    return own, near, far, last


def copy_kernel(_, x, *outs):
    n = outs[0].shape[0]
    for i, o in enumerate(outs):
        o[...] = x[i * n : i * n + n]


def order_weights(at, own, far, near, last, out):
    rest = out.shape[0] - 512
    blocks = own[...], far[...], near[...], jnp.concatenate([p[...] for p in last], axis=0)
    for g, w in enumerate(in_order(at[1], *blocks)):
        out[g * 128 : g * 128 + 128, :] = w[:128]
        out[512 + g * rest // 4 : 512 + (g + 1) * rest // 4, :] = w[128:]


def order_kernel(at, own, far, near, one, twice, three, four, out):
    order_weights(at, own, far, near, (one, twice, three, four), out)


def take_last_kernel(_, weights, out):
    out[...] = weights[LAYERS - 1]


def mixed_rows(at, mixed):
    half = mixed[0].shape[0] * 2 // 3
    mixed = [m[...] for m in mixed[:3]] + [jnp.concatenate([m[...] for m in mixed[3:]], axis=0)]
    blocks = in_order(at[1], *[m[:half, :] for m in mixed])
    rest = in_order(at[1], *[m[half:, :] for m in mixed])
    rest = [jnp.concatenate([r[:, :64], r[:, 64:]], axis=0) for r in rest]
    pairs = [jnp.concatenate(rest[g : g + 2], axis=1) for g in (0, 2)]
    return jnp.concatenate([*blocks, *pairs], axis=1)


def feed_front(at, l, x, mixed, weights, pack, up, after_ref, normed_ref):
    after = x + row_of(pack, OUT_BIAS + 2 * l) + dot(mixed_rows(at, mixed), weights[...])
    after_ref[...] = after
    hat, _ = norm_parts(after)
    normed = (hat * row_of(pack, GAIN + 2 * l + 1) + row_of(pack, SHIFT + 2 * l + 1)).astype(BF16)
    normed_ref[...] = normed
    return gelu_both(dot(normed, up[l]) + row_of(pack, UP_BIAS + l))


def first_feed(i, at, patches, weights, pack, up, down, *refs):
    *mixed, after, normed, active_ref, slope_ref, keep, low, high, held = refs
    rows = chunk(i, after.shape[0])
    x, _ = entry_of(patches[rows, :], pack, rows)
    active, slope = feed_front(at, 0, x, mixed, weights, pack, up, after, normed)
    active = active.astype(BF16)
    active_ref[...] = active
    slope_ref[...] = slope.astype(BF16)
    share_out(at, dot(active, down[0]), held, (low, high), keep)


def last_feed(i, at, x, weights, pack, up, down, top, *refs):
    *mixed, after, normed, active_ref, dup_ref, sums_ref, keep, low, high, held = refs
    active, slope = feed_front(at, 1, x[...], mixed, weights, pack, up, after, normed)
    active_ref[...] = active.astype(BF16)
    branch = top[chunk(i, after.shape[0]), :]
    dup = (dot_t(branch, down[1]) * slope).astype(BF16)
    dup_ref[...] = dup
    add_rows(sums_ref, True, [dup.astype(F32), branch.astype(F32)])
    share_out(at, dot_t(dup, up[1]), held, (low, high), keep)


def down_kernel(at, active_a, active_b, down, keep, send, held):
    for i, active in enumerate((active_a, active_b)):
        share_out(at, dot(active[...], down[1]), held, (send.at[i],), keep.at[i])


def output_kernel(at, after_a, after_b, pack, own, one, two_, three, out_ref):
    half = after_a.shape[0]
    for i, after in enumerate((after_a, after_b)):
        y = after[...] + joined(at, own.at[i], chunk_of(i, (one, two_, three))) + row_of(pack, OUT_BIAS + 3)
        out_ref[chunk(i, half), :] = y.astype(BF16)


def attn_front(l, i, at, after, above, pack, out_w, mixed, own, *refs):
    *others, grad_ref, attn_ref, held_ref, sums_ref = refs
    width = mixed.shape[1]
    half = after.shape[0]
    cot = joined(at, own, others)
    pulled, prod = norm_back(after[...], row_of(pack, GAIN + 2 * l + 1), cot)
    above = above[chunk(i, half), :] if above.shape[0] > half else above[...]
    grad = pulled + above.astype(F32)
    grad_ref[...] = grad
    attn = grad.astype(BF16)
    attn_ref[...] = attn
    add_rows(sums_ref, True, [prod, cot, grad])
    mixed_grad = dot_t(attn, out_w[l]).astype(BF16).astype(F32)
    for h in range(width // HD):
        lanes = h // 2 * 128
        mine, place = head_lanes(half, h)
        size = min(128, width - lanes)
        mix = mixed[:, lanes : lanes + size].astype(F32)
        grads = mixed_grad[:, lanes : lanes + size]
        if size < 128:
            fill = jnp.zeros((half, 128 - size), F32)
            mix, grads = (jnp.concatenate([v, fill], axis=1) for v in (mix, grads))
        inner = jnp.sum(jnp.where(mine, mix * grads, 0.0), axis=-1, keepdims=True)
        one, twice, three = split_three(-inner)
        marks = jnp.where(place == 4, one, jnp.where(place == 5, twice, jnp.where(place == 6, three, 0.0)))
        held_ref[:, h * 128 : h * 128 + 128] = jnp.where(mine, grads, marks).astype(BF16)


def attend_back(l, at, qkv_a, qkv_b, pack, q_a, q_b, g_a, g_b, weight, dproj_ref, sums_ref, *refs):
    *refs, turned, held = refs
    if l:
        keeps, sends = refs[:2], (refs[2:4], refs[4:])
    else:
        *refs, stacked = refs
        n = stacked.shape[0] // 2
        keeps, sends = [refs[0].at[i] for i in range(2)], [(stacked.at[pl.ds(i * n, n)],) for i in range(2)]
    qkv, q_held, g_held = (qkv_a, qkv_b), (q_a, q_b), (g_a, g_b)
    half, width = qkv_a.shape
    length = 2 * half
    part = width // 3
    heads = q_a.shape[1] // 128
    seg = column(row_of(pack, SEG)).astype(jnp.int32)
    for h in range(heads):
        lanes = h // 2 * 128
        mine, place = head_lanes(half, h)
        ones = ((place >= 4) & (place < 7)).astype(F32)
        qh = two(q_held, slice(h * 128, h * 128 + 128))
        gh = two(g_held, slice(h * 128, h * 128 + 128))
        for i in range(2):
            rows = chunk(i, half)
            apart = jnp.where((place < 4) & (place != seg[rows]), NEGATIVE, ones)
            bare = qkv[i][:, part + lanes : part + lanes + 128]
            keys = jnp.where(mine, bare.astype(F32), apart).astype(BF16)
            values = qkv[i][:, 2 * part + lanes : 2 * part + lanes + 128].astype(F32)
            values = jnp.where(mine, values, ones).astype(BF16)
            probs = jnp.exp(dot_t(keys, qh))
            ds = (probs * dot_t(values, gh)).astype(BF16)
            gv = dot(probs.astype(BF16), gh).astype(BF16)
            gk = dot(ds, qh).astype(BF16)
            for base, g in ((part, gk), (2 * part, gv)):
                cols = slice(base + lanes, base + lanes + 128)
                if h % 2:
                    g = jnp.where(mine, g.astype(F32), dproj_ref[rows, cols].astype(F32)).astype(BF16)
                elif h == heads - 1:
                    g = jnp.where(mine, g.astype(F32), 0.0).astype(BF16)
                dproj_ref[rows, cols] = g
            dq = t_dot(bare, ds)
            if i == 0:
                turned[...] = dq
            else:
                turned[...] += dq
        dq = jnp.transpose(turned[...]) * HD**-0.5
        cols = slice(lanes, lanes + 128)
        mine, _ = head_lanes(length, h)
        if h % 2:
            dq = jnp.where(mine, dq, dproj_ref[:, cols].astype(F32))
        elif h == heads - 1:
            dq = jnp.where(mine, dq, 0.0)
        dproj_ref[:, cols] = dq.astype(BF16)
    cols = weight.shape[2]
    for i in range(2):
        dproj = dproj_ref[chunk(i, half), :]
        add_rows(sums_ref, i == 0, [dproj.astype(F32)])
        share = sum(dot(dproj[:, c * part : c * part + cols], weight[l, c]) for c in range(3))
        share_out(at, share, held, sends[i], keeps[i])
    if not l:
        n = refs[1].shape[0]
        for i, piece in enumerate(refs[1:]):
            piece[...] = stacked[i * n : i * n + n]


def feed_back(
    i, at, x, own, low, high, above, pack, down, slope, up, grad_ref, branch_ref, dup_ref, sums_ref, keep, *sends
):
    *sends, held = sends
    cot = joined(at, own, (low, high))
    pulled, prod = norm_back(x[...], row_of(pack, GAIN + 2), cot)
    grad = pulled + above[...]
    grad_ref[...] = grad
    branch = grad.astype(BF16)
    branch_ref[...] = branch
    dup = (dot_t(branch, down[0]) * slope[...].astype(F32)).astype(BF16)
    dup_ref[...] = dup
    add_rows(sums_ref, True, [prod, cot, grad, dup.astype(F32)])
    share_out(at, dot_t(dup, up[0]), held, sends, keep)


def tail_sums_kernel(
    at, patches, pack, above_a, above_b, feed_one_a, feed_one_b, feed_zero_a, feed_zero_b,
    front_one_a, front_one_b, front_zero_a, front_zero_b, back_one, back_zero, keep, *refs,
):
    *sends, out = refs
    out[...] = jnp.zeros_like(out)
    half = above_a.shape[0]
    for i, above in enumerate((above_a, above_b)):
        rows = chunk(i, half)
        cot = joined(at, keep.at[i], chunk_of(i, sends))
        x, on = entry_of(patches[rows, :], pack, rows)
        pulled, prod = norm_back(x, row_of(pack, GAIN), cot)
        embed = jnp.where(on, pulled + 0.25 * above[...], 0.0)
        for base, v in ((V_EMBED, embed), (V_GAIN, prod), (V_SHIFT, cot)):
            out[base : base + 1, :] += jnp.sum(v, axis=0, keepdims=True)
    feed_one = feed_one_a[...] + feed_one_b[...]
    feed_zero = feed_zero_a[...] + feed_zero_b[...]
    front_zero = front_zero_a[...] + front_zero_b[...]
    front_one = front_one_a[...] + front_one_b[...]
    for base, v, n in (
        (V_GAIN + 1, front_zero, 0),
        (V_GAIN + 2, feed_zero, 0),
        (V_GAIN + 3, front_one, 0),
        (V_SHIFT + 1, front_zero, 1),
        (V_SHIFT + 2, feed_zero, 1),
        (V_SHIFT + 3, front_one, 1),
        (V_OUT, front_zero, 2),
        (V_OUT + 1, feed_zero, 2),
        (V_OUT + 2, front_one, 2),
        (V_OUT + 3, feed_one, 1),
    ):
        out[base : base + 1, :] = 0.25 * v[n : n + 1, :]
    out[V_UP : V_UP + 1, :] = feed_zero[3:4, :]
    out[V_UP + 1 : V_UP + 2, :] = feed_one[0:1, :]
    out[V_IN : V_IN + 1, :] = back_zero[0:1, :]
    out[V_IN + 1 : V_IN + 2, :] = back_one[0:1, :]


def add_shared_kernel(_, mine, got, out):
    row = lax.broadcasted_iota(jnp.int32, mine.shape, 0)
    out[...] = mine[...] + jnp.where(row < OWN, got[...], 0.0)


def add_kernel(_, mine, got, out):
    out[...] = mine[...] + got[...]


def unpack_kernel(_, mine, got, embed, gain, shift, in_bias, out_bias, up_bias):
    v = mine[...] + got[...]
    embed[...] = v[V_EMBED]
    cols = in_bias.shape[2]
    last = v.shape[1] // 3 * 2
    for l in range(LAYERS):
        for base, ref in ((V_GAIN, gain), (V_SHIFT, shift), (V_OUT, out_bias)):
            ref[l] = v[base + 2 * l : base + 2 * l + 2]
        in_bias[l, 0:1, :] = v[V_IN + l : V_IN + l + 1, :cols]
        in_bias[l, 1:2, :] = v[V_IN + l : V_IN + l + 1, last : last + cols]
    up_bias[...] = v[V_UP : V_UP + LAYERS]


def patches_kernel(at, patches, pack, above_a, above_b, own, other_a, other_b, out_ref):
    half = above_a.shape[0]
    for i, (above, other) in enumerate(((above_a, other_a), (above_b, other_b))):
        rows = chunk(i, half)
        x, on = entry_of(patches[rows, :], pack, rows)
        pulled, _ = norm_back(x, row_of(pack, GAIN), joined(at, own.at[i], (other,)))
        out_ref[rows, :] = jnp.where(on, 0.0, pulled + above[...]).astype(BF16)


def split_rows(value, held, bit):
    size = 2 * held.shape[1]
    rows = value.shape[0] // size
    for n in range(size):
        held[n // bit % 2, n // (2 * bit) * bit + n % bit] = value[n * rows : n * rows + rows].astype(BF16)


def spread(refs, n):
    if len(refs) == n:
        return [r[...] for r in refs]
    half = refs[0].shape[0] // n
    return [refs[0][chunk(i, half), :] for i in range(n)]


def put(ref, i, cols, value):
    rows = value.shape[-2]
    ref[i, :rows, cols] = value
    if ref.shape[1] > rows:
        ref[i, rows:, cols] = jnp.zeros((*value.shape[:-2], ref.shape[1] - rows, value.shape[-1]), BF16)


def cut_terms(at, bit, value, refs):
    *pieces, held = refs
    split_rows(value, held, bit)
    mine = at[2] // bit
    n = pieces[0].shape[2]
    for i, ref in enumerate(pieces):
        cols = slice(i // 2 * n, i // 2 * n + n)
        put(ref, slice(None), slice(None), held[(mine + 1 + i) % 2, :, :, cols])


def feed_grads(parts, bit, at, *refs):
    cuts = refs[-2 * parts - 1 :]
    *args, right_a, right_b = refs[: -2 * parts - 1]
    left = spread(args, 2)
    cut_terms(at, bit, t_dot(left[0], right_a[...]) + t_dot(left[1], right_b[...]), cuts)


def attn_grads(parts, bit, at, normed_a, normed_b, dproj, attn_a, attn_b, mixed_a, mixed_b, *refs):
    cols = mixed_a.shape[1]
    half, part = normed_a.shape[0], dproj.shape[1] // 3
    g = t_dot(normed_a[...], dproj[:half, :]) + t_dot(normed_b[...], dproj[half:, :])
    o = t_dot(attn_a[...], mixed_a[...]) + t_dot(attn_b[...], mixed_b[...])
    pieces = [g[:, c * part : c * part + cols] for c in range(3)] + [o]
    whole_lanes = [p[:, :128] for p in pieces]
    rest = [
        jnp.concatenate([pieces[i][:, 128:], pieces[i + 1][:, 128:]], axis=1) for i in range(0, 4, 2)
    ]
    cut_terms(at, bit, jnp.concatenate(whole_lanes + rest, axis=1), refs)


def halve(bit, under, n_out, at, *refs):
    pairs, outs = refs[: len(refs) - 2 * n_out], refs[len(refs) - 2 * n_out :]
    mine = (at[2] // bit) % 2
    n = outs[0].shape[2]
    first = 0
    for held, got in zip(pairs[::2], pairs[1::2]):
        last = first + held.shape[2]
        for p in range(n_out):
            low, high = max(first, p * n), min(last, p * n + n)
            if low >= high:
                continue
            source, target = slice(low - first, high - first), slice(low - p * n, high - p * n)
            for i in range(outs[0].shape[0]):
                for ref, side in ((outs[2 * p], 1 - mine), (outs[2 * p + 1], mine)):
                    j = i // under * 2 * under + side * under + i % under
                    both = held[j, :, source].astype(F32) + got[j, : held.shape[1], source].astype(F32)
                    put(ref, i, target, both.astype(BF16))
        first = last


def split_pairs(cur, low, mine):
    pairs = cur.reshape(cur.shape[0] // (2 * low), 2, low, *cur.shape[1:])
    return [
        lax.dynamic_index_in_dim(pairs, side, 1, keepdims=False).reshape(-1, *cur.shape[1:]) for side in (1 - mine, mine)
    ]


def add_bf16(mine, got):
    return (mine[...].astype(F32) + got[...].astype(F32)).astype(BF16)


def add_bf16_kernel(_, mine, *refs):
    *gots, out = refs
    first = 0
    for g in gots:
        rows = slice(first, first + g.shape[0])
        out[rows] = add_bf16(mine.at[rows], g)
        first += g.shape[0]


def add_whole_kernel(_, mine, got, out):
    out[...] = add_bf16(mine, got)


def add_pieces_kernel(_, mine, got, out, *pieces):
    s = add_bf16(mine, got)
    out[...] = s
    n = pieces[0].shape[0]
    for i, p in enumerate(pieces):
        p[...] = s[i * n : i * n + n]


def chunk_of(i, pieces):
    n = pieces[1].shape[0] // 2
    return (pieces[0], pieces[1].at[pl.ds(0, n)]) if i == 0 else (pieces[1].at[pl.ds(n, n)], pieces[2])


def add_pair_kernel(_, mine, *refs):
    *gots, out = refs
    for i in range(2):
        first = 0
        for piece in chunk_of(i, gots):
            rows = slice(first, first + piece.shape[0])
            out[i, rows] = add_bf16(mine.at[i, rows], piece)
            first += piece.shape[0]


def add_chunks_kernel(_, mine, got, out_a, out_b):
    v = add_bf16(mine, got)
    out_a[...], out_b[...] = v[0], v[1]


def add_cut_kernel(_, mine_a, mine_b, got_a, got_b, out, one, two_, three):
    a, b = add_bf16(mine_a, got_a), add_bf16(mine_b, got_b)
    out[0], out[1] = a, b
    n = one.shape[0]
    one[...], three[...] = a[:n], b[-n:]
    two_[: n // 2], two_[n // 2 :] = a[n:], b[: n // 2]


def add_halves_kernel(_, mine, got, out, low, high):
    v = add_bf16(mine, got)
    out[...] = v
    low[...], high[...] = v[0], v[1]


def totals(refs):
    return jnp.concatenate(
        [k[0].astype(F32) + g[0].astype(F32) for k, g in zip(refs[::2], refs[1::2])], axis=1
    )


def finish_feed(n_zero, _, *refs):
    *refs, down, up = refs
    ff = up.shape[2]
    for l, part in enumerate((refs[:n_zero], refs[n_zero:])):
        v = totals(part)
        down[l], up[l] = v[:, :ff], v[:, ff:]


def finish_attn_kernel(_, *refs):
    *refs, in_ref, out_ref = refs
    cols = in_ref.shape[3]
    rest = cols - 128
    both = totals(refs)
    width = both.shape[1] // LAYERS
    for n in range(LAYERS):
        l = LAYERS - 1 - n
        v = both[:, n * width : n * width + width]
        for c in range(4):
            first, last = v[:, c * 128 : c * 128 + 128], v[:, 512 + c * rest : 512 + c * rest + rest]
            if c < 3:
                in_ref[l, c, :, :128] = first
                in_ref[l, c, :, 128:] = last
            else:
                out_ref[l] = jnp.transpose(jnp.concatenate([first, last], axis=1))


def blend(slow, weight):
    return DECAY * slow + (1.0 - DECAY) * weight.astype(F32)


def own_lanes(at, rows, width):
    place = lax.broadcasted_iota(jnp.int32, (rows, width), 0) + at[2] * rows
    return (lax.broadcasted_iota(jnp.int32, (rows, width), 1) == place).astype(BF16)


def average_up_kernel(at, in_w, up_w, slow_in, slow_up, fresh_in, fresh_up):
    rows, width = slow_up.shape[1:]
    pick = own_lanes(at, rows, width)
    for l in range(LAYERS):
        for c in range(3):
            fresh_in[l, c] = blend(slow_in[l, c], dot_t(pick, in_w[l, c]))
        fresh_up[l] = blend(slow_up[l], up_w[l, pl.ds(pl.multiple_of(at[2] * rows, 16), rows), :])


def average_down_kernel(at, out_w, down_w, slow_out, slow_down, fresh_out, fresh_down):
    rows, width = slow_down.shape[1:]
    pick = own_lanes(at, rows, down_w.shape[2])
    for l in range(LAYERS):
        fresh_out[l] = blend(slow_out[l], dot_t(out_w[l], pick))
        fresh_down[l] = blend(slow_down[l], dot_t(pick, down_w[l]))


def average_small_kernel(_, *refs):
    n = len(refs) // 3
    for slow, weight, fresh in zip(refs[:n], refs[n : 2 * n], refs[2 * n :]):
        fresh[...] = blend(slow[...], weight[...])


def per_device(
    patches,
    segment_ids,
    mask_flags,
    upstream,
    mask_embed,
    norm_gain,
    norm_shift,
    in_weight,
    in_bias,
    out_weight,
    out_bias,
    up_weight,
    up_bias,
    down_weight,
    slow_mask_embed,
    slow_norm_gain,
    slow_norm_shift,
    slow_in_weight,
    slow_in_bias,
    slow_out_weight,
    slow_out_bias,
    slow_up_weight,
    slow_up_bias,
    slow_down_weight,
):
    rows_here, length, width = patches.shape
    count = rows_here * length
    cols = in_weight.shape[3]
    ff = down_weight.shape[1]
    size = lax.axis_size("rows")
    piece = width // size
    aligned = piece % 16 == 0
    half = count // 2
    quarter = half // 2
    tokens = patches.reshape(count, width)
    top = upstream.reshape(count, width)
    weight_in = in_weight.transpose(0, 2, 3, 1)
    part = 3 * 128 * -(-cols // 128)
    heads = cols // HD
    act, act32, wide = shape((half, width)), shape((half, width), F32), shape((half, part))
    hid, held = shape((half, ff)), shape((half, heads * 128))
    small, pair = shape((quarter, width)), shape((2, quarter, width))
    eight, eighth, bit_of = shape((8, width), F32), shape((quarter // 2, width)), shape((quarter // 4, width))
    two_cores = [pltpu.VMEM((2, quarter, width), BF16)]
    last = []

    def call(body, outs, args, touch=(), free=False, **kwargs):
        if free:
            return run(body, outs, args, **kwargs)
        result = run(body, outs, args, after=tuple(last) + tuple(touch), **kwargs)
        last[:] = [min(result, key=lambda r: r.size)]
        return result

    def add(keep, gots, **kwargs):
        return call(add_bf16_kernel, [shape(keep.shape)], (keep, *gots), **kwargs)[0]

    def add_own(keep, got, parts=2, **kwargs):
        out = [shape((quarter // parts, width))] * parts
        own, *pieces = call(add_pieces_kernel, [small] + out, (keep, got), **kwargs)
        return (own, *(swap(p, "tp", 1) for p in pieces))

    def exchange(keep, sends, **kwargs):
        s = add(keep, [swap(s, "tp", 1) for s in sends], **kwargs)
        return s, swap(s, "tp", 2)

    def terms(kernel, parts, bit, args, more=0, **kwargs):
        n = width // parts
        if aligned:
            return call(
                named(kernel, parts, bit), [shape((size // 2, piece + r, n)) for r in (more, 0)] * parts, args,
                scratch=[pltpu.VMEM((2, size // 2, piece, width), BF16)], **kwargs,
            )
        if kernel is attn_grads:
            normed_a, normed_b, dproj_in, attn_a, attn_b, *mixed_in = args
            g = t_dot(jnp.concatenate([normed_a, normed_b]), dproj_in)
            o = t_dot(jnp.concatenate([attn_a, attn_b]), jnp.concatenate(mixed_in))
            pieces = [g[:, c * part // 3 : c * part // 3 + cols] for c in range(3)] + [o]
            sums = jnp.concatenate([p[:, :128] for p in pieces] + [p[:, 128:] for p in pieces], axis=1)
        else:
            sums = t_dot(jnp.concatenate(args[:-2]), jnp.concatenate(args[-2:]))
        sums = sums.astype(BF16).reshape(size, piece, width)
        mine = lax.axis_index("rows") // bit % 2
        return [x for i in range(parts) for x in split_pairs(sums[:, :, i * n : i * n + n], bit, mine)]

    def step(pieces, bit, low, parts, more=0, **kwargs):
        count_in, rows, _ = pieces[0].shape
        n = sum(p.shape[2] for p in pieces[::2]) // parts
        if aligned:
            return call(
                named(halve, bit, low, parts), [shape((count_in // 2, rows + r, n)) for r in (more, 0)] * parts,
                pieces, **kwargs,
            )
        cur = [(k.astype(F32) + g.astype(F32)).astype(BF16) for k, g in zip(pieces[::2], pieces[1::2])]
        cur, mine = jnp.concatenate(cur, axis=2), lax.axis_index("rows") // bit % 2
        return [x for i in range(parts) for x in split_pairs(cur[:, :, i * n : i * n + n], low, mine)]

    bits = [1 << i for i in range(size.bit_length() - 1)]
    later = bits[1:] + bits[:1]

    class Scatter:
        def __init__(self, order):
            self.order, self.done, self.pieces = order, 0, ()

        def take(self, cuts):
            for send, keep in zip(cuts[::2], cuts[1::2]):
                self.pieces += (keep, swap(send, "rows", self.order[self.done]))

        def add(self, kernel, parts, args, **kwargs):
            self.take(terms(kernel, parts, self.order[0], args, **kwargs))

        def advance(self, parts=1, **kwargs):
            self.done += 1
            bit = self.order[self.done]
            low = 1 << sum(x < bit for x in self.order[self.done :])
            cuts = step(self.pieces, bit, low, parts, **kwargs)
            self.pieces = ()
            self.take(cuts)

        def came(self):
            return self.pieces[1::2]

        def finish(self):
            while self.done + 1 < len(self.order):
                self.advance()
            return self.pieces

    def mix(l):
        parts, blocks = [], []
        for i in range(2):
            m, packed, q = call(
                named(attend, l, i), [shape((half, cols)), shape((half + quarter, 128)), held], (*qkv[l], pack)
            )
            parts.append((m, q))
            blocks.append((packed, swap(packed, "tp", 2), swap(packed, "tp", 1)))
        mixed[l], q_held[l] = zip(*parts)
        return blocks

    def last_blocks(far, i):
        pieces = (far,)
        if i == 0:
            pieces = call(copy_kernel, [shape((far.shape[0] // 2, 128))] * 2, (far,))
        return [swap(p, "tp", 1) for p in pieces]

    def front(l, above, sums, parts, between=lambda: None):
        results = []
        for i, (s, got) in enumerate(sums):
            own = add_own(s, got, parts)
            results.append(
                call(
                    named(attn_front, l, i), [act32, act, held, eight],
                    (after[l][i], above[i], pack, out_weight, mixed[l][i], *own),
                )
            )
            if i == 0:
                between()
        return zip(*results)

    def back(l, shares, **kwargs):
        extra = [] if l else [pltpu.VMEM((half, width), BF16)]
        dproj, sums, *shares = call(
            named(attend_back, l), [shape((count, part)), shape((8, part), F32)] + shares,
            (*qkv[l], pack, *q_held[l], *g_held, weight_in), scratch=extra + [pltpu.VMEM((128, count), F32)] + two_cores, **kwargs,
        )
        return dproj, sums, shares

    normed, qkv, mixed, q_held, after, normed_two, active = {}, {}, {}, {}, {}, {}, {}

    far_args = (norm_gain, norm_shift, out_bias, up_bias, mask_embed, segment_ids, mask_flags, in_bias, tokens, weight_in)
    *far_args, far_weight = [pltpu.with_memory_space_constraint(a, pltpu.HBM) for a in far_args + (out_weight,)]
    block = (cols, width)
    own = call(
        take_kernel, [shape(block)], (far_weight,), scratch=[pltpu.SemaphoreType.DMA((1,))], far=1
    )[0]
    far, near = swap(own, "tp", 2), swap(own, "tp", 1)
    scratch = [pltpu.VMEM(a.shape, a.dtype) for a in far_args[:9]]
    scratch += [pltpu.VMEM(weight_in.shape[1:], BF16), pltpu.SemaphoreType.DMA((10,))]
    pack, *rest = call(
        first_project_kernel, [shape((PACKED, width), F32), act, act, wide, wide], far_args,
        scratch=scratch, far=len(far_args),
    )
    normed[0], qkv[0] = rest[:2], rest[2:]
    blocks = mix(0)
    pieces = call(copy_kernel, [shape((cols // 4, width))] * 4, (far,))
    out_zero = call(
        order_kernel, [shape((4 * cols, width))], (own, far, near, *(swap(p, "tp", 1) for p in pieces))
    )[0]
    slows = (slow_mask_embed, slow_norm_gain, slow_norm_shift, slow_in_bias, slow_out_bias, slow_up_bias)
    fresh_small = call(
        average_small_kernel, [shape(v.shape, F32) for v in slows],
        slows + (mask_embed, norm_gain, norm_shift, in_bias, out_bias, up_bias),
    )
    parts = []
    for i in range(2):
        packed, far, near = blocks[i]
        parts.append(
            call(
                named(first_feed, i), [act32, act, hid, hid, small, eighth, eighth],
                (tokens, out_zero, pack, up_weight, down_weight, packed, far, near, *last_blocks(far, i)), scratch=two_cores,
            )
        )
    after[0], normed_two[0], active[0], slope, keeps, *sends = zip(*parts)
    sums = [exchange(keeps[i], [s[i] for s in sends]) for i in range(2)]
    own = call(take_last_kernel, [shape(block)], (out_weight,))[0]
    far, near = swap(own, "tp", 2), swap(own, "tp", 1)
    if aligned:
        slow_down = slow_down_weight.transpose(0, 2, 1)
        slow_in = slow_in_weight.transpose(0, 2, 1, 3)
        fresh_out_weight, fresh_down = call(
            average_down_kernel, [shape(slow_out_weight.shape, F32), shape(slow_down.shape, F32)],
            (out_weight, down_weight, slow_out_weight, slow_down),
        )
        fresh_in, fresh_up_weight = call(
            average_up_kernel, [shape(slow_in.shape, F32), shape(slow_up_weight.shape, F32)],
            (weight_in, up_weight, slow_in, slow_up_weight),
        )
        fresh_in_weight, fresh_down_weight = fresh_in.transpose(0, 2, 1, 3), fresh_down.transpose(0, 2, 1)
    else:
        start = lax.axis_index("rows") * piece
        fresh_in_weight, fresh_out_weight, fresh_up_weight, fresh_down_weight = (
            blend(slow, lax.dynamic_slice_in_dim(weight, start, piece, dim))
            for slow, weight, dim in (
                (slow_in_weight, in_weight, 1),
                (slow_out_weight, out_weight, 2),
                (slow_up_weight, up_weight, 1),
                (slow_down_weight, down_weight, 2),
            )
        )
    parts = []
    for i, (s, got) in enumerate(sums):
        parts.append(call(next_project_kernel, [act32, act, wide], (after[0][i], *add_own(s, got), pack, weight_in)))
    x_next, normed[1], qkv[1] = zip(*parts)
    blocks = mix(1)
    pieces = call(copy_kernel, [shape((cols // 4, width))] * 4, (far,))
    out_one = call(
        order_kernel, [shape((4 * cols, width))], (own, far, near, *(swap(p, "tp", 1) for p in pieces))
    )[0]
    parts = []
    for i in range(2):
        packed, far, near = blocks[i]
        parts.append(
            call(
                named(last_feed, i), [act32, act, hid, hid, eight, small, eighth, eighth],
                (x_next[i], out_one, pack, up_weight, down_weight, top, packed, far, near, *last_blocks(far, i)),
                scratch=two_cores,
            )
        )
    after[1], normed_two[1], active[1], dup, feed_one, keeps, *sends = zip(*parts)
    sums = [exchange(keeps[i], [s[i] for s in sends]) for i in range(2)]
    feed_scatter, attn_scatter = {1: Scatter(bits)}, {0: Scatter(bits), 1: Scatter(bits)}
    feed_scatter[1].add(feed_grads, 1, (top, *active[1]), free=True)
    feed_scatter[1].add(feed_grads, 1, (*normed_two[1], *dup))

    grad_after, attn, g_held, front_one = front(1, (top, top), sums, 2)
    dproj, back_one, (keep_a, keep_b, *sends) = back(1, [small] * 2 + [eighth] * 4)
    sums = [exchange(keep_a, sends[:2], touch=feed_scatter[1].came()[:1]), exchange(keep_b, sends[2:])]
    attn_scatter[1].add(attn_grads, 1, (*normed[1], dproj, *attn, *mixed[1]), more=16)
    feed_scatter[1].advance(more=16)

    parts = []
    for i, (s, got) in enumerate(sums):
        own = add_own(s, got)
        parts.append(
            call(
                named(feed_back, i), [act32, act, hid, eight, small, small],
                (x_next[i], *own, grad_after[i], pack, down_weight, slope[i], up_weight), scratch=two_cores,
            )
        )
    sends = [x[5:] for x in parts]
    above, branch, dup, feed_zero, keeps = zip(*(x[:5] for x in parts))
    touch = (*attn_scatter[1].came(), *feed_scatter[1].came())
    sums = [exchange(keeps[i], sends[i], touch=touch if i else ()) for i in range(2)]
    feed_scatter[0] = Scatter(bits)
    feed_scatter[0].add(feed_grads, 1, (*branch, *active[0]), free=True)
    feed_scatter[0].add(feed_grads, 1, (*normed_two[0], *dup))
    grad_after, attn, g_held, front_zero = front(0, above, sums, 2, feed_scatter[1].advance)
    dproj, back_zero, (keep, *sends) = back(0, [pair] + [shape((half // 3, width))] * 3, touch=feed_scatter[0].came()[:1])
    attn_scatter[1].add(attn_grads, 1, (*normed[0], dproj, *attn, *mixed[0]))
    feed_scatter[0].advance()
    s = call(
        add_pair_kernel, [pair], (keep, *(swap(x, "tp", 1) for x in sends)), touch=feed_scatter[1].came()
    )[0]
    got = swap(s, "tp", 2)
    total = call(
        tail_sums_kernel, [shape((SUMMED, width), F32)],
        (tokens, pack, *grad_after, *feed_one, *feed_zero, *front_one, *front_zero, back_one, back_zero, keep, *sends),
    )[0]
    out_keep, out_send = call(down_kernel, [pair, pair], (*active[1], down_weight), scratch=two_cores)
    out_came = swap(out_send, "tp", 1)
    vector = [shape(total.shape, F32)]
    total = call(add_shared_kernel, vector, (total, swap(total, "tp", 1)))[0]
    got_total = swap(total, "tp", 2)
    attn_scatter[1].advance()
    feed_scatter[0].advance()
    own, *other = call(add_halves_kernel, [pair, small, small], (s, got))
    other = [swap(x, "tp", 1) for x in other]
    grad_patches = call(
        patches_kernel, [shape((count, width))], (tokens, pack, *grad_after, own, *other)
    )[0].reshape(patches.shape)
    total = call(add_shared_kernel, vector, (total, got_total))[0]
    order = bits
    got_total = swap(total, "rows", order[0])
    out_sums = call(add_chunks_kernel, [small, small], (out_keep, out_came))
    out_came = [swap(x, "tp", 2) for x in out_sums]
    total = call(add_kernel, vector, (total, got_total))[0]
    got_total = swap(total, "rows", order[1])
    attn_scatter[1].advance(touch=feed_scatter[0].came())
    total = call(add_kernel, vector, (total, got_total))[0]
    got_total = swap(total, "rows", order[2])
    out_sum, *pieces = call(
        add_cut_kernel, [pair] + [shape((half // 3, width))] * 3, (*out_sums, *out_came)
    )
    pieces = [swap(x, "tp", 1) for x in pieces]
    zero, one = feed_scatter[0].finish(), feed_scatter[1].finish()
    grad_down, grad_up_weight = call(
        named(finish_feed, len(zero)), [shape((LAYERS, piece, ff), F32)] * 2, zero + one
    )
    both = shape((LAYERS, 2, width), F32)
    layer_out = call(output_kernel, [shape((count, width))], (*after[1], pack, out_sum, *pieces))[0]
    layer_out = layer_out.reshape(patches.shape)
    grad_mask_embed, grad_norm_gain, grad_norm_shift, grad_in_bias, grad_out_bias, grad_up_bias = call(
        unpack_kernel,
        [shape((width,), F32), both, both, shape(in_bias.shape, F32), both, shape(up_bias.shape, F32)],
        (total, got_total),
    )
    one = attn_scatter[1].finish()
    grad_in, grad_out_weight = call(
        finish_attn_kernel, [shape((LAYERS, 3, piece, cols), F32), shape((LAYERS, cols, piece), F32)], one
    )
    return (
        layer_out,
        grad_patches,
        grad_mask_embed,
        grad_norm_gain,
        grad_norm_shift,
        grad_in.transpose(0, 2, 1, 3),
        grad_in_bias,
        grad_out_weight,
        grad_out_bias,
        grad_up_weight,
        grad_up_bias,
        grad_down.transpose(0, 2, 1),
        fresh_small[0],
        fresh_small[1],
        fresh_small[2],
        fresh_in_weight,
        fresh_small[3],
        fresh_out_weight,
        fresh_small[4],
        fresh_up_weight,
        fresh_small[5],
        fresh_down_weight,
    )


def solution(mesh):
    placed = (
        P("rows", None, None),
        P("rows", None),
        P("rows", None),
        P("rows", None, None),
        P(),
        P(),
        P(),
        P(None, None, None, "tp"),
        P(None, None, "tp"),
        P(None, "tp", None),
        P(),
        P(None, None, "tp"),
        P(None, "tp"),
        P(None, "tp", None),
        P(),
        P(),
        P(),
        P(None, "rows", None, "tp"),
        P(None, None, "tp"),
        P(None, "tp", "rows"),
        P(),
        P(None, "rows", "tp"),
        P(None, "tp"),
        P(None, "tp", "rows"),
    )
    return jax.shard_map(
        per_device,
        mesh=mesh,
        in_specs=placed,
        out_specs=(
            P("rows", None, None),
            P("rows", None, None),
            P(),
            P(),
            P(),
            P(None, "rows", None, "tp"),
            P(None, None, "tp"),
            P(None, "tp", "rows"),
            P(),
            P(None, "rows", "tp"),
            P(None, "tp"),
            P(None, "tp", "rows"),
            P(),
            P(),
            P(),
            P(None, "rows", None, "tp"),
            P(None, None, "tp"),
            P(None, "tp", "rows"),
            P(),
            P(None, "rows", "tp"),
            P(None, "tp"),
            P(None, "tp", "rows"),
        ),
        check_vma=False,
    )
```

```python
import functools

import jax
import jax.numpy as jnp
from jax import lax
from jax.experimental import pallas as pl
from jax.experimental.pallas import tpu as pltpu
from jax.sharding import PartitionSpec as P

HD = 64
LAYERS = 2
EPSILON = 1e-06
DECAY = 0.8
NEGATIVE = -1e30
F32 = jnp.float32
BF16 = jnp.bfloat16


def swap(x, axis, bit):
    n = lax.axis_size(axis)
    return lax.ppermute(x, axis, [(i, i ^ bit) for i in range(n)])


def shape(dims, dtype=BF16):
    return jax.ShapeDtypeStruct(tuple(dims), dtype)


def run(body, outs, args, after=(), scratch=(), vmem=16, far=0):
    n_in, n_after = len(args), len(after)

    def kernel(*refs):
        me = lax.axis_index("tp")
        body((me % 2, me, lax.axis_index("rows")), *refs[:n_in], *refs[n_in + n_after :])

    near = pl.BlockSpec(memory_space=pltpu.VMEM)
    anywhere = pl.BlockSpec(memory_space=pl.ANY)
    return pl.pallas_call(
        kernel,
        in_specs=[near] * (n_in - far) + [anywhere] * (far + n_after),
        out_specs=[near] * len(outs),
        out_shape=outs,
        scratch_shapes=scratch,
        name=body.__name__,
        compiler_params=pltpu.CompilerParams(vmem_limit_bytes=vmem * 1024 * 1024),
        cost_estimate=pl.CostEstimate(flops=1, bytes_accessed=1, transcendentals=0),
    )(*args, *after)


def named(body, *first):
    kernel = functools.partial(body, *first)
    kernel.__name__ = body.__name__ + "_" + "_".join(map(str, first))
    return kernel


def dot(a, b):
    return jnp.dot(a, b, preferred_element_type=F32)


def dot_t(a, b):
    return lax.dot_general(a, b, (((1,), (1,)), ((), ())), preferred_element_type=F32)


def t_dot(a, b):
    return lax.dot_general(a, b, (((0,), (0,)), ((), ())), preferred_element_type=F32)


GAIN, SHIFT, OUT_BIAS, UP_BIAS, EMBED, SEG, FLAG, IN_BIAS, PACKED = 0, 4, 8, 12, 14, 15, 16, 17, 24
V_EMBED, V_GAIN, V_SHIFT, V_OUT, OWN, V_UP, V_IN, SUMMED = 0, 1, 5, 9, 13, 13, 15, 24


def norm_parts(values):
    center = values - jnp.mean(values, axis=-1, keepdims=True)
    spread = jnp.mean(center * center, axis=-1, keepdims=True)
    inv = lax.rsqrt(spread + EPSILON)
    return center * inv, inv


def norm_back(values, gain, cot):
    hat, inv = norm_parts(values)
    w = cot * gain
    mean_w = jnp.mean(w, axis=-1, keepdims=True)
    mean_wh = jnp.mean(w * hat, axis=-1, keepdims=True)
    return inv * (w - mean_w - hat * mean_wh), cot * hat


def column(row, lanes=128):
    return jnp.transpose(jnp.broadcast_to(row, (lanes, row.shape[1])))


def split_three(v):
    one = v.astype(BF16).astype(F32)
    two = (v - one).astype(BF16).astype(F32)
    return one, two, v - one - two


def chunk(i, half):
    return slice(i * half, i * half + half)


def row_of(pack, i):
    return pack[i : i + 1, :]


def add_rows(ref, first, rows):
    if first:
        ref[...] = jnp.zeros_like(ref)
    for n, r in enumerate(rows):
        ref[n : n + 1, :] += jnp.sum(r, axis=0, keepdims=True)


def share_out(at, value, held, sends, keep):
    half = value.shape[0] // 2
    for c in range(2):
        held[c] = value[c * half : c * half + half].astype(BF16)
    keep[...] = held[at[0]]
    if len(sends) == 1:
        sends[0][...] = held[1 - at[0]]
        return
    first = 0
    for s in sends:
        n = s.shape[0]
        s[...] = held[1 - at[0], first : first + n]
        first += n


def joined(at, own, others):
    own = own[...].astype(F32)
    other = jnp.concatenate([o[...].astype(F32) for o in others], axis=0)
    low = at[0] == 0
    return jnp.concatenate([jnp.where(low, own, other), jnp.where(low, other, own)], axis=0)


def entry_of(patches, pack, rows):
    on = column(pack[FLAG : FLAG + 1, rows])[:, :1] > 0.0
    return jnp.where(on, row_of(pack, EMBED), patches.astype(F32)), on


def project(x, l, pack, weight, normed_ref, qkv_ref):
    hat, _ = norm_parts(x)
    normed = (hat * row_of(pack, GAIN + 2 * l) + row_of(pack, SHIFT + 2 * l)).astype(BF16)
    normed_ref[...] = normed
    bias = row_of(pack, IN_BIAS + l)
    part, cols = qkv_ref.shape[1] // 3, weight.shape[1]
    for c in range(3):
        first = c * part
        out = (dot_t(normed, weight[c]) + bias[:, first : first + cols]).astype(BF16)
        if c == 0:
            out = out * jnp.asarray(HD**-0.5, BF16)
        qkv_ref[:, first : first + cols] = out
        qkv_ref[:, first + cols : first + part] = jnp.zeros((out.shape[0], part - cols), BF16)


def take_kernel(_, weights, out, sem):
    copy = pltpu.make_async_copy(weights.at[0], out, sem.at[0])
    copy.start()
    copy.wait()


def first_project_kernel(_, *refs):
    far, outs, held, sem = refs[:10], refs[10:15], refs[15:25], refs[25]
    pack, normed, qkv = outs[0], outs[1:3], outs[3:5]
    gain, shift, out_bias, up_bias, embed, seg, flags, in_bias, tokens, weight = far
    sources = [gain, shift, out_bias, up_bias, embed, seg, flags, in_bias, tokens, weight.at[0]]
    copies = [pltpu.make_async_copy(src, dst, sem.at[i]) for i, (src, dst) in enumerate(zip(sources, held))]
    for c in copies:
        c.start()
    for c in copies[:8]:
        c.wait()
    gain, shift, out_bias, up_bias, embed, seg, flags, in_bias, tokens, weight = held[:10]
    pack[...] = jnp.zeros_like(pack)
    for l in range(LAYERS):
        for base, ref in ((GAIN, gain), (SHIFT, shift), (OUT_BIAS, out_bias)):
            pack[base + 2 * l : base + 2 * l + 2, :] = ref[l]
        cols = in_bias.shape[2]
        last = pack.shape[1] // 3 * 2
        pack[IN_BIAS + l : IN_BIAS + l + 1, :cols] = in_bias[l, 0:1]
        pack[IN_BIAS + l : IN_BIAS + l + 1, last : last + cols] = in_bias[l, 1:2]
    pack[UP_BIAS : UP_BIAS + LAYERS, :] = up_bias[...]
    pack[EMBED : EMBED + 1, :] = embed[...].reshape(1, pack.shape[1])
    pack[SEG : SEG + 1, :] = seg[...].astype(F32)
    pack[FLAG : FLAG + 1, :] = flags[...].astype(F32)
    for c in copies[8:10]:
        c.wait()
    for i in range(2):
        rows = chunk(i, normed[i].shape[0])
        x, _on = entry_of(tokens[rows, :], pack, rows)
        project(x, 0, pack, weight, normed[i], qkv[i])


def next_project_kernel(at, after, own, low, high, pack, weight, x_ref, normed, qkv):
    x = after[...] + joined(at, own, (low, high)) + row_of(pack, OUT_BIAS + 1)
    x_ref[...] = x
    project(x, 1, pack, weight.at[1], normed, qkv)


def head_lanes(rows, h):
    lane = lax.broadcasted_iota(jnp.int32, (rows, 128), 1)
    upper = lane >= 64
    mine = upper if h % 2 else jnp.logical_not(upper)
    return mine, lane % 64


def two(refs, cols):
    return jnp.concatenate([r[:, cols] for r in refs], axis=0)


def attend(l, i, _, qkv_a, qkv_b, pack, mixed_ref, packed_ref, held_ref):
    qkv = (qkv_a, qkv_b)
    half, part = qkv_a.shape[0], qkv_a.shape[1] // 3
    heads, width = held_ref.shape[1] // 128, mixed_ref.shape[1]
    seg = column(row_of(pack, SEG)).astype(jnp.int32)
    for h in range(heads):
        lanes = h // 2 * 128
        mine, place = head_lanes(2 * half, h)
        apart = jnp.where((place < 4) & (place != seg), NEGATIVE, 0.0)
        keys = two(qkv, slice(part + lanes, part + lanes + 128))
        keys = jnp.where(mine, keys.astype(F32), apart).astype(BF16)
        values = two(qkv, slice(2 * part + lanes, 2 * part + lanes + 128))
        size = min(128, width - lanes)
        mine, place = mine[:half], place[:half]
        marks = (place == seg[chunk(i, half)]).astype(F32)
        q = qkv[i][:, lanes : lanes + 128].astype(F32)
        scores = dot_t(jnp.where(mine, q, marks).astype(BF16), keys)
        top = jnp.max(scores, axis=-1, keepdims=True)
        expo = jnp.exp(scores - top)
        total = jnp.sum(expo, axis=-1, keepdims=True)
        out = dot(expo.astype(BF16), values) / total
        one, twice, three = split_three(-(top + jnp.log(total)))
        marks = marks + jnp.where(
            place == 4, one, jnp.where(place == 5, twice, jnp.where(place == 6, three, 0.0))
        )
        held_ref[:, h * 128 : h * 128 + 128] = jnp.where(mine, q, marks).astype(BF16)
        if h % 2:
            out = jnp.where(mine, out, mixed_ref[:, lanes : lanes + 128].astype(F32))
        out = out[:, :size].astype(BF16)
        mixed_ref[:, lanes : lanes + size] = out
        if size == 128:
            packed_ref[:half, :] = out
        else:
            packed_ref[half:, :size] = out[: half // 2]
            packed_ref[half:, size:] = out[half // 2 :]


def gelu_both(u):
    phi = 0.5 * (1.0 + lax.erf(u * (0.5**0.5)))
    return u * phi, phi + u * jnp.exp(-0.5 * u * u) * 0.3989422804014327


def in_order(me, own, far, near, last):
    core, chip = me % 2 == 1, me // 2 == 1

    def pick(on, one, other):
        return jnp.where(on, other, one), jnp.where(on, one, other)

    own, far = pick(chip, own, far)
    near, last = pick(chip, near, last)
    own, near = pick(core, own, near)
    far, last = pick(core, far, last)
    return own, near, far, last


def copy_kernel(_, x, *outs):
    n = outs[0].shape[0]
    for i, o in enumerate(outs):
        o[...] = x[i * n : i * n + n]


def order_weights(at, own, far, near, last, out):
    rest = out.shape[0] - 512
    blocks = own[...], far[...], near[...], jnp.concatenate([p[...] for p in last], axis=0)
    for g, w in enumerate(in_order(at[1], *blocks)):
        out[g * 128 : g * 128 + 128, :] = w[:128]
        out[512 + g * rest // 4 : 512 + (g + 1) * rest // 4, :] = w[128:]


def order_kernel(at, own, far, near, one, twice, three, four, out):
    order_weights(at, own, far, near, (one, twice, three, four), out)


def take_last_kernel(_, weights, out):
    out[...] = weights[LAYERS - 1]


def mixed_rows(at, mixed):
    half = mixed[0].shape[0] * 2 // 3
    mixed = [m[...] for m in mixed[:3]] + [jnp.concatenate([m[...] for m in mixed[3:]], axis=0)]
    blocks = in_order(at[1], *[m[:half, :] for m in mixed])
    rest = in_order(at[1], *[m[half:, :] for m in mixed])
    rest = [jnp.concatenate([r[:, :64], r[:, 64:]], axis=0) for r in rest]
    pairs = [jnp.concatenate(rest[g : g + 2], axis=1) for g in (0, 2)]
    return jnp.concatenate([*blocks, *pairs], axis=1)


def feed_front(at, l, x, mixed, weights, pack, up, after_ref, normed_ref):
    after = x + row_of(pack, OUT_BIAS + 2 * l) + dot(mixed_rows(at, mixed), weights[...])
    after_ref[...] = after
    hat, _ = norm_parts(after)
    normed = (hat * row_of(pack, GAIN + 2 * l + 1) + row_of(pack, SHIFT + 2 * l + 1)).astype(BF16)
    normed_ref[...] = normed
    return gelu_both(dot(normed, up[l]) + row_of(pack, UP_BIAS + l))


def first_feed(i, at, patches, weights, pack, up, down, *refs):
    *mixed, after, normed, active_ref, slope_ref, keep, low, high, held = refs
    rows = chunk(i, after.shape[0])
    x, _ = entry_of(patches[rows, :], pack, rows)
    active, slope = feed_front(at, 0, x, mixed, weights, pack, up, after, normed)
    active = active.astype(BF16)
    active_ref[...] = active
    slope_ref[...] = slope.astype(BF16)
    share_out(at, dot(active, down[0]), held, (low, high), keep)


def last_feed(i, at, x, weights, pack, up, down, top, *refs):
    *mixed, after, normed, active_ref, dup_ref, sums_ref, keep, low, high, held = refs
    active, slope = feed_front(at, 1, x[...], mixed, weights, pack, up, after, normed)
    active_ref[...] = active.astype(BF16)
    branch = top[chunk(i, after.shape[0]), :]
    dup = (dot_t(branch, down[1]) * slope).astype(BF16)
    dup_ref[...] = dup
    add_rows(sums_ref, True, [dup.astype(F32), branch.astype(F32)])
    share_out(at, dot_t(dup, up[1]), held, (low, high), keep)


def down_kernel(at, active_a, active_b, down, keep, send, held):
    for i, active in enumerate((active_a, active_b)):
        share_out(at, dot(active[...], down[1]), held, (send.at[i],), keep.at[i])


def output_kernel(at, after_a, after_b, pack, own, one, two_, three, out_ref):
    half = after_a.shape[0]
    for i, after in enumerate((after_a, after_b)):
        y = after[...] + joined(at, own.at[i], chunk_of(i, (one, two_, three))) + row_of(pack, OUT_BIAS + 3)
        out_ref[chunk(i, half), :] = y.astype(BF16)


def attn_front(l, i, at, after, above, pack, out_w, mixed, own, *refs):
    *others, grad_ref, attn_ref, held_ref, sums_ref = refs
    width = mixed.shape[1]
    half = after.shape[0]
    cot = joined(at, own, others)
    pulled, prod = norm_back(after[...], row_of(pack, GAIN + 2 * l + 1), cot)
    above = above[chunk(i, half), :] if above.shape[0] > half else above[...]
    grad = pulled + above.astype(F32)
    grad_ref[...] = grad
    attn = grad.astype(BF16)
    attn_ref[...] = attn
    add_rows(sums_ref, True, [prod, cot, grad])
    mixed_grad = dot_t(attn, out_w[l]).astype(BF16).astype(F32)
    for h in range(width // HD):
        lanes = h // 2 * 128
        mine, place = head_lanes(half, h)
        size = min(128, width - lanes)
        mix = mixed[:, lanes : lanes + size].astype(F32)
        grads = mixed_grad[:, lanes : lanes + size]
        if size < 128:
            fill = jnp.zeros((half, 128 - size), F32)
            mix, grads = (jnp.concatenate([v, fill], axis=1) for v in (mix, grads))
        inner = jnp.sum(jnp.where(mine, mix * grads, 0.0), axis=-1, keepdims=True)
        one, twice, three = split_three(-inner)
        marks = jnp.where(place == 4, one, jnp.where(place == 5, twice, jnp.where(place == 6, three, 0.0)))
        held_ref[:, h * 128 : h * 128 + 128] = jnp.where(mine, grads, marks).astype(BF16)


def attend_back(l, at, qkv_a, qkv_b, pack, q_a, q_b, g_a, g_b, weight, dproj_ref, sums_ref, *refs):
    *refs, turned, held = refs
    if l:
        keeps, sends = refs[:2], (refs[2:4], refs[4:])
    else:
        *refs, stacked = refs
        n = stacked.shape[0] // 2
        keeps, sends = [refs[0].at[i] for i in range(2)], [(stacked.at[pl.ds(i * n, n)],) for i in range(2)]
    qkv, q_held, g_held = (qkv_a, qkv_b), (q_a, q_b), (g_a, g_b)
    half, width = qkv_a.shape
    length = 2 * half
    part = width // 3
    heads = q_a.shape[1] // 128
    seg = column(row_of(pack, SEG)).astype(jnp.int32)
    for h in range(heads):
        lanes = h // 2 * 128
        mine, place = head_lanes(half, h)
        ones = ((place >= 4) & (place < 7)).astype(F32)
        qh = two(q_held, slice(h * 128, h * 128 + 128))
        gh = two(g_held, slice(h * 128, h * 128 + 128))
        for i in range(2):
            rows = chunk(i, half)
            apart = jnp.where((place < 4) & (place != seg[rows]), NEGATIVE, ones)
            bare = qkv[i][:, part + lanes : part + lanes + 128]
            keys = jnp.where(mine, bare.astype(F32), apart).astype(BF16)
            values = qkv[i][:, 2 * part + lanes : 2 * part + lanes + 128].astype(F32)
            values = jnp.where(mine, values, ones).astype(BF16)
            probs = jnp.exp(dot_t(keys, qh))
            ds = (probs * dot_t(values, gh)).astype(BF16)
            gv = dot(probs.astype(BF16), gh).astype(BF16)
            gk = dot(ds, qh).astype(BF16)
            for base, g in ((part, gk), (2 * part, gv)):
                cols = slice(base + lanes, base + lanes + 128)
                if h % 2:
                    g = jnp.where(mine, g.astype(F32), dproj_ref[rows, cols].astype(F32)).astype(BF16)
                elif h == heads - 1:
                    g = jnp.where(mine, g.astype(F32), 0.0).astype(BF16)
                dproj_ref[rows, cols] = g
            dq = t_dot(bare, ds)
            if i == 0:
                turned[...] = dq
            else:
                turned[...] += dq
        dq = jnp.transpose(turned[...]) * HD**-0.5
        cols = slice(lanes, lanes + 128)
        mine, _ = head_lanes(length, h)
        if h % 2:
            dq = jnp.where(mine, dq, dproj_ref[:, cols].astype(F32))
        elif h == heads - 1:
            dq = jnp.where(mine, dq, 0.0)
        dproj_ref[:, cols] = dq.astype(BF16)
    cols = weight.shape[2]
    for i in range(2):
        dproj = dproj_ref[chunk(i, half), :]
        add_rows(sums_ref, i == 0, [dproj.astype(F32)])
        share = sum(dot(dproj[:, c * part : c * part + cols], weight[l, c]) for c in range(3))
        share_out(at, share, held, sends[i], keeps[i])
    if not l:
        n = refs[1].shape[0]
        for i, piece in enumerate(refs[1:]):
            piece[...] = stacked[i * n : i * n + n]


def feed_back(
    i, at, x, own, low, high, above, pack, down, slope, up, grad_ref, branch_ref, dup_ref, sums_ref, keep, *sends
):
    *sends, held = sends
    cot = joined(at, own, (low, high))
    pulled, prod = norm_back(x[...], row_of(pack, GAIN + 2), cot)
    grad = pulled + above[...]
    grad_ref[...] = grad
    branch = grad.astype(BF16)
    branch_ref[...] = branch
    dup = (dot_t(branch, down[0]) * slope[...].astype(F32)).astype(BF16)
    dup_ref[...] = dup
    add_rows(sums_ref, True, [prod, cot, grad, dup.astype(F32)])
    share_out(at, dot_t(dup, up[0]), held, sends, keep)


def tail_sums_kernel(
    at, patches, pack, above_a, above_b, feed_one_a, feed_one_b, feed_zero_a, feed_zero_b,
    front_one_a, front_one_b, front_zero_a, front_zero_b, back_one, back_zero, keep, *refs,
):
    *sends, out = refs
    out[...] = jnp.zeros_like(out)
    half = above_a.shape[0]
    for i, above in enumerate((above_a, above_b)):
        rows = chunk(i, half)
        cot = joined(at, keep.at[i], chunk_of(i, sends))
        x, on = entry_of(patches[rows, :], pack, rows)
        pulled, prod = norm_back(x, row_of(pack, GAIN), cot)
        embed = jnp.where(on, pulled + 0.25 * above[...], 0.0)
        for base, v in ((V_EMBED, embed), (V_GAIN, prod), (V_SHIFT, cot)):
            out[base : base + 1, :] += jnp.sum(v, axis=0, keepdims=True)
    feed_one = feed_one_a[...] + feed_one_b[...]
    feed_zero = feed_zero_a[...] + feed_zero_b[...]
    front_zero = front_zero_a[...] + front_zero_b[...]
    front_one = front_one_a[...] + front_one_b[...]
    for base, v, n in (
        (V_GAIN + 1, front_zero, 0),
        (V_GAIN + 2, feed_zero, 0),
        (V_GAIN + 3, front_one, 0),
        (V_SHIFT + 1, front_zero, 1),
        (V_SHIFT + 2, feed_zero, 1),
        (V_SHIFT + 3, front_one, 1),
        (V_OUT, front_zero, 2),
        (V_OUT + 1, feed_zero, 2),
        (V_OUT + 2, front_one, 2),
        (V_OUT + 3, feed_one, 1),
    ):
        out[base : base + 1, :] = 0.25 * v[n : n + 1, :]
    out[V_UP : V_UP + 1, :] = feed_zero[3:4, :]
    out[V_UP + 1 : V_UP + 2, :] = feed_one[0:1, :]
    out[V_IN : V_IN + 1, :] = back_zero[0:1, :]
    out[V_IN + 1 : V_IN + 2, :] = back_one[0:1, :]


def add_shared_kernel(_, mine, got, out):
    row = lax.broadcasted_iota(jnp.int32, mine.shape, 0)
    out[...] = mine[...] + jnp.where(row < OWN, got[...], 0.0)


def add_kernel(_, mine, got, out):
    out[...] = mine[...] + got[...]


def unpack_kernel(_, mine, got, embed, gain, shift, in_bias, out_bias, up_bias):
    v = mine[...] + got[...]
    embed[...] = v[V_EMBED]
    cols = in_bias.shape[2]
    last = v.shape[1] // 3 * 2
    for l in range(LAYERS):
        for base, ref in ((V_GAIN, gain), (V_SHIFT, shift), (V_OUT, out_bias)):
            ref[l] = v[base + 2 * l : base + 2 * l + 2]
        in_bias[l, 0:1, :] = v[V_IN + l : V_IN + l + 1, :cols]
        in_bias[l, 1:2, :] = v[V_IN + l : V_IN + l + 1, last : last + cols]
    up_bias[...] = v[V_UP : V_UP + LAYERS]


def patches_kernel(at, patches, pack, above_a, above_b, own, other_a, other_b, out_ref):
    half = above_a.shape[0]
    for i, (above, other) in enumerate(((above_a, other_a), (above_b, other_b))):
        rows = chunk(i, half)
        x, on = entry_of(patches[rows, :], pack, rows)
        pulled, _ = norm_back(x, row_of(pack, GAIN), joined(at, own.at[i], (other,)))
        out_ref[rows, :] = jnp.where(on, 0.0, pulled + above[...]).astype(BF16)


def split_rows(value, held, bit):
    size = 2 * held.shape[1]
    rows = value.shape[0] // size
    for n in range(size):
        held[n // bit % 2, n // (2 * bit) * bit + n % bit] = value[n * rows : n * rows + rows].astype(BF16)


def spread(refs, n):
    if len(refs) == n:
        return [r[...] for r in refs]
    half = refs[0].shape[0] // n
    return [refs[0][chunk(i, half), :] for i in range(n)]


def put(ref, i, cols, value):
    rows = value.shape[-2]
    ref[i, :rows, cols] = value
    if ref.shape[1] > rows:
        ref[i, rows:, cols] = jnp.zeros((*value.shape[:-2], ref.shape[1] - rows, value.shape[-1]), BF16)


def cut_terms(at, bit, value, refs):
    *pieces, held = refs
    split_rows(value, held, bit)
    mine = at[2] // bit
    n = pieces[0].shape[2]
    for i, ref in enumerate(pieces):
        cols = slice(i // 2 * n, i // 2 * n + n)
        put(ref, slice(None), slice(None), held[(mine + 1 + i) % 2, :, :, cols])


def feed_grads(parts, bit, at, *refs):
    cuts = refs[-2 * parts - 1 :]
    *args, right_a, right_b = refs[: -2 * parts - 1]
    left = spread(args, 2)
    cut_terms(at, bit, t_dot(left[0], right_a[...]) + t_dot(left[1], right_b[...]), cuts)


def attn_grads(parts, bit, at, normed_a, normed_b, dproj, attn_a, attn_b, mixed_a, mixed_b, *refs):
    cols = mixed_a.shape[1]
    half, part = normed_a.shape[0], dproj.shape[1] // 3
    g = t_dot(normed_a[...], dproj[:half, :]) + t_dot(normed_b[...], dproj[half:, :])
    o = t_dot(attn_a[...], mixed_a[...]) + t_dot(attn_b[...], mixed_b[...])
    pieces = [g[:, c * part : c * part + cols] for c in range(3)] + [o]
    whole_lanes = [p[:, :128] for p in pieces]
    rest = [
        jnp.concatenate([pieces[i][:, 128:], pieces[i + 1][:, 128:]], axis=1) for i in range(0, 4, 2)
    ]
    cut_terms(at, bit, jnp.concatenate(whole_lanes + rest, axis=1), refs)


def halve(bit, under, n_out, at, *refs):
    pairs, outs = refs[: len(refs) - 2 * n_out], refs[len(refs) - 2 * n_out :]
    mine = (at[2] // bit) % 2
    n = outs[0].shape[2]
    first = 0
    for held, got in zip(pairs[::2], pairs[1::2]):
        last = first + held.shape[2]
        for p in range(n_out):
            low, high = max(first, p * n), min(last, p * n + n)
            if low >= high:
                continue
            source, target = slice(low - first, high - first), slice(low - p * n, high - p * n)
            for i in range(outs[0].shape[0]):
                for ref, side in ((outs[2 * p], 1 - mine), (outs[2 * p + 1], mine)):
                    j = i // under * 2 * under + side * under + i % under
                    both = held[j, :, source].astype(F32) + got[j, : held.shape[1], source].astype(F32)
                    put(ref, i, target, both.astype(BF16))
        first = last


def split_pairs(cur, low, mine):
    pairs = cur.reshape(cur.shape[0] // (2 * low), 2, low, *cur.shape[1:])
    return [
        lax.dynamic_index_in_dim(pairs, side, 1, keepdims=False).reshape(-1, *cur.shape[1:]) for side in (1 - mine, mine)
    ]


def add_bf16(mine, got):
    return (mine[...].astype(F32) + got[...].astype(F32)).astype(BF16)


def add_bf16_kernel(_, mine, *refs):
    *gots, out = refs
    first = 0
    for g in gots:
        rows = slice(first, first + g.shape[0])
        out[rows] = add_bf16(mine.at[rows], g)
        first += g.shape[0]


def add_whole_kernel(_, mine, got, out):
    out[...] = add_bf16(mine, got)


def add_pieces_kernel(_, mine, got, out, *pieces):
    s = add_bf16(mine, got)
    out[...] = s
    n = pieces[0].shape[0]
    for i, p in enumerate(pieces):
        p[...] = s[i * n : i * n + n]


def chunk_of(i, pieces):
    n = pieces[1].shape[0] // 2
    return (pieces[0], pieces[1].at[pl.ds(0, n)]) if i == 0 else (pieces[1].at[pl.ds(n, n)], pieces[2])


def add_pair_kernel(_, mine, *refs):
    *gots, out = refs
    for i in range(2):
        first = 0
        for piece in chunk_of(i, gots):
            rows = slice(first, first + piece.shape[0])
            out[i, rows] = add_bf16(mine.at[i, rows], piece)
            first += piece.shape[0]


def add_chunks_kernel(_, mine, got, out_a, out_b):
    v = add_bf16(mine, got)
    out_a[...], out_b[...] = v[0], v[1]


def add_cut_kernel(_, mine_a, mine_b, got_a, got_b, out, one, two_, three):
    a, b = add_bf16(mine_a, got_a), add_bf16(mine_b, got_b)
    out[0], out[1] = a, b
    n = one.shape[0]
    one[...], three[...] = a[:n], b[-n:]
    two_[: n // 2], two_[n // 2 :] = a[n:], b[: n // 2]


def add_halves_kernel(_, mine, got, out, low, high):
    v = add_bf16(mine, got)
    out[...] = v
    low[...], high[...] = v[0], v[1]


def totals(refs):
    return jnp.concatenate(
        [k[0].astype(F32) + g[0].astype(F32) for k, g in zip(refs[::2], refs[1::2])], axis=1
    )


def finish_feed(n_zero, _, *refs):
    *refs, down, up = refs
    ff = up.shape[2]
    for l, part in enumerate((refs[:n_zero], refs[n_zero:])):
        v = totals(part)
        down[l], up[l] = v[:, :ff], v[:, ff:]


def finish_attn_kernel(_, *refs):
    *refs, in_ref, out_ref = refs
    cols = in_ref.shape[3]
    rest = cols - 128
    both = totals(refs)
    width = both.shape[1] // LAYERS
    for n in range(LAYERS):
        l = LAYERS - 1 - n
        v = both[:, n * width : n * width + width]
        for c in range(4):
            first, last = v[:, c * 128 : c * 128 + 128], v[:, 512 + c * rest : 512 + c * rest + rest]
            if c < 3:
                in_ref[l, c, :, :128] = first
                in_ref[l, c, :, 128:] = last
            else:
                out_ref[l] = jnp.transpose(jnp.concatenate([first, last], axis=1))


def blend(slow, weight):
    return DECAY * slow + (1.0 - DECAY) * weight.astype(F32)


def own_lanes(at, rows, width):
    place = lax.broadcasted_iota(jnp.int32, (rows, width), 0) + at[2] * rows
    return (lax.broadcasted_iota(jnp.int32, (rows, width), 1) == place).astype(BF16)


def average_up_kernel(at, in_w, up_w, slow_in, slow_up, fresh_in, fresh_up):
    rows, width = slow_up.shape[1:]
    pick = own_lanes(at, rows, width)
    for l in range(LAYERS):
        for c in range(3):
            fresh_in[l, c] = blend(slow_in[l, c], dot_t(pick, in_w[l, c]))
        fresh_up[l] = blend(slow_up[l], up_w[l, pl.ds(pl.multiple_of(at[2] * rows, 16), rows), :])


def average_down_kernel(at, out_w, down_w, slow_out, slow_down, fresh_out, fresh_down):
    rows, width = slow_down.shape[1:]
    pick = own_lanes(at, rows, down_w.shape[2])
    for l in range(LAYERS):
        fresh_out[l] = blend(slow_out[l], dot_t(out_w[l], pick))
        fresh_down[l] = blend(slow_down[l], dot_t(pick, down_w[l]))


def average_small_kernel(_, *refs):
    n = len(refs) // 3
    for slow, weight, fresh in zip(refs[:n], refs[n : 2 * n], refs[2 * n :]):
        fresh[...] = blend(slow[...], weight[...])


def per_device(
    patches,
    segment_ids,
    mask_flags,
    upstream,
    mask_embed,
    norm_gain,
    norm_shift,
    in_weight,
    in_bias,
    out_weight,
    out_bias,
    up_weight,
    up_bias,
    down_weight,
    slow_mask_embed,
    slow_norm_gain,
    slow_norm_shift,
    slow_in_weight,
    slow_in_bias,
    slow_out_weight,
    slow_out_bias,
    slow_up_weight,
    slow_up_bias,
    slow_down_weight,
):
    rows_here, length, width = patches.shape
    count = rows_here * length
    cols = in_weight.shape[3]
    ff = down_weight.shape[1]
    size = lax.axis_size("rows")
    piece = width // size
    aligned = piece % 16 == 0
    half = count // 2
    quarter = half // 2
    tokens = patches.reshape(count, width)
    top = upstream.reshape(count, width)
    weight_in = in_weight.transpose(0, 2, 3, 1)
    part = 3 * 128 * -(-cols // 128)
    heads = cols // HD
    act, act32, wide = shape((half, width)), shape((half, width), F32), shape((half, part))
    hid, held = shape((half, ff)), shape((half, heads * 128))
    small, pair = shape((quarter, width)), shape((2, quarter, width))
    eight, eighth, bit_of = shape((8, width), F32), shape((quarter // 2, width)), shape((quarter // 4, width))
    two_cores = [pltpu.VMEM((2, quarter, width), BF16)]
    last = []

    def call(body, outs, args, touch=(), free=False, **kwargs):
        if free:
            return run(body, outs, args, **kwargs)
        result = run(body, outs, args, after=tuple(last) + tuple(touch), **kwargs)
        last[:] = [min(result, key=lambda r: r.size)]
        return result

    def add(keep, gots, **kwargs):
        return call(add_bf16_kernel, [shape(keep.shape)], (keep, *gots), **kwargs)[0]

    def add_own(keep, got, parts=2, **kwargs):
        out = [shape((quarter // parts, width))] * parts
        own, *pieces = call(add_pieces_kernel, [small] + out, (keep, got), **kwargs)
        return (own, *(swap(p, "tp", 1) for p in pieces))

    def exchange(keep, sends, **kwargs):
        s = add(keep, [swap(s, "tp", 1) for s in sends], **kwargs)
        return s, swap(s, "tp", 2)

    def terms(kernel, parts, bit, args, more=0, **kwargs):
        n = width // parts
        if aligned:
            return call(
                named(kernel, parts, bit), [shape((size // 2, piece + r, n)) for r in (more, 0)] * parts, args,
                scratch=[pltpu.VMEM((2, size // 2, piece, width), BF16)], **kwargs,
            )
        if kernel is attn_grads:
            normed_a, normed_b, dproj_in, attn_a, attn_b, *mixed_in = args
            g = t_dot(jnp.concatenate([normed_a, normed_b]), dproj_in)
            o = t_dot(jnp.concatenate([attn_a, attn_b]), jnp.concatenate(mixed_in))
            pieces = [g[:, c * part // 3 : c * part // 3 + cols] for c in range(3)] + [o]
            sums = jnp.concatenate([p[:, :128] for p in pieces] + [p[:, 128:] for p in pieces], axis=1)
        else:
            sums = t_dot(jnp.concatenate(args[:-2]), jnp.concatenate(args[-2:]))
        sums = sums.astype(BF16).reshape(size, piece, width)
        mine = lax.axis_index("rows") // bit % 2
        return [x for i in range(parts) for x in split_pairs(sums[:, :, i * n : i * n + n], bit, mine)]

    def step(pieces, bit, low, parts, more=0, **kwargs):
        count_in, rows, _ = pieces[0].shape
        n = sum(p.shape[2] for p in pieces[::2]) // parts
        if aligned:
            return call(
                named(halve, bit, low, parts), [shape((count_in // 2, rows + r, n)) for r in (more, 0)] * parts,
                pieces, **kwargs,
            )
        cur = [(k.astype(F32) + g.astype(F32)).astype(BF16) for k, g in zip(pieces[::2], pieces[1::2])]
        cur, mine = jnp.concatenate(cur, axis=2), lax.axis_index("rows") // bit % 2
        return [x for i in range(parts) for x in split_pairs(cur[:, :, i * n : i * n + n], low, mine)]

    bits = [1 << i for i in range(size.bit_length() - 1)]
    later = bits[1:] + bits[:1]

    class Scatter:
        def __init__(self, order):
            self.order, self.done, self.pieces = order, 0, ()

        def take(self, cuts):
            for send, keep in zip(cuts[::2], cuts[1::2]):
                self.pieces += (keep, swap(send, "rows", self.order[self.done]))

        def add(self, kernel, parts, args, **kwargs):
            self.take(terms(kernel, parts, self.order[0], args, **kwargs))

        def advance(self, parts=1, **kwargs):
            self.done += 1
            bit = self.order[self.done]
            low = 1 << sum(x < bit for x in self.order[self.done :])
            cuts = step(self.pieces, bit, low, parts, **kwargs)
            self.pieces = ()
            self.take(cuts)

        def came(self):
            return self.pieces[1::2]

        def finish(self):
            while self.done + 1 < len(self.order):
                self.advance()
            return self.pieces

    def mix(l, touch=()):
        parts, blocks = [], []
        for i in range(2):
            m, packed, q = call(
                named(attend, l, i), [shape((half, cols)), shape((half + quarter, 128)), held], (*qkv[l], pack),
                touch=touch if i else (),
            )
            parts.append((m, q))
            blocks.append((packed, swap(packed, "tp", 2), swap(packed, "tp", 1)))
        mixed[l], q_held[l] = zip(*parts)
        return blocks

    def last_blocks(far, i):
        pieces = (far,)
        if i == 0:
            pieces = call(copy_kernel, [shape((far.shape[0] // 2, 128))] * 2, (far,))
        return [swap(p, "tp", 1) for p in pieces]

    def front(l, above, sums, parts, between=lambda: None):
        results = []
        for i, (s, got) in enumerate(sums):
            own = add_own(s, got, parts)
            results.append(
                call(
                    named(attn_front, l, i), [act32, act, held, eight],
                    (after[l][i], above[i], pack, out_weight, mixed[l][i], *own),
                )
            )
            if i == 0:
                between()
        return zip(*results)

    def back(l, shares, **kwargs):
        extra = [] if l else [pltpu.VMEM((half, width), BF16)]
        dproj, sums, *shares = call(
            named(attend_back, l), [shape((count, part)), shape((8, part), F32)] + shares,
            (*qkv[l], pack, *q_held[l], *g_held, weight_in), scratch=extra + [pltpu.VMEM((128, count), F32)] + two_cores, **kwargs,
        )
        return dproj, sums, shares

    normed, qkv, mixed, q_held, after, normed_two, active = {}, {}, {}, {}, {}, {}, {}

    far_args = (norm_gain, norm_shift, out_bias, up_bias, mask_embed, segment_ids, mask_flags, in_bias, tokens, weight_in)
    *far_args, far_weight = [pltpu.with_memory_space_constraint(a, pltpu.HBM) for a in far_args + (out_weight,)]
    block = (cols, width)
    own = call(
        take_kernel, [shape(block)], (far_weight,), scratch=[pltpu.SemaphoreType.DMA((1,))], far=1
    )[0]
    far, near = swap(own, "tp", 2), swap(own, "tp", 1)
    scratch = [pltpu.VMEM(a.shape, a.dtype) for a in far_args[:9]]
    scratch += [pltpu.VMEM(weight_in.shape[1:], BF16), pltpu.SemaphoreType.DMA((10,))]
    pack, *rest = call(
        first_project_kernel, [shape((PACKED, width), F32), act, act, wide, wide], far_args,
        scratch=scratch, far=len(far_args),
    )
    normed[0], qkv[0] = rest[:2], rest[2:]
    blocks = mix(0)
    pieces = call(copy_kernel, [shape((cols // 4, width))] * 4, (far,))
    out_zero = call(
        order_kernel, [shape((4 * cols, width))], (own, far, near, *(swap(p, "tp", 1) for p in pieces))
    )[0]
    slows = (slow_mask_embed, slow_norm_gain, slow_norm_shift, slow_in_bias, slow_out_bias, slow_up_bias)
    fresh_small = call(
        average_small_kernel, [shape(v.shape, F32) for v in slows],
        slows + (mask_embed, norm_gain, norm_shift, in_bias, out_bias, up_bias),
    )
    parts = []
    for i in range(2):
        packed, far, near = blocks[i]
        parts.append(
            call(
                named(first_feed, i), [act32, act, hid, hid, small, eighth, eighth],
                (tokens, out_zero, pack, up_weight, down_weight, packed, far, near, *last_blocks(far, i)), scratch=two_cores,
            )
        )
    after[0], normed_two[0], active[0], slope, keeps, *sends = zip(*parts)
    sums = [exchange(keeps[i], [s[i] for s in sends]) for i in range(2)]
    own = call(take_last_kernel, [shape(block)], (out_weight,))[0]
    far, near = swap(own, "tp", 2), swap(own, "tp", 1)
    if aligned:
        slow_down = slow_down_weight.transpose(0, 2, 1)
        slow_in = slow_in_weight.transpose(0, 2, 1, 3)
        fresh_out_weight, fresh_down = call(
            average_down_kernel, [shape(slow_out_weight.shape, F32), shape(slow_down.shape, F32)],
            (out_weight, down_weight, slow_out_weight, slow_down),
        )
        fresh_in, fresh_up_weight = call(
            average_up_kernel, [shape(slow_in.shape, F32), shape(slow_up_weight.shape, F32)],
            (weight_in, up_weight, slow_in, slow_up_weight),
        )
        fresh_in_weight, fresh_down_weight = fresh_in.transpose(0, 2, 1, 3), fresh_down.transpose(0, 2, 1)
    else:
        start = lax.axis_index("rows") * piece
        fresh_in_weight, fresh_out_weight, fresh_up_weight, fresh_down_weight = (
            blend(slow, lax.dynamic_slice_in_dim(weight, start, piece, dim))
            for slow, weight, dim in (
                (slow_in_weight, in_weight, 1),
                (slow_out_weight, out_weight, 2),
                (slow_up_weight, up_weight, 1),
                (slow_down_weight, down_weight, 2),
            )
        )
    parts = []
    for i, (s, got) in enumerate(sums):
        parts.append(call(next_project_kernel, [act32, act, wide], (after[0][i], *add_own(s, got), pack, weight_in)))
    x_next, normed[1], qkv[1] = zip(*parts)
    blocks = mix(1, [far])
    first = last_blocks(blocks[0][1], 0)
    pieces = call(copy_kernel, [shape((cols // 4, width))] * 4, (far,))
    out_one = call(
        order_kernel, [shape((4 * cols, width))], (own, far, near, *(swap(p, "tp", 1) for p in pieces))
    )[0]
    parts = []
    for i in range(2):
        packed, far, near = blocks[i]
        parts.append(
            call(
                named(last_feed, i), [act32, act, hid, hid, eight, small, eighth, eighth],
                (x_next[i], out_one, pack, up_weight, down_weight, top, packed, far, near, *(last_blocks(far, 1) if i else first)),
                scratch=two_cores,
            )
        )
    after[1], normed_two[1], active[1], dup, feed_one, keeps, *sends = zip(*parts)
    sums = [exchange(keeps[i], [s[i] for s in sends]) for i in range(2)]
    feed_scatter, attn_scatter = {1: Scatter(bits)}, {0: Scatter(bits), 1: Scatter(bits)}
    feed_scatter[1].add(feed_grads, 1, (top, *active[1]), free=True)
    feed_scatter[1].add(feed_grads, 1, (*normed_two[1], *dup))

    grad_after, attn, g_held, front_one = front(1, (top, top), sums, 2)
    dproj, back_one, (keep_a, keep_b, *sends) = back(1, [small] * 2 + [eighth] * 4)
    sums = [exchange(keep_a, sends[:2], touch=feed_scatter[1].came()[:1]), exchange(keep_b, sends[2:])]
    attn_scatter[1].add(attn_grads, 1, (*normed[1], dproj, *attn, *mixed[1]), more=16)
    feed_scatter[1].advance(more=16)

    parts = []
    for i, (s, got) in enumerate(sums):
        own = add_own(s, got)
        parts.append(
            call(
                named(feed_back, i), [act32, act, hid, eight, small, small],
                (x_next[i], *own, grad_after[i], pack, down_weight, slope[i], up_weight), scratch=two_cores,
            )
        )
    sends = [x[5:] for x in parts]
    above, branch, dup, feed_zero, keeps = zip(*(x[:5] for x in parts))
    touch = (*attn_scatter[1].came(), *feed_scatter[1].came())
    sums = [exchange(keeps[i], sends[i], touch=touch if i else ()) for i in range(2)]
    feed_scatter[0] = Scatter(bits)
    feed_scatter[0].add(feed_grads, 1, (*branch, *active[0]), free=True)
    feed_scatter[0].add(feed_grads, 1, (*normed_two[0], *dup))
    grad_after, attn, g_held, front_zero = front(0, above, sums, 2, feed_scatter[1].advance)
    dproj, back_zero, (keep, *sends) = back(0, [pair] + [shape((half // 3, width))] * 3, touch=feed_scatter[0].came()[:1])
    attn_scatter[1].add(attn_grads, 1, (*normed[0], dproj, *attn, *mixed[0]))
    feed_scatter[0].advance()
    s = call(
        add_pair_kernel, [pair], (keep, *(swap(x, "tp", 1) for x in sends)), touch=feed_scatter[1].came()
    )[0]
    got = swap(s, "tp", 2)
    total = call(
        tail_sums_kernel, [shape((SUMMED, width), F32)],
        (tokens, pack, *grad_after, *feed_one, *feed_zero, *front_one, *front_zero, back_one, back_zero, keep, *sends),
    )[0]
    out_keep, out_send = call(down_kernel, [pair, pair], (*active[1], down_weight), scratch=two_cores)
    out_came = swap(out_send, "tp", 1)
    vector = [shape(total.shape, F32)]
    total = call(add_shared_kernel, vector, (total, swap(total, "tp", 1)))[0]
    got_total = swap(total, "tp", 2)
    attn_scatter[1].advance()
    feed_scatter[0].advance()
    own, *other = call(add_halves_kernel, [pair, small, small], (s, got))
    other = [swap(x, "tp", 1) for x in other]
    grad_patches = call(
        patches_kernel, [shape((count, width))], (tokens, pack, *grad_after, own, *other)
    )[0].reshape(patches.shape)
    total = call(add_shared_kernel, vector, (total, got_total))[0]
    order = bits
    got_total = swap(total, "rows", order[0])
    out_sums = call(add_chunks_kernel, [small, small], (out_keep, out_came))
    out_came = [swap(x, "tp", 2) for x in out_sums]
    total = call(add_kernel, vector, (total, got_total))[0]
    got_total = swap(total, "rows", order[1])
    attn_scatter[1].advance(touch=feed_scatter[0].came())
    total = call(add_kernel, vector, (total, got_total))[0]
    got_total = swap(total, "rows", order[2])
    out_sum, *pieces = call(
        add_cut_kernel, [pair] + [shape((half // 3, width))] * 3, (*out_sums, *out_came)
    )
    pieces = [swap(x, "tp", 1) for x in pieces]
    zero, one = feed_scatter[0].finish(), feed_scatter[1].finish()
    grad_down, grad_up_weight = call(
        named(finish_feed, len(zero)), [shape((LAYERS, piece, ff), F32)] * 2, zero + one
    )
    both = shape((LAYERS, 2, width), F32)
    layer_out = call(output_kernel, [shape((count, width))], (*after[1], pack, out_sum, *pieces))[0]
    layer_out = layer_out.reshape(patches.shape)
    grad_mask_embed, grad_norm_gain, grad_norm_shift, grad_in_bias, grad_out_bias, grad_up_bias = call(
        unpack_kernel,
        [shape((width,), F32), both, both, shape(in_bias.shape, F32), both, shape(up_bias.shape, F32)],
        (total, got_total),
    )
    one = attn_scatter[1].finish()
    grad_in, grad_out_weight = call(
        finish_attn_kernel, [shape((LAYERS, 3, piece, cols), F32), shape((LAYERS, cols, piece), F32)], one
    )
    return (
        layer_out,
        grad_patches,
        grad_mask_embed,
        grad_norm_gain,
        grad_norm_shift,
        grad_in.transpose(0, 2, 1, 3),
        grad_in_bias,
        grad_out_weight,
        grad_out_bias,
        grad_up_weight,
        grad_up_bias,
        grad_down.transpose(0, 2, 1),
        fresh_small[0],
        fresh_small[1],
        fresh_small[2],
        fresh_in_weight,
        fresh_small[3],
        fresh_out_weight,
        fresh_small[4],
        fresh_up_weight,
        fresh_small[5],
        fresh_down_weight,
    )


def solution(mesh):
    placed = (
        P("rows", None, None),
        P("rows", None),
        P("rows", None),
        P("rows", None, None),
        P(),
        P(),
        P(),
        P(None, None, None, "tp"),
        P(None, None, "tp"),
        P(None, "tp", None),
        P(),
        P(None, None, "tp"),
        P(None, "tp"),
        P(None, "tp", None),
        P(),
        P(),
        P(),
        P(None, "rows", None, "tp"),
        P(None, None, "tp"),
        P(None, "tp", "rows"),
        P(),
        P(None, "rows", "tp"),
        P(None, "tp"),
        P(None, "tp", "rows"),
    )
    return jax.shard_map(
        per_device,
        mesh=mesh,
        in_specs=placed,
        out_specs=(
            P("rows", None, None),
            P("rows", None, None),
            P(),
            P(),
            P(),
            P(None, "rows", None, "tp"),
            P(None, None, "tp"),
            P(None, "tp", "rows"),
            P(),
            P(None, "rows", "tp"),
            P(None, "tp"),
            P(None, "tp", "rows"),
            P(),
            P(),
            P(),
            P(None, "rows", None, "tp"),
            P(None, None, "tp"),
            P(None, "tp", "rows"),
            P(),
            P(None, "rows", "tp"),
            P(None, "tp"),
            P(None, "tp", "rows"),
        ),
        check_vma=False,
    )
```
